256 devices in a mesh: dp: 32 (over y, z), tensor: 8 (over x, core).
Axes of the slice: x: 4, y: 4, z: 8, core: 2. Of those that a mesh axis runs over, the one named last changes fastest.
Arguments:
- queries: bfloat16 [4096, 5120], P('dp', 'tensor'), may hold values from -64 to 64
- response_key_value: bfloat16 [4096, 2048], P('dp', 'tensor'), may hold values from -6 to 6
- prompt_kv: bfloat16 [32, 8, 64, 2048], P('dp', None, None, 'tensor'), may hold values from -6 to 6
- prompt_group: int32 [32, 8], P('dp'), may hold values from 0 to 7, as said below
- response_order: int32 [32], replicated, may hold values from 0 to 31, as said below
- live_blocks: int32 [32], P('dp'), may hold values from 1 to 1
- out_weight: bfloat16 [5120, 5120], P('tensor'), may hold values from -0.078125 to 0.078125
- grad_out: bfloat16 [4096, 5120], P('dp', 'tensor'), may hold values from -6 to 6
Outputs:
- grad_queries: bfloat16 [4096, 5120], P('dp', 'tensor')
- grad_resp_kv: bfloat16 [4096, 2048], P('dp', 'tensor')
- grad_prompt_kv: bfloat16 [32, 8, 64, 2048], P('dp', None, None, 'tensor')
The draws below stay inside these ranges and needn't reach their ends.
Inputs may be any that keep to these rules, and one draw needn't show every extreme that they name: `prompt_group`: each row holds every group number once. `response_order`: every response number appears once; response r belongs to group r // 4.
All inputs are finite; a program needn't handle non-finite values.
Results may differ from the reference program's by a relative error of at most 0.012.
Values may be sent and summed in bfloat16 or wider, within the bound.
A program may use at most 64 MiB of HBM per device.

```python
import math
import jax
import jax.numpy as jnp
from jax import lax

D = 5120
QUERY_HEADS = 40
KEY_VALUE_HEADS = 8
HEAD_SIZE = 128
QB = 128
RESPONSE_LENGTH = 128
PROMPT_BLOCK = 64
RESPONSE_TOKENS = 4096
N_DP = 32


def shared_layout(key):
    base_key = jax.random.fold_in(key, 11)
    row_keys = jax.random.split(jax.random.fold_in(base_key, 1), N_DP)
    prompt_group = jax.vmap(lambda one_key: jax.random.permutation(one_key, N_DP // 4))(row_keys).astype(jnp.int32)
    response_order = jax.random.permutation(jax.random.fold_in(base_key, 2), N_DP).astype(jnp.int32)
    return (prompt_group, response_order)


def shared_prompt(key):
    base_key = jax.random.fold_in(key, 13)
    complete_shape = (N_DP, N_DP // 4, PROMPT_BLOCK, 2 * KEY_VALUE_HEADS * HEAD_SIZE)
    bell_values = jnp.clip(jax.random.normal(jax.random.fold_in(base_key, 1), complete_shape, jnp.float32), -6.0, 6.0)
    return bell_values


def draw_prompt_kv(key, part):
    bell_values = shared_prompt(key)
    values = bell_values
    return values.astype(jnp.bfloat16)


def draw_queries(key, part):
    key = jax.random.fold_in(key, 5)
    complete_shape = (N_DP * RESPONSE_LENGTH, QUERY_HEADS * HEAD_SIZE)
    values = jnp.clip(jax.random.normal(jax.random.fold_in(key, 1), complete_shape, jnp.float32), -6.0, 6.0)
    return values.astype(jnp.bfloat16)


def draw_prompt_group(key, part):
    prompt_group, response_order = shared_layout(key)
    return prompt_group


def draw_response_order(key, part):
    prompt_group, response_order = shared_layout(key)
    return response_order


def draw_live_blocks(key, part):
    key = jax.random.fold_in(key, 9)
    counts = jax.random.randint(jax.random.fold_in(key, 1), (N_DP,), 1, RESPONSE_LENGTH // QB + 1)
    chosen = jax.random.randint(jax.random.fold_in(key, 2), (), 0, N_DP)
    lane_index = lax.broadcasted_iota(jnp.int32, (N_DP,), 0)
    return jnp.where(lane_index == chosen, RESPONSE_LENGTH // QB, counts).astype(jnp.int32)


def levels(stream_key, shape, cuts, least, top_value):
    loudness, own = 1.0, jax.random.fold_in(stream_key, 6)
    for position, shards_of in cuts:
        heights = jnp.exp(jax.random.uniform(jax.random.fold_in(own, position), (shards_of,), jnp.float32, least / len(cuts), top_value / len(cuts)))
        loudness = loudness * jnp.repeat(heights, shape[position] // shards_of).reshape([-1 if axis == position else 1 for axis in range(len(shape))])
    return loudness


def bell_draw(key, dims, deviation, most, pieces=(), kind=jnp.bfloat16):
    drawn = deviation * jax.random.normal(key, dims, jnp.float32)
    if pieces:
        drawn = drawn * levels(key, dims, pieces, -0.22, 0.18)
    return jnp.clip(drawn, -most, most).astype(kind)


def setup_inputs(seed: int = 0) -> dict:
    arg_keys = jax.random.split(jax.random.key(seed), 9)
    queries = draw_queries(jax.random.fold_in(arg_keys[8], 71), 0)
    response_key_value = bell_draw(arg_keys[1], (RESPONSE_TOKENS, 2 * KEY_VALUE_HEADS * HEAD_SIZE), 1.0, 6.0, ((0, 32), (1, 8)))
    prompt_kv = draw_prompt_kv(jax.random.fold_in(arg_keys[8], 71), 0)
    prompt_group = draw_prompt_group(jax.random.fold_in(arg_keys[8], 71), 0)
    response_order = draw_response_order(jax.random.fold_in(arg_keys[8], 71), 0)
    live_blocks = draw_live_blocks(jax.random.fold_in(arg_keys[8], 71), 0)
    out_weight = bell_draw(arg_keys[6], (QUERY_HEADS * HEAD_SIZE, D), (QUERY_HEADS * HEAD_SIZE) ** -0.5, 0.078125, ((0, 8),))
    grad_out = bell_draw(arg_keys[7], (RESPONSE_TOKENS, D), 1.0, 6.0, ((0, 32), (1, 8)))
    return {"queries": queries, "response_key_value": response_key_value, "prompt_kv": prompt_kv, "prompt_group": prompt_group, "response_order": response_order, "live_blocks": live_blocks, "out_weight": out_weight, "grad_out": grad_out}


def head_pass(query_head, grad_head, keys_all, vals_all):
    score_scale = 1.0 / math.sqrt(HEAD_SIZE)
    prompt_length = PROMPT_BLOCK * N_DP
    query_f = query_head.astype(jnp.float32)
    grad_f = grad_head.astype(jnp.float32)
    keys_f = keys_all.astype(jnp.float32)
    vals_f = vals_all.astype(jnp.float32)
    scores = jnp.einsum('thd,kd->htk', query_f, keys_f) * score_scale
    query_pos = lax.broadcasted_iota(jnp.int32, scores.shape, 1)
    key_pos = lax.broadcasted_iota(jnp.int32, scores.shape, 2)
    visible = jnp.logical_or(key_pos < prompt_length, key_pos - prompt_length <= query_pos)
    scores = jnp.where(visible, scores, -jnp.inf)
    row_max = lax.optimization_barrier(jnp.max(scores, axis=2, keepdims=True))
    expo_all = jnp.exp(scores - row_max)
    probs = expo_all / lax.optimization_barrier(jnp.sum(expo_all, axis=2, keepdims=True))
    weights_bf = lax.optimization_barrier(probs.astype(jnp.bfloat16))
    weights_f = weights_bf.astype(jnp.float32)
    attended = jnp.einsum('htk,kd->thd', weights_f, vals_f)
    row_delta = lax.optimization_barrier(jnp.sum(grad_f * attended, axis=2)).T
    back_probs = jnp.einsum('thd,kd->htk', grad_f, vals_f)
    dscore = probs * (back_probs - row_delta[:, :, None])
    dscore_bf = lax.optimization_barrier(dscore.astype(jnp.bfloat16))
    dscore_f = dscore_bf.astype(jnp.float32)
    grad_query = jnp.einsum('htk,kd->thd', dscore_f, keys_f) * score_scale
    grad_keys = jnp.einsum('htk,thd->kd', dscore_f, query_f) * score_scale
    grad_vals = jnp.einsum('htk,thd->kd', weights_f, grad_f)
    return (grad_query.astype(jnp.bfloat16), grad_keys, grad_vals)

def reference(queries, response_key_value, prompt_kv, prompt_group, response_order, live_blocks, out_weight, grad_out):
    groups = N_DP // 4
    key_value_width = 2 * KEY_VALUE_HEADS * HEAD_SIZE
    group_count = QUERY_HEADS // KEY_VALUE_HEADS
    prompt_length = PROMPT_BLOCK * N_DP
    slot_of = jnp.argsort(prompt_group, axis=1).astype(jnp.int32)
    ordered = jnp.take_along_axis(prompt_kv, slot_of[:, :, None, None], axis=1)
    group_prompt = jnp.transpose(ordered, (1, 0, 2, 3)).reshape(groups, prompt_length, key_value_width)
    attention_gradient = jnp.dot(grad_out, out_weight.T, preferred_element_type=jnp.float32)
    row_ids = jnp.arange(N_DP * RESPONSE_LENGTH, dtype=jnp.int32)
    live_rows = live_blocks[row_ids // RESPONSE_LENGTH] * QB
    attention_gradient = jnp.where((row_ids % RESPONSE_LENGTH < live_rows)[:, None], attention_gradient, 0.0).astype(jnp.bfloat16)
    group_ids = (response_order // 4).astype(jnp.int32)

    def one_response(totals, position_index):
        group_id = group_ids[position_index]
        prompt_row_block = lax.dynamic_index_in_dim(group_prompt, group_id, 0, keepdims=False)
        response_rows = lax.dynamic_slice_in_dim(response_key_value, position_index * RESPONSE_LENGTH, RESPONSE_LENGTH, 0)
        query_row_block = lax.dynamic_slice_in_dim(queries, position_index * RESPONSE_LENGTH, RESPONSE_LENGTH, 0).reshape(RESPONSE_LENGTH, KEY_VALUE_HEADS, group_count, HEAD_SIZE)
        gradient_rows = lax.dynamic_slice_in_dim(attention_gradient, position_index * RESPONSE_LENGTH, RESPONSE_LENGTH, 0).reshape(RESPONSE_LENGTH, KEY_VALUE_HEADS, group_count, HEAD_SIZE)
        key_value_total = jnp.concatenate([prompt_row_block, response_rows], axis=0).reshape(prompt_length + RESPONSE_LENGTH, KEY_VALUE_HEADS, 2, HEAD_SIZE)
        head_inputs = (jnp.transpose(query_row_block, (1, 0, 2, 3)), jnp.transpose(gradient_rows, (1, 0, 2, 3)), jnp.transpose(key_value_total[:, :, 0], (1, 0, 2)), jnp.transpose(key_value_total[:, :, 1], (1, 0, 2)))
        grad_query, grad_keys, grad_vals = lax.map(lambda items: head_pass(*items), head_inputs)
        grad_rows_q = jnp.transpose(grad_query, (1, 0, 2, 3)).reshape(RESPONSE_LENGTH, QUERY_HEADS * HEAD_SIZE)
        kv_grad = jnp.transpose(jnp.stack([grad_keys, grad_vals], axis=2), (1, 0, 2, 3)).reshape(prompt_length + RESPONSE_LENGTH, key_value_width)
        current = lax.dynamic_index_in_dim(totals, group_id, 0, keepdims=False)
        totals = lax.dynamic_update_index_in_dim(totals, current + kv_grad[:prompt_length], group_id, 0)
        return (totals, (grad_rows_q, kv_grad[prompt_length:].astype(jnp.bfloat16)))
    initial = jnp.zeros((groups, prompt_length, key_value_width), jnp.float32)
    totals, (grad_q, grad_resp) = lax.scan(one_response, initial, jnp.arange(N_DP, dtype=jnp.int32))
    grad_queries = grad_q.reshape(N_DP * RESPONSE_LENGTH, QUERY_HEADS * HEAD_SIZE)
    grad_resp_kv = grad_resp.reshape(N_DP * RESPONSE_LENGTH, key_value_width)
    by_block = jnp.transpose(totals.reshape(groups, N_DP, PROMPT_BLOCK, key_value_width), (1, 0, 2, 3))
    grad_prompt_kv = jnp.take_along_axis(by_block, prompt_group[:, :, None, None], axis=1).astype(jnp.bfloat16)
    return (grad_queries, grad_resp_kv, grad_prompt_kv)
```

```python
import math

import jax
import jax.numpy as jnp
from jax import lax
from jax.experimental import pallas as pl
from jax.experimental.pallas import tpu as pltpu
from jax.sharding import PartitionSpec as P

HEAD = 128
HEADS = 5
WIDTH = HEAD * HEADS
TOKENS = 128
BLOCK = 64
GROUPS = 8
NY, NZ, NX = 4, 8, 4
PIECES = 8
KEYS = NZ * BLOCK
SCALE = 1.0 / math.sqrt(HEAD)
EXP2_SCALE = SCALE * math.log2(math.e)
N_COPIES = 80
MESH = pl.DeviceIdType.MESH
BF16, F32 = jnp.bfloat16, jnp.float32


def mm(a, b):
    return jnp.dot(a, b, preferred_element_type=F32)


def mm_t(a, b):
    return lax.dot_general(a, b, (((1,), (1,)), ((), ())), preferred_element_type=F32)


def fold(x, op):
    return op(x.reshape(x.shape[0] // 8, 8, x.shape[1]), axis=0)


def each(count, step):
    def run(index, carry):
        step(index)
        return carry

    lax.fori_loop(0, count, run, 0)


def each_pair(count, step):
    def both(index):
        step(2 * index)
        step(2 * index + 1)

    each(count // 2, both)


def kernel(
    q_ref, rkv_ref, pkv_ref, pg_ref, ro_ref, lb_ref, w_ref, go_ref,
    oq_ref, or_ref, op_ref,
    q_v, rkv_v, pkv_v, go_v, oq_v, or_v, op_v,
    w_v, gox, gos, g_own, q_buf, g_buf, qs, gs,
    own, r1, st2, st3, st4, kv,
    e_buf, e_own, p_buf, p_own, dp_buf, dp_own, ds_buf, ds_own,
    tops, sums, dots, coef, shares, row_delta, stat_out, stat_in, del_out, del_in,
    s2, s3, s4, q2, q3, q4, summed, back_in, dkv, dq_send, dq_recv,
    marks, in_sem, out_sem, w_sem, send_sem, recv_sem,
):
    dp = lax.axis_index("dp")
    tensor = lax.axis_index("tensor")
    y, z = dp // NZ, dp % NZ
    x, core = tensor // 2, tensor % 2

    def at_z(step):
        return (y * NZ + (z + step + NZ) % NZ, tensor)

    def at_y(step):
        return (((y + step + NY) % NY) * NZ + z, tensor)

    def at_x(step):
        return (dp, ((x + step + NX) % NX) * 2 + core)

    sibling = (dp, x * 2 + 1 - core)

    numbers = {}
    started = []

    def remote(name, src, dst, device):
        n = numbers.setdefault(name, len(numbers))
        return pltpu.make_async_remote_copy(
            src_ref=src, dst_ref=dst, send_sem=send_sem.at[n], recv_sem=recv_sem.at[n],
            device_id=device, device_id_type=MESH,
        )

    def go(copy):
        copy.start()
        started.append(copy)

    barrier = pltpu.get_barrier_semaphore()
    partners = [at_z(step) for step in (1, -1, 2, -2, 3, -3)]
    partners += [at_y(1), at_y(2), at_y(3), at_x(1), at_x(-1), sibling]
    for partner in partners:
        pl.semaphore_signal(barrier, inc=1, device_id=partner, device_id_type=MESH)
    in_copies = [
        pltpu.make_async_copy(src, dst, in_sem.at[n])
        for n, (src, dst) in enumerate(
            [(pkv_ref, pkv_v), (go_ref, go_v), (q_ref, q_v), (rkv_ref, rkv_v)]
        )
    ]
    for copy in in_copies:
        copy.start()

    w_copies = []
    for r in range(NX):
        for other in range(2):
            piece = ((x + r) % NX) * 2 + (core if other == 0 else 1 - core)
            copy = pltpu.make_async_copy(
                w_ref.at[:, pl.ds(pl.multiple_of(piece * WIDTH, WIDTH), WIDTH)],
                w_v.at[r * 2 + other], w_sem.at[r * 2 + other],
            )
            copy.start()
            w_copies.append(copy)

    in_copies[0].wait()
    for g in range(GROUPS):
        slot = jnp.int32(0)
        for c in range(GROUPS):
            slot = jnp.where(pg_ref[0, c] == g, c, slot)
        block = pkv_v[0, slot]
        own[0, g] = block[:, :HEAD]
        own[1, g] = block[:, HEAD:]
    for copy in in_copies[1:]:
        copy.wait()
    pl.semaphore_wait(barrier, len(partners))

    def hop(step, c, d):
        sign = 1 if d == 0 else -1
        src, dst, device = {
            1: (own.at[c], r1[c][d], at_z(sign)),
            2: (st2.at[c, d], kv.at[c, :, pl.ds((3 + d) * BLOCK, BLOCK)], at_z(sign)),
            3: (st3.at[c, d], kv.at[c, :, pl.ds((5 + d) * BLOCK, BLOCK)], at_z(2 * sign)),
            4: (
                st4.at[c, d], kv.at[c, pl.ds(2 * d, 2), pl.ds(7 * BLOCK, BLOCK)],
                at_z(3 * sign),
            ),
        }[step]
        return remote(("hop", step, c, d), src, dst, device)

    half = TOKENS // 2

    def ring_copy(name, src, buf, before, after, way, part):
        rows = pl.ds(part * half, half)
        dst = buf.at[1 if way == 0 else 3, rows]
        return remote((name, way, part), src.at[rows], dst, before if way == 0 else after)

    def ring_pass(name, buf, before, after, way):
        rows = pl.ds(way * half, half)
        return remote(
            (name, way, 2), buf.at[1 if way == 0 else 3, rows], buf.at[2, rows],
            before if way == 0 else after,
        )

    def ring_first(*ring):
        for turn in range(2):
            for way in range(2):
                go(ring_copy(*ring, way, way if turn == 0 else 1 - way))

    def ring_second(name, src, buf, before, after):
        for way in range(2):
            ring_copy(name, src, buf, before, after, way, way).wait_recv()
            go(ring_pass(name, buf, before, after, way))

    def ring_rest(name, src, buf, before, after):
        for way in range(2):
            ring_copy(name, src, buf, before, after, way, 1 - way).wait_recv()

    def ring_last(name, src, buf, before, after):
        for way in range(2):
            ring_pass(name, buf, before, after, way).wait_recv()

    x_ring = ("x", go_v, gox, at_x(-1), at_x(1))
    q_ring = ("q", q_v, q_buf, at_y(-1), at_y(1))
    g_ring = ("g", g_own, g_buf, at_y(-1), at_y(1))

    def share(r):
        src = go_v if r == 0 else gox.at[r]
        return remote(("share", r), src, gos.at[r], sibling)

    ring_first(*x_ring)
    for d in range(2):
        go(hop(1, 0, d))
    go(share(0))
    ring_first(*q_ring)

    groups = {
        step: [ro_ref[((y + j) % NY) * NZ + (z + step + NZ) % NZ] // 4 for j in range(NY)]
        for step in range(-3, 4)
    }
    my_groups = groups[0]

    def relay(c):
        for d in range(2):
            sign = 1 if d == 0 else -1
            hop(1, c, d).wait_recv()
            for i in range(2):
                st4[c, d, i] = r1[c][d][groups[3 * sign][2 * d + i]]
            go(hop(4, c, d))
            for j in range(NY):
                st3[c, d, j] = r1[c][d][groups[2 * sign][j]]
            go(hop(3, c, d))
            for j in range(NY):
                st2[c, d, j] = r1[c][d][groups[sign][j]]
            go(hop(2, c, d))

    def stack_heads(raw, stacked, j):
        for h in range(HEADS):
            stacked[j, h * HEAD : (h + 1) * HEAD, :] = raw[:, h * HEAD : (h + 1) * HEAD]

    levels = [(0, 1), (1, 2), (3, 2), (5, 3)]

    def weigh(s):
        top = jnp.max(fold(s, jnp.max), axis=0, keepdims=True)
        e = jnp.exp2((s - top) * EXP2_SCALE)
        return top, e, jnp.sum(fold(e, jnp.sum), axis=0, keepdims=True)

    def scores(j, level):
        first, count = levels[level][0] * BLOCK, levels[level][1] * BLOCK
        top, e, total = weigh(mm_t(kv[0, j, first : first + count, :], qs[j]))
        e_buf[j, first : first + count, :] = e.astype(BF16)
        tops[j, level : level + 1, :] = top
        sums[j, level : level + 1, :] = total

    def slopes(j, level):
        first, count = levels[level][0] * BLOCK, levels[level][1] * BLOCK
        terms = mm_t(kv[1, j, first : first + count, :], gs[j])
        dp_buf[j, first : first + count, :] = terms
        products = terms * e_buf[j, first : first + count, :].astype(F32)
        dots[j, level : level + 1, :] = jnp.sum(fold(products, jnp.sum), axis=0, keepdims=True)

    def take(c, level):
        for j in range(NY):
            g = my_groups[j]
            if level == 0:
                kv[c, j, 0:BLOCK, :] = own[c, g]
            else:
                kv[c, j, BLOCK : 2 * BLOCK, :] = r1[c][0][g]
                kv[c, j, 2 * BLOCK : 3 * BLOCK, :] = r1[c][1][g]

    def arrived(c, steps):
        for step in steps:
            for d in range(2):
                hop(step, c, d).wait_recv()

    def project(piece, block):
        w_copies[piece].wait()
        return mm_t(w_v[piece], block[...])

    grad = project(0, go_v)
    for d in range(2):
        go(hop(1, 1, d))
    tops[...] = jnp.full(tops.shape, -jnp.inf, F32)
    sums[...] = jnp.zeros(sums.shape, F32)
    dots[...] = jnp.zeros(dots.shape, F32)
    del_out[...] = jnp.zeros(del_out.shape, F32)
    share(0).wait_recv()
    grad = grad + project(1, gos.at[0])

    stack_heads(q_v[...], qs, 0)
    s = mm_t(rkv_v[:, :HEAD], qs[0])
    key_pos = lax.broadcasted_iota(jnp.int32, s.shape, 0)
    query_pos = lax.broadcasted_iota(jnp.int32, s.shape, 1) % TOKENS
    top, e, total = weigh(jnp.where(key_pos <= query_pos, s, -jnp.inf))
    e_own[...] = e.astype(BF16)
    tops[0, 5:6, :] = top
    sums[0, 5:6, :] = total

    ring_second(*x_ring)
    ring_rest(*x_ring)
    go(share(1))
    go(share(3))
    relay(0)
    ring_second(*q_ring)
    grad = grad + project(2, gox.at[1])
    grad = grad + project(6, gox.at[3])
    ring_last(*x_ring)
    go(share(2))
    share(1).wait_recv()
    grad = grad + project(3, gos.at[1])
    share(3).wait_recv()
    grad = grad + project(7, gos.at[3])
    relay(1)
    grad = grad + project(4, gox.at[2])
    share(2).wait_recv()
    grad = grad + project(5, gos.at[2])
    column = lax.broadcasted_iota(jnp.int32, grad.shape, 1)
    grad = jnp.where(column < lb_ref[0] * TOKENS, grad, 0.0).astype(BF16)
    for h in range(HEADS):
        head = grad[h * HEAD : (h + 1) * HEAD, :].T
        gs[0, h * HEAD : (h + 1) * HEAD, :] = head
        g_own[:, h * HEAD : (h + 1) * HEAD] = head
    ring_first(*g_ring)
    ring_rest(*q_ring)
    for level in range(2):
        take(0, level)
        take(1, level)
    for j in (1, 3):
        stack_heads(q_buf[j], qs, j)
    for j in (0, 1, 3):
        scores(j, 0)
        scores(j, 1)
    ring_last(*q_ring)
    stack_heads(q_buf[2], qs, 2)
    scores(2, 0)
    scores(2, 1)
    arrived(0, (2,))
    each(NY, lambda j: scores(j, 2))
    ring_second(*g_ring)
    arrived(0, (3, 4))
    each(NY, lambda j: scores(j, 3))

    for j in range(NY):
        top = jnp.max(tops[j], axis=0, keepdims=True)
        share_of = jnp.exp2((tops[j] - top) * EXP2_SCALE)
        shares[j] = share_of
        stat_out[j : j + 1, :] = top
        stat_out[NY + j : NY + j + 1, :] = jnp.sum(sums[j] * share_of, axis=0, keepdims=True)

    def stat(k):
        return remote(("stat", k), stat_out, stat_in.at[k], at_y(k))

    def delta(k):
        return remote(("delta", k), del_out, del_in.at[k], at_y(k))

    for k in range(1, NY):
        go(stat(k))
    ring_rest(*g_ring)
    for j in (1, 3):
        stack_heads(g_buf[j], gs, j)
    for j in (0, 1, 3):
        slopes(j, 0)
        slopes(j, 1)
    terms = mm_t(rkv_v[:, HEAD:], gs[0])
    dp_own[...] = terms
    products = terms * e_own[...].astype(F32)
    dots[0, 5:6, :] = jnp.sum(fold(products, jnp.sum), axis=0, keepdims=True)
    ring_last(*g_ring)
    stack_heads(g_buf[2], gs, 2)
    for k in range(1, NY):
        stat(k).wait_recv()
    for j in range(NY):
        mine = stat_out[j : j + 1, :]
        others = [stat_in[k, (j + k) % NY : (j + k) % NY + 1, :] for k in range(1, NY)]
        highest = mine
        for other in others:
            highest = jnp.maximum(highest, other)
        factors = [jnp.exp2((top - highest) * EXP2_SCALE) for top in [mine] + others]
        total = stat_out[NY + j : NY + j + 1, :] * factors[0]
        for k in range(1, NY):
            line = NY + (j + k) % NY
            total = total + stat_in[k, line : line + 1, :] * factors[k]
        for k in range(NY):
            row_delta[k, j : j + 1, :] = factors[k] / total
        coef[j] = shares[j] * (factors[0] / total)

    def back(step, c, d):
        sign = -1 if d == 0 else 1
        src, dst, device = {
            2: (s2.at[c, d], q2.at[c, d], at_z(sign)),
            3: (s3.at[c, d], q3.at[c, d], at_z(2 * sign)),
            4: (s4.at[c, pl.ds(2 * d, 2)], q4.at[c, d], at_z(3 * sign)),
            1: (summed.at[c, d], back_in[c][d], at_z(sign)),
        }[step]
        return remote(("back", step, c, d), src, dst, device)

    def fill(c, j, level):
        first, count = levels[level][0] * BLOCK, levels[level][1] * BLOCK
        rows = slice(first, first + count)
        if c == 1:
            p_buf[j, rows, :] = (
                e_buf[j, rows, :].astype(F32) * coef[j, level : level + 1, :]
            ).astype(BF16)
        else:
            ds_buf[j, rows, :] = (
                p_buf[j, rows, :].astype(F32) * (dp_buf[j, rows, :] - row_delta[0, pl.ds(j, 1), :])
            ).astype(BF16)

    def grads(c, j, first, count):
        if c == 1:
            return mm(p_buf[j, first : first + count, :], gs[j])
        return mm(ds_buf[j, first : first + count, :], qs[j]) * SCALE

    def far(c):
        def outer(j):
            fill(c, j, 3)
            terms = grads(c, j, 5 * BLOCK, 3 * BLOCK).astype(BF16)
            s3[c, 0, j] = terms[:BLOCK]
            s3[c, 1, j] = terms[BLOCK : 2 * BLOCK]
            s4[c, j] = terms[2 * BLOCK :]

        def inner(j):
            fill(c, j, 2)
            terms = grads(c, j, 3 * BLOCK, 2 * BLOCK).astype(BF16)
            s2[c, 0, j] = terms[:BLOCK]
            s2[c, 1, j] = terms[BLOCK:]

        each(NY, outer)
        for step in (4, 3):
            for d in range(2):
                go(back(step, c, d))
        each(NY, inner)
        for d in range(2):
            go(back(2, c, d))

    def near(c):
        def one(j):
            for level in range(2):
                fill(c, j, level)
            dkv[c, j] = grads(c, j, 0, 3 * BLOCK)

        each(NY, one)

    def my_terms(c, first, g):
        total = dkv[c, 0, first : first + BLOCK, :] * marks[g]
        for j in range(1, NY):
            total = total + dkv[c, j, first : first + BLOCK, :] * marks[j * GROUPS + g]
        return total

    def add_up(c):
        for d in range(2):
            for step in (4, 3, 2):
                back(step, c, d).wait_recv()

            def one(g):
                total = my_terms(c, (1 + d) * BLOCK, g)
                for i in range(NY):
                    base = NY + 10 * d + i
                    total = total + q2[c, d, i].astype(F32) * marks[base * GROUPS + g]
                    total = total + q3[c, d, i].astype(F32) * marks[(base + 4) * GROUPS + g]
                for i in range(2):
                    total = total + q4[c, d, i].astype(F32) * marks[
                        (NY + 10 * d + 8 + i) * GROUPS + g
                    ]
                summed[c, d, g] = total.astype(BF16)

            each_pair(GROUPS, one)
            go(back(1, c, d))

    def out_copy(c):
        columns = pl.ds(c * HEAD, HEAD)
        return pltpu.make_async_copy(
            op_v.at[c], op_ref.at[0, :, :, columns], out_sem.at[c]
        )

    def finish(c):
        for d in range(2):
            back(1, c, d).wait_recv()
        for slot in range(GROUPS):
            g = pg_ref[0, slot]
            total = back_in[c][0][g].astype(F32) + back_in[c][1][g].astype(F32)
            op_v[c, slot] = (total + my_terms(c, 0, g)).astype(BF16)
        out_copy(c).start()

    far(1)
    slopes(2, 0)
    slopes(2, 1)
    arrived(1, (2,))
    each(NY, lambda j: slopes(j, 2))
    arrived(1, (3, 4))
    each(NY, lambda j: slopes(j, 3))
    for j in range(NY):
        del_out[j : j + 1, :] = jnp.sum(dots[j] * shares[j], axis=0, keepdims=True)
    for k in range(1, NY):
        go(delta(k))
    near(1)
    for k in range(1, NY):
        delta(k).wait_recv()
    for j in range(NY):
        total = del_out[j : j + 1, :] * row_delta[0, j : j + 1, :]
        for k in range(1, NY):
            line = (j + k) % NY
            total = total + del_in[k, line : line + 1, :] * row_delta[k, j : j + 1, :]
        row_delta[0, j : j + 1, :] = total
    far(0)
    listed = list(my_groups)
    for d, sign in ((0, 1), (1, -1)):
        listed += groups[sign] + groups[2 * sign] + groups[3 * sign][2 * d : 2 * d + 2]
    for n, group in enumerate(listed):
        for g in range(GROUPS):
            marks[n * GROUPS + g] = jnp.where(group == g, 1.0, 0.0).astype(F32)
    near(0)
    p_own[...] = (e_own[...].astype(F32) * coef[0, 5:6, :]).astype(BF16)
    ds_own[...] = (
        p_own[...].astype(F32) * (dp_own[...] - row_delta[0, 0:1, :])
    ).astype(BF16)

    def dq_copy(j):
        return remote(("dq", j), dq_send.at[j], dq_recv.at[j], at_y(j))

    for j in range(1, NY):
        dq_send[j] = mm(kv[0, j].T, ds_buf[j]).astype(BF16)
        go(dq_copy(j))
    add_up(1)
    or_v[:, :HEAD] = (mm(ds_own[...], qs[0]) * SCALE).astype(BF16)
    or_v[:, HEAD:] = mm(p_own[...], gs[0]).astype(BF16)
    or_copy = pltpu.make_async_copy(or_v, or_ref, out_sem.at[2])
    or_copy.start()
    dq = mm(kv[0, 0].T, ds_buf[0]) + mm(rkv_v[:, :HEAD].T, ds_own[...])
    add_up(0)
    for j in range(1, NY):
        dq_copy(j).wait_recv()
        dq = dq + dq_recv[j].astype(F32)
    dq = dq * SCALE
    for h in range(HEADS):
        oq_v[:, h * HEAD : (h + 1) * HEAD] = dq[:, h * HEAD : (h + 1) * HEAD].T.astype(BF16)
    oq_copy = pltpu.make_async_copy(oq_v, oq_ref, out_sem.at[3])
    oq_copy.start()
    finish(1)
    for copy in started:
        copy.wait_send()
    finish(0)
    or_copy.wait()
    oq_copy.wait()
    out_copy(1).wait()
    out_copy(0).wait()


def hand_on(*refs):
    sources, targets, held, sem = refs[:3], refs[3:6], refs[6:9], refs[9]
    reads = [pltpu.make_async_copy(sources[n], held[n], sem.at[0, n]) for n in range(3)]
    writes = [pltpu.make_async_copy(held[n], targets[n], sem.at[1, n]) for n in range(3)]
    for copy in reads:
        copy.start()
    for read, write in zip(reads, writes):
        read.wait()
        write.start()
    for copy in writes:
        copy.wait()


def body(
    queries, response_key_value, prompt_kv, prompt_group, response_order, live_blocks,
    out_weight, grad_out,
):
    hbm = pl.BlockSpec(memory_space=pl.ANY)
    smem = pl.BlockSpec(memory_space=pltpu.SMEM)
    block = (BLOCK, HEAD)
    square = (WIDTH, WIDTH)

    def space(*shape, kind=BF16):
        return pltpu.VMEM(shape, kind)

    def streams():
        return [[space(GROUPS, *block) for _ in range(2)] for _ in range(2)]

    scratch = [
        space(*queries.shape),
        space(*response_key_value.shape),
        space(*prompt_kv.shape),
        space(*grad_out.shape),
        space(*queries.shape),
        space(*response_key_value.shape),
        space(2, GROUPS, *block),
        space(PIECES, *square),
        space(NX, TOKENS, WIDTH),
        space(NX, TOKENS, WIDTH),
        space(TOKENS, WIDTH),
        space(NY, TOKENS, WIDTH),
        space(NY, TOKENS, WIDTH),
        space(NY, WIDTH, HEAD),
        space(NY, WIDTH, HEAD),
        space(2, GROUPS, *block),
        streams(),
        space(2, 2, NY, *block),
        space(2, 2, NY, *block),
        space(2, 2, 2, *block),
        space(2, NY, KEYS, HEAD),
        space(NY, KEYS, WIDTH),
        space(TOKENS, WIDTH),
        space(NY, KEYS, WIDTH),
        space(TOKENS, WIDTH),
        space(NY, KEYS, WIDTH, kind=F32),
        space(TOKENS, WIDTH, kind=F32),
        space(NY, KEYS, WIDTH),
        space(TOKENS, WIDTH),
        space(NY, 8, WIDTH, kind=F32),
        space(NY, 8, WIDTH, kind=F32),
        space(NY, 8, WIDTH, kind=F32),
        space(NY, 8, WIDTH, kind=F32),
        space(NY, 8, WIDTH, kind=F32),
        space(NY, 8, WIDTH, kind=F32),
        space(8, WIDTH, kind=F32),
        space(NY, 8, WIDTH, kind=F32),
        space(8, WIDTH, kind=F32),
        space(NY, 8, WIDTH, kind=F32),
        space(2, 2, NY, *block),
        space(2, 2, NY, *block),
        space(2, NY, *block),
        space(2, 2, NY, *block),
        space(2, 2, NY, *block),
        space(2, 2, 2, *block),
        space(2, 2, GROUPS, *block),
        streams(),
        space(2, NY, 3 * BLOCK, HEAD, kind=F32),
        space(NY, HEAD, WIDTH),
        space(NY, HEAD, WIDTH),
        pltpu.SMEM(((NY + 20) * GROUPS,), F32),
        pltpu.SemaphoreType.DMA((4,)),
        pltpu.SemaphoreType.DMA((4,)),
        pltpu.SemaphoreType.DMA((PIECES,)),
        pltpu.SemaphoreType.DMA((N_COPIES,)),
        pltpu.SemaphoreType.DMA((N_COPIES,)),
    ]
    kinds = tuple(
        jax.ShapeDtypeStruct(a.shape, BF16) for a in (queries, response_key_value, prompt_kv)
    )
    outs = pl.pallas_call(
        kernel,
        out_shape=kinds,
        in_specs=[hbm, hbm, hbm, smem, smem, smem, hbm, hbm],
        out_specs=(hbm, hbm, hbm),
        scratch_shapes=scratch,
        compiler_params=pltpu.CompilerParams(
            collective_id=0, has_side_effects=True, vmem_limit_bytes=56 * 1024 * 1024
        ),
        cost_estimate=pl.CostEstimate(
            flops=3_000_000_000, bytes_accessed=8_000_000, transcendentals=1_400_000
        ),
    )(
        queries, response_key_value, prompt_kv, prompt_group, response_order, live_blocks,
        out_weight, grad_out,
    )
    return pl.pallas_call(
        hand_on,
        out_shape=kinds,
        in_specs=[hbm, hbm, hbm],
        out_specs=(hbm, hbm, hbm),
        scratch_shapes=[pltpu.VMEM(a.shape, BF16) for a in kinds]
        + [pltpu.SemaphoreType.DMA((2, 3))],
        compiler_params=pltpu.CompilerParams(vmem_limit_bytes=56 * 1024 * 1024),
    )(*outs)


def solution(mesh):
    return jax.shard_map(
        body,
        mesh=mesh,
        in_specs=(
            P("dp", "tensor"),
            P("dp", "tensor"),
            P("dp", None, None, "tensor"),
            P("dp", None),
            P(),
            P("dp"),
            P("tensor", None),
            P("dp", "tensor"),
        ),
        out_specs=(P("dp", "tensor"), P("dp", "tensor"), P("dp", None, None, "tensor")),
        check_vma=False,
    )
```

```python
import math

import jax
import jax.numpy as jnp
from jax import lax
from jax.experimental import pallas as pl
from jax.experimental.pallas import tpu as pltpu
from jax.sharding import PartitionSpec as P

HEAD = 128
HEADS = 5
WIDTH = HEAD * HEADS
TOKENS = 128
BLOCK = 64
GROUPS = 8
NY, NZ, NX = 4, 8, 4
PIECES = 8
KEYS = NZ * BLOCK
SCALE = 1.0 / math.sqrt(HEAD)
EXP2_SCALE = SCALE * math.log2(math.e)
N_COPIES = 80
MESH = pl.DeviceIdType.MESH
BF16, F32 = jnp.bfloat16, jnp.float32


def mm(a, b):
    return jnp.dot(a, b, preferred_element_type=F32)


def mm_t(a, b):
    return lax.dot_general(a, b, (((1,), (1,)), ((), ())), preferred_element_type=F32)


def fold(x, op):
    return op(x.reshape(x.shape[0] // 8, 8, x.shape[1]), axis=0)


def each(count, step):
    def run(index, carry):
        step(index)
        return carry

    lax.fori_loop(0, count, run, 0)


def each_pair(count, step):
    def both(index):
        step(2 * index)
        step(2 * index + 1)

    each(count // 2, both)


def kernel(
    q_ref, rkv_ref, pkv_ref, pg_ref, ro_ref, lb_ref, w_ref, go_ref,
    oq_ref, or_ref, op_ref,
    q_v, rkv_v, pkv_v, go_v,
    w_v, gox, gos, g_own, q_buf, g_buf, qs, gs,
    own, r1, st2, st3, st4, kv,
    e_buf, e_own, p_buf, p_own, dp_buf, dp_own, ds_buf, ds_own,
    tops, sums, dots, coef, shares, row_delta, stat_out, stat_in, del_out, del_in,
    s2, s3, s4, q2, q3, q4, summed, back_in, dkv, dq_send, dq_recv,
    marks, in_sem, w_sem, send_sem, recv_sem,
):
    dp = lax.axis_index("dp")
    tensor = lax.axis_index("tensor")
    y, z = dp // NZ, dp % NZ
    x, core = tensor // 2, tensor % 2

    def at_z(step):
        return (y * NZ + (z + step + NZ) % NZ, tensor)

    def at_y(step):
        return (((y + step + NY) % NY) * NZ + z, tensor)

    def at_x(step):
        return (dp, ((x + step + NX) % NX) * 2 + core)

    sibling = (dp, x * 2 + 1 - core)

    numbers = {}
    started = []

    def remote(name, src, dst, device):
        n = numbers.setdefault(name, len(numbers))
        return pltpu.make_async_remote_copy(
            src_ref=src, dst_ref=dst, send_sem=send_sem.at[n], recv_sem=recv_sem.at[n],
            device_id=device, device_id_type=MESH,
        )

    def go(copy):
        copy.start()
        started.append(copy)

    barrier = pltpu.get_barrier_semaphore()
    partners = [at_z(step) for step in (1, -1, 2, -2, 3, -3)]
    partners += [at_y(1), at_y(2), at_y(3), at_x(1), at_x(-1), sibling]
    for partner in partners:
        pl.semaphore_signal(barrier, inc=1, device_id=partner, device_id_type=MESH)
    in_copies = [
        pltpu.make_async_copy(src, dst, in_sem.at[n])
        for n, (src, dst) in enumerate(
            [(pkv_ref, pkv_v), (go_ref, go_v), (q_ref, q_v), (rkv_ref, rkv_v)]
        )
    ]
    for copy in in_copies:
        copy.start()

    w_copies = []
    for r in range(NX):
        for other in range(2):
            piece = ((x + r) % NX) * 2 + (core if other == 0 else 1 - core)
            copy = pltpu.make_async_copy(
                w_ref.at[:, pl.ds(pl.multiple_of(piece * WIDTH, WIDTH), WIDTH)],
                w_v.at[r * 2 + other], w_sem.at[r * 2 + other],
            )
            copy.start()
            w_copies.append(copy)

    in_copies[0].wait()
    for g in range(GROUPS):
        slot = jnp.int32(0)
        for c in range(GROUPS):
            slot = jnp.where(pg_ref[0, c] == g, c, slot)
        block = pkv_v[0, slot]
        own[0, g] = block[:, :HEAD]
        own[1, g] = block[:, HEAD:]
    for copy in in_copies[1:]:
        copy.wait()
    pl.semaphore_wait(barrier, len(partners))

    def hop(step, c, d):
        sign = 1 if d == 0 else -1
        src, dst, device = {
            1: (own.at[c], r1[c][d], at_z(sign)),
            2: (st2.at[c, d], kv.at[c, :, pl.ds((3 + d) * BLOCK, BLOCK)], at_z(sign)),
            3: (st3.at[c, d], kv.at[c, :, pl.ds((5 + d) * BLOCK, BLOCK)], at_z(2 * sign)),
            4: (
                st4.at[c, d], kv.at[c, pl.ds(2 * d, 2), pl.ds(7 * BLOCK, BLOCK)],
                at_z(3 * sign),
            ),
        }[step]
        return remote(("hop", step, c, d), src, dst, device)

    half = TOKENS // 2

    def ring_copy(name, src, buf, before, after, way, part):
        rows = pl.ds(part * half, half)
        dst = buf.at[1 if way == 0 else 3, rows]
        return remote((name, way, part), src.at[rows], dst, before if way == 0 else after)

    def ring_pass(name, buf, before, after, way):
        rows = pl.ds(way * half, half)
        return remote(
            (name, way, 2), buf.at[1 if way == 0 else 3, rows], buf.at[2, rows],
            before if way == 0 else after,
        )

    def ring_first(*ring):
        for turn in range(2):
            for way in range(2):
                go(ring_copy(*ring, way, way if turn == 0 else 1 - way))

    def ring_second(name, src, buf, before, after):
        for way in range(2):
            ring_copy(name, src, buf, before, after, way, way).wait_recv()
            go(ring_pass(name, buf, before, after, way))

    def ring_rest(name, src, buf, before, after):
        for way in range(2):
            ring_copy(name, src, buf, before, after, way, 1 - way).wait_recv()

    def ring_last(name, src, buf, before, after):
        for way in range(2):
            ring_pass(name, buf, before, after, way).wait_recv()

    x_ring = ("x", go_v, gox, at_x(-1), at_x(1))
    q_ring = ("q", q_v, q_buf, at_y(-1), at_y(1))
    g_ring = ("g", g_own, g_buf, at_y(-1), at_y(1))

    def share(r):
        src = go_v if r == 0 else gox.at[r]
        return remote(("share", r), src, gos.at[r], sibling)

    ring_first(*x_ring)
    for d in range(2):
        go(hop(1, 0, d))
    go(share(0))

    groups = {
        step: [ro_ref[((y + j) % NY) * NZ + (z + step + NZ) % NZ] // 4 for j in range(NY)]
        for step in range(-3, 4)
    }
    my_groups = groups[0]

    def relay(c):
        for d in range(2):
            sign = 1 if d == 0 else -1
            hop(1, c, d).wait_recv()
            for i in range(2):
                st4[c, d, i] = r1[c][d][groups[3 * sign][2 * d + i]]
            go(hop(4, c, d))
            for j in range(NY):
                st3[c, d, j] = r1[c][d][groups[2 * sign][j]]
            go(hop(3, c, d))
            for j in range(NY):
                st2[c, d, j] = r1[c][d][groups[sign][j]]
            go(hop(2, c, d))

    def stack_heads(raw, stacked, j):
        for h in range(HEADS):
            stacked[j, h * HEAD : (h + 1) * HEAD, :] = raw[:, h * HEAD : (h + 1) * HEAD]

    levels = [(0, 1), (1, 2), (3, 2), (5, 3)]

    def weigh(s):
        top = jnp.max(fold(s, jnp.max), axis=0, keepdims=True)
        e = jnp.exp2((s - top) * EXP2_SCALE)
        return top, e, jnp.sum(fold(e, jnp.sum), axis=0, keepdims=True)

    def scores(j, level):
        first, count = levels[level][0] * BLOCK, levels[level][1] * BLOCK
        top, e, total = weigh(mm_t(kv[0, j, first : first + count, :], qs[j]))
        e_buf[j, first : first + count, :] = e.astype(BF16)
        tops[j, level : level + 1, :] = top
        sums[j, level : level + 1, :] = total

    def slopes(j, level):
        first, count = levels[level][0] * BLOCK, levels[level][1] * BLOCK
        terms = mm_t(kv[1, j, first : first + count, :], gs[j])
        dp_buf[j, first : first + count, :] = terms
        products = terms * e_buf[j, first : first + count, :].astype(F32)
        dots[j, level : level + 1, :] = jnp.sum(fold(products, jnp.sum), axis=0, keepdims=True)

    def take(c, level):
        for j in range(NY):
            g = my_groups[j]
            if level == 0:
                kv[c, j, 0:BLOCK, :] = own[c, g]
            else:
                kv[c, j, BLOCK : 2 * BLOCK, :] = r1[c][0][g]
                kv[c, j, 2 * BLOCK : 3 * BLOCK, :] = r1[c][1][g]

    def arrived(c, steps):
        for step in steps:
            for d in range(2):
                hop(step, c, d).wait_recv()

    def project(piece, block):
        w_copies[piece].wait()
        return mm_t(w_v[piece], block[...])

    grad = project(0, go_v)
    for d in range(2):
        go(hop(1, 1, d))
    tops[...] = jnp.full(tops.shape, -jnp.inf, F32)
    sums[...] = jnp.zeros(sums.shape, F32)
    dots[...] = jnp.zeros(dots.shape, F32)
    del_out[...] = jnp.zeros(del_out.shape, F32)
    share(0).wait_recv()
    grad = grad + project(1, gos.at[0])

    stack_heads(q_v[...], qs, 0)
    s = mm_t(rkv_v[:, :HEAD], qs[0])
    key_pos = lax.broadcasted_iota(jnp.int32, s.shape, 0)
    query_pos = lax.broadcasted_iota(jnp.int32, s.shape, 1) % TOKENS
    top, e, total = weigh(jnp.where(key_pos <= query_pos, s, -jnp.inf))
    e_own[...] = e.astype(BF16)
    tops[0, 5:6, :] = top
    sums[0, 5:6, :] = total

    ring_second(*x_ring)
    ring_rest(*x_ring)
    go(share(1))
    go(share(3))
    relay(0)
    ring_first(*q_ring)
    grad = grad + project(2, gox.at[1])
    grad = grad + project(6, gox.at[3])
    ring_last(*x_ring)
    go(share(2))
    share(1).wait_recv()
    grad = grad + project(3, gos.at[1])
    share(3).wait_recv()
    grad = grad + project(7, gos.at[3])
    relay(1)
    ring_second(*q_ring)
    grad = grad + project(4, gox.at[2])
    share(2).wait_recv()
    grad = grad + project(5, gos.at[2])
    column = lax.broadcasted_iota(jnp.int32, grad.shape, 1)
    grad = jnp.where(column < lb_ref[0] * TOKENS, grad, 0.0).astype(BF16)
    for h in range(HEADS):
        head = grad[h * HEAD : (h + 1) * HEAD, :].T
        gs[0, h * HEAD : (h + 1) * HEAD, :] = head
        g_own[:, h * HEAD : (h + 1) * HEAD] = head
    ring_first(*g_ring)
    ring_rest(*q_ring)
    for level in range(2):
        take(0, level)
        take(1, level)
    for j in (1, 3):
        stack_heads(q_buf[j], qs, j)
    for j in (0, 1, 3):
        scores(j, 0)
        scores(j, 1)
    ring_last(*q_ring)
    stack_heads(q_buf[2], qs, 2)
    scores(2, 0)
    scores(2, 1)
    arrived(0, (2,))
    each(NY, lambda j: scores(j, 2))
    ring_second(*g_ring)
    arrived(0, (3, 4))
    each(NY, lambda j: scores(j, 3))

    for j in range(NY):
        top = jnp.max(tops[j], axis=0, keepdims=True)
        share_of = jnp.exp2((tops[j] - top) * EXP2_SCALE)
        shares[j] = share_of
        stat_out[j : j + 1, :] = top
        stat_out[NY + j : NY + j + 1, :] = jnp.sum(sums[j] * share_of, axis=0, keepdims=True)

    def stat(k):
        return remote(("stat", k), stat_out, stat_in.at[k], at_y(k))

    def delta(k):
        return remote(("delta", k), del_out, del_in.at[k], at_y(k))

    for k in range(1, NY):
        go(stat(k))
    ring_rest(*g_ring)
    for j in (1, 3):
        stack_heads(g_buf[j], gs, j)
    for j in (0, 1, 3):
        slopes(j, 0)
        slopes(j, 1)
    terms = mm_t(rkv_v[:, HEAD:], gs[0])
    dp_own[...] = terms
    products = terms * e_own[...].astype(F32)
    dots[0, 5:6, :] = jnp.sum(fold(products, jnp.sum), axis=0, keepdims=True)
    ring_last(*g_ring)
    stack_heads(g_buf[2], gs, 2)
    for k in range(1, NY):
        stat(k).wait_recv()
    for j in range(NY):
        mine = stat_out[j : j + 1, :]
        others = [stat_in[k, (j + k) % NY : (j + k) % NY + 1, :] for k in range(1, NY)]
        highest = mine
        for other in others:
            highest = jnp.maximum(highest, other)
        factors = [jnp.exp2((top - highest) * EXP2_SCALE) for top in [mine] + others]
        total = stat_out[NY + j : NY + j + 1, :] * factors[0]
        for k in range(1, NY):
            line = NY + (j + k) % NY
            total = total + stat_in[k, line : line + 1, :] * factors[k]
        for k in range(NY):
            row_delta[k, j : j + 1, :] = factors[k] / total
        coef[j] = shares[j] * (factors[0] / total)

    def back(step, c, d):
        sign = -1 if d == 0 else 1
        src, dst, device = {
            2: (s2.at[c, d], q2.at[c, d], at_z(sign)),
            3: (s3.at[c, d], q3.at[c, d], at_z(2 * sign)),
            4: (s4.at[c, pl.ds(2 * d, 2)], q4.at[c, d], at_z(3 * sign)),
            1: (summed.at[c, d], back_in[c][d], at_z(sign)),
        }[step]
        return remote(("back", step, c, d), src, dst, device)

    def fill(c, j, level):
        first, count = levels[level][0] * BLOCK, levels[level][1] * BLOCK
        rows = slice(first, first + count)
        if c == 1:
            p_buf[j, rows, :] = (
                e_buf[j, rows, :].astype(F32) * coef[j, level : level + 1, :]
            ).astype(BF16)
        else:
            ds_buf[j, rows, :] = (
                p_buf[j, rows, :].astype(F32) * (dp_buf[j, rows, :] - row_delta[0, pl.ds(j, 1), :])
            ).astype(BF16)

    def grads(c, j, first, count):
        if c == 1:
            return mm(p_buf[j, first : first + count, :], gs[j])
        return mm(ds_buf[j, first : first + count, :], qs[j]) * SCALE

    def far(c):
        def outer(j):
            fill(c, j, 3)
            terms = grads(c, j, 5 * BLOCK, 3 * BLOCK).astype(BF16)
            s3[c, 0, j] = terms[:BLOCK]
            s3[c, 1, j] = terms[BLOCK : 2 * BLOCK]
            s4[c, j] = terms[2 * BLOCK :]

        def inner(j):
            fill(c, j, 2)
            terms = grads(c, j, 3 * BLOCK, 2 * BLOCK).astype(BF16)
            s2[c, 0, j] = terms[:BLOCK]
            s2[c, 1, j] = terms[BLOCK:]

        each(NY, outer)
        for step in (4, 3):
            for d in range(2):
                go(back(step, c, d))
        each(NY, inner)
        for d in range(2):
            go(back(2, c, d))

    def near(c):
        def one(j):
            for level in range(2):
                fill(c, j, level)
            dkv[c, j] = grads(c, j, 0, 3 * BLOCK)

        each(NY, one)

    def my_terms(c, first, g):
        total = dkv[c, 0, first : first + BLOCK, :] * marks[g]
        for j in range(1, NY):
            total = total + dkv[c, j, first : first + BLOCK, :] * marks[j * GROUPS + g]
        return total

    def add_up(c):
        for d in range(2):
            for step in (4, 3, 2):
                back(step, c, d).wait_recv()

            def one(g):
                total = my_terms(c, (1 + d) * BLOCK, g)
                for i in range(NY):
                    base = NY + 10 * d + i
                    total = total + q2[c, d, i].astype(F32) * marks[base * GROUPS + g]
                    total = total + q3[c, d, i].astype(F32) * marks[(base + 4) * GROUPS + g]
                for i in range(2):
                    total = total + q4[c, d, i].astype(F32) * marks[
                        (NY + 10 * d + 8 + i) * GROUPS + g
                    ]
                summed[c, d, g] = total.astype(BF16)

            each_pair(GROUPS, one)
            go(back(1, c, d))

    def finish(c):
        for d in range(2):
            back(1, c, d).wait_recv()
        for slot in range(GROUPS):
            g = pg_ref[0, slot]
            total = back_in[c][0][g].astype(F32) + back_in[c][1][g].astype(F32)
            op_ref[0, slot, :, c * HEAD : (c + 1) * HEAD] = (
                total + my_terms(c, 0, g)
            ).astype(BF16)

    far(1)
    slopes(2, 0)
    slopes(2, 1)
    arrived(1, (2,))
    each(NY, lambda j: slopes(j, 2))
    arrived(1, (3, 4))
    each(NY, lambda j: slopes(j, 3))
    for j in range(NY):
        del_out[j : j + 1, :] = jnp.sum(dots[j] * shares[j], axis=0, keepdims=True)
    for k in range(1, NY):
        go(delta(k))
    near(1)
    for k in range(1, NY):
        delta(k).wait_recv()
    for j in range(NY):
        total = del_out[j : j + 1, :] * row_delta[0, j : j + 1, :]
        for k in range(1, NY):
            line = (j + k) % NY
            total = total + del_in[k, line : line + 1, :] * row_delta[k, j : j + 1, :]
        row_delta[0, j : j + 1, :] = total
    far(0)
    listed = list(my_groups)
    for d, sign in ((0, 1), (1, -1)):
        listed += groups[sign] + groups[2 * sign] + groups[3 * sign][2 * d : 2 * d + 2]
    for n, group in enumerate(listed):
        for g in range(GROUPS):
            marks[n * GROUPS + g] = jnp.where(group == g, 1.0, 0.0).astype(F32)
    near(0)
    p_own[...] = (e_own[...].astype(F32) * coef[0, 5:6, :]).astype(BF16)
    ds_own[...] = (
        p_own[...].astype(F32) * (dp_own[...] - row_delta[0, 0:1, :])
    ).astype(BF16)

    def dq_copy(j):
        return remote(("dq", j), dq_send.at[j], dq_recv.at[j], at_y(j))

    for j in range(1, NY):
        dq_send[j] = mm(kv[0, j].T, ds_buf[j]).astype(BF16)
        go(dq_copy(j))
    add_up(1)
    or_ref[:, :HEAD] = (mm(ds_own[...], qs[0]) * SCALE).astype(BF16)
    or_ref[:, HEAD:] = mm(p_own[...], gs[0]).astype(BF16)
    dq = mm(kv[0, 0].T, ds_buf[0]) + mm(rkv_v[:, :HEAD].T, ds_own[...])
    add_up(0)
    for j in range(1, NY):
        dq_copy(j).wait_recv()
        dq = dq + dq_recv[j].astype(F32)
    dq = dq * SCALE
    for h in range(HEADS):
        oq_ref[:, h * HEAD : (h + 1) * HEAD] = dq[:, h * HEAD : (h + 1) * HEAD].T.astype(BF16)
    finish(1)
    for copy in started:
        copy.wait_send()
    finish(0)


def hand_on(*refs):
    sem = refs[6]
    copies = [pltpu.make_async_copy(refs[n], refs[3 + n], sem.at[n]) for n in range(3)]
    for copy in copies:
        copy.start()
    for copy in copies:
        copy.wait()


def body(
    queries, response_key_value, prompt_kv, prompt_group, response_order, live_blocks,
    out_weight, grad_out,
):
    hbm = pl.BlockSpec(memory_space=pl.ANY)
    vmem = pl.BlockSpec(memory_space=pltpu.VMEM)
    smem = pl.BlockSpec(memory_space=pltpu.SMEM)
    block = (BLOCK, HEAD)
    square = (WIDTH, WIDTH)

    def space(*shape, kind=BF16):
        return pltpu.VMEM(shape, kind)

    def streams():
        return [[space(GROUPS, *block) for _ in range(2)] for _ in range(2)]

    scratch = [
        space(*queries.shape),
        space(*response_key_value.shape),
        space(*prompt_kv.shape),
        space(*grad_out.shape),
        space(PIECES, *square),
        space(NX, TOKENS, WIDTH),
        space(NX, TOKENS, WIDTH),
        space(TOKENS, WIDTH),
        space(NY, TOKENS, WIDTH),
        space(NY, TOKENS, WIDTH),
        space(NY, WIDTH, HEAD),
        space(NY, WIDTH, HEAD),
        space(2, GROUPS, *block),
        streams(),
        space(2, 2, NY, *block),
        space(2, 2, NY, *block),
        space(2, 2, 2, *block),
        space(2, NY, KEYS, HEAD),
        space(NY, KEYS, WIDTH),
        space(TOKENS, WIDTH),
        space(NY, KEYS, WIDTH),
        space(TOKENS, WIDTH),
        space(NY, KEYS, WIDTH, kind=F32),
        space(TOKENS, WIDTH, kind=F32),
        space(NY, KEYS, WIDTH),
        space(TOKENS, WIDTH),
        space(NY, 8, WIDTH, kind=F32),
        space(NY, 8, WIDTH, kind=F32),
        space(NY, 8, WIDTH, kind=F32),
        space(NY, 8, WIDTH, kind=F32),
        space(NY, 8, WIDTH, kind=F32),
        space(NY, 8, WIDTH, kind=F32),
        space(8, WIDTH, kind=F32),
        space(NY, 8, WIDTH, kind=F32),
        space(8, WIDTH, kind=F32),
        space(NY, 8, WIDTH, kind=F32),
        space(2, 2, NY, *block),
        space(2, 2, NY, *block),
        space(2, NY, *block),
        space(2, 2, NY, *block),
        space(2, 2, NY, *block),
        space(2, 2, 2, *block),
        space(2, 2, GROUPS, *block),
        streams(),
        space(2, NY, 3 * BLOCK, HEAD, kind=F32),
        space(NY, HEAD, WIDTH),
        space(NY, HEAD, WIDTH),
        pltpu.SMEM(((NY + 20) * GROUPS,), F32),
        pltpu.SemaphoreType.DMA((4,)),
        pltpu.SemaphoreType.DMA((PIECES,)),
        pltpu.SemaphoreType.DMA((N_COPIES,)),
        pltpu.SemaphoreType.DMA((N_COPIES,)),
    ]
    kinds = tuple(
        jax.ShapeDtypeStruct(a.shape, BF16) for a in (queries, response_key_value, prompt_kv)
    )
    outs = pl.pallas_call(
        kernel,
        out_shape=tuple(pltpu.VMEM(a.shape, BF16) for a in kinds),
        in_specs=[hbm, hbm, hbm, smem, smem, smem, hbm, hbm],
        out_specs=(vmem, vmem, vmem),
        scratch_shapes=scratch,
        compiler_params=pltpu.CompilerParams(
            collective_id=0, has_side_effects=True, vmem_limit_bytes=56 * 1024 * 1024
        ),
        cost_estimate=pl.CostEstimate(
            flops=3_000_000_000, bytes_accessed=8_000_000, transcendentals=1_400_000
        ),
    )(
        queries, response_key_value, prompt_kv, prompt_group, response_order, live_blocks,
        out_weight, grad_out,
    )
    return pl.pallas_call(
        hand_on,
        out_shape=kinds,
        in_specs=[vmem, vmem, vmem],
        out_specs=(hbm, hbm, hbm),
        scratch_shapes=[pltpu.SemaphoreType.DMA((3,))],
    )(*outs)


def solution(mesh):
    return jax.shard_map(
        body,
        mesh=mesh,
        in_specs=(
            P("dp", "tensor"),
            P("dp", "tensor"),
            P("dp", None, None, "tensor"),
            P("dp", None),
            P(),
            P("dp"),
            P("tensor", None),
            P("dp", "tensor"),
        ),
        out_specs=(P("dp", "tensor"), P("dp", "tensor"), P("dp", None, None, "tensor")),
        check_vma=False,
    )
```

```python
import math

import jax
import jax.numpy as jnp
from jax import lax
from jax.experimental import pallas as pl
from jax.experimental.pallas import tpu as pltpu
from jax.sharding import PartitionSpec as P

HEAD = 128
HEADS = 5
WIDTH = HEAD * HEADS
TOKENS = 128
BLOCK = 64
GROUPS = 8
NY, NZ, NX = 4, 8, 4
PIECES = 8
PROMPT = NZ * NY * BLOCK
SLOT = NY * BLOCK
SCALE = 1.0 / math.sqrt(HEAD)
EXP2_SCALE = SCALE * math.log2(math.e)
N_COPIES = 150
MESH = pl.DeviceIdType.MESH
BF16, F32 = jnp.bfloat16, jnp.float32

def mm(a, b):
    return jnp.dot(a, b, preferred_element_type=F32)


def mm_t(a, b):
    return lax.dot_general(a, b, (((1,), (1,)), ((), ())), preferred_element_type=F32)


def fold(x, op):
    return op(x.reshape(x.shape[0] // 8, 8, x.shape[1]), axis=0)


def each(count, step):
    def run(index, carry):
        step(index)
        return carry

    lax.fori_loop(0, count, run, 0)


def each_pair(count, step):
    def both(index):
        step(2 * index)
        step(2 * index + 1)

    each(count // 2, both)


LEVELS = [(0,), (1, 2), (3, 4), (5, 6, 7)]
LAST = 8


def kernel(
    q_ref, rkv_ref, pkv_ref, pg_ref, ro_ref, lb_ref, w_ref, go_ref,
    oq_ref, or_ref, op_ref,
    q_v, pkv_v, go_v,
    w_v, gox, gos, qs, gs,
    own, r1, picked, picked_own, kv,
    e_buf, p_buf, dp_buf, ds_buf,
    tops, sums, dots, coef, row_delta,
    terms, relayed, direct, summed, back_in,
    marks, in_sem, w_sem, send_sem, recv_sem,
):
    dp = lax.axis_index("dp")
    tensor = lax.axis_index("tensor")
    y, z = dp // NZ, dp % NZ
    x, core = tensor // 2, tensor % 2

    def at(dy, dz):
        return (((y + dy) % NY) * NZ + (z + dz + NZ) % NZ, tensor)

    def at_x(step):
        return (dp, ((x + step + NX) % NX) * 2 + core)

    sibling = (dp, x * 2 + 1 - core)

    numbers = {}
    started = []

    def remote(name, src, dst, device):
        n = numbers.setdefault(name, len(numbers))
        return pltpu.make_async_remote_copy(
            src_ref=src, dst_ref=dst, send_sem=send_sem.at[n], recv_sem=recv_sem.at[n],
            device_id=device, device_id_type=MESH,
        )

    def go(copy):
        copy.start()
        started.append(copy)

    barrier = pltpu.get_barrier_semaphore()
    partners = [at(dy, dz) for dz in range(-3, 4) for dy in range(NY) if (dy, dz) != (0, 0)]
    partners += [at_x(1), at_x(-1), sibling]
    for partner in partners:
        pl.semaphore_signal(barrier, inc=1, device_id=partner, device_id_type=MESH)
    in_copies = [
        pltpu.make_async_copy(src, dst, in_sem.at[n])
        for n, (src, dst) in enumerate(
            [
                (pkv_ref, pkv_v), (go_ref, go_v), (q_ref, q_v),
                (rkv_ref.at[:, pl.ds(0, HEAD)], kv.at[0, pl.ds(PROMPT, TOKENS)]),
                (rkv_ref.at[:, pl.ds(HEAD, HEAD)], kv.at[1, pl.ds(PROMPT, TOKENS)]),
            ]
        )
    ]
    for copy in in_copies:
        copy.start()

    w_copies = []
    for r in range(NX):
        for other in range(2):
            piece = ((x + r) % NX) * 2 + (core if other == 0 else 1 - core)
            copy = pltpu.make_async_copy(
                w_ref.at[:, pl.ds(pl.multiple_of(piece * WIDTH, WIDTH), WIDTH)],
                w_v.at[r * 2 + other], w_sem.at[r * 2 + other],
            )
            copy.start()
            w_copies.append(copy)

    groups = {
        dz: [ro_ref[((y + dy) % NY) * NZ + (z + dz + NZ) % NZ] // 4 for dy in range(NY)]
        for dz in range(-3, 4)
    }

    in_copies[0].wait()
    for g in range(GROUPS):
        slot = jnp.int32(0)
        for c in range(GROUPS):
            slot = jnp.where(pg_ref[0, c] == g, c, slot)
        block = pkv_v[0, slot]
        own[0, g] = block[:, :HEAD]
        own[1, g] = block[:, HEAD:]
    for c in range(2):
        for dy in range(NY):
            if dy == 0:
                kv[c, 0:BLOCK, :] = own[c, groups[0][0]]
            else:
                picked_own[c, dy] = own[c, groups[0][dy]]
    for copy in in_copies[1:]:
        copy.wait()
    pl.semaphore_wait(barrier, len(partners))

    def first_hop(c, d):
        return remote(("first", c, d), own.at[c], r1[c][d], at(0, 1 if d == 0 else -1))

    def place(slot, dy):
        return pl.ds(slot * SLOT + (dy % NY) * BLOCK, BLOCK)

    def own_copy(c, dy):
        return remote(
            ("own", c, dy), picked_own.at[c, dy], kv.at[c, place(0, -dy)], at(dy, 0)
        )

    def forward(c, d, m, dy):
        slot = 7 if m == 3 else 1 + d + 2 * m
        return remote(
            ("forward", c, d, m, dy), picked.at[c, d, m, dy], kv.at[c, place(slot, -dy)],
            at(dy, m if d == 0 else -m),
        )

    def sent(d, m):
        if m == 3:
            return (2 * d, 2 * d + 1)
        return (1, 2, 3) if m == 0 else (0, 1, 2, 3)

    def relay(c):
        for d in range(2):
            sign = 1 if d == 0 else -1
            first_hop(c, d).wait_recv()
            for m in (3, 2, 1, 0):
                for dy in sent(d, m):
                    picked[c, d, m, dy] = r1[c][d][groups[sign * m][dy]]
                    go(forward(c, d, m, dy))
            kv[c, (1 + d) * SLOT : (1 + d) * SLOT + BLOCK, :] = r1[c][d][groups[0][0]]

    def arrived(c, level):
        if level == 0:
            for dy in range(1, NY):
                own_copy(c, dy).wait_recv()
        else:
            for m in (3, 2) if level == 3 else (level - 1,):
                for d in range(2):
                    for dy in sent(d, m):
                        forward(c, d, m, dy).wait_recv()

    half = TOKENS // 2

    def x_copy(way, part):
        rows = pl.ds(part * half, half)
        return remote(
            ("x", way, part), go_v.at[rows], gox.at[1 if way == 0 else 3, rows],
            at_x(-1 if way == 0 else 1),
        )

    def x_pass(way):
        rows = pl.ds(way * half, half)
        return remote(
            ("x", way, 2), gox.at[1 if way == 0 else 3, rows], gox.at[2, rows],
            at_x(-1 if way == 0 else 1),
        )

    def share(r):
        src = go_v if r == 0 else gox.at[r]
        return remote(("share", r), src, gos.at[r], sibling)

    for way in range(2):
        go(x_copy(way, way))
    for d in range(2):
        go(first_hop(0, d))
    for way in range(2):
        go(x_copy(way, 1 - way))
    go(share(0))
    for dy in range(1, NY):
        go(own_copy(0, dy))

    def rows_of(chunk):
        if isinstance(chunk, int) and chunk == LAST:
            return pl.ds(PROMPT, TOKENS)
        return pl.ds(pl.multiple_of(chunk * SLOT, SLOT), SLOT)

    def scores(chunk):
        rows = rows_of(chunk)
        s = mm_t(kv[0, rows, :], qs[...])
        if isinstance(chunk, int) and chunk == LAST:
            key_pos = lax.broadcasted_iota(jnp.int32, s.shape, 0)
            query_pos = lax.broadcasted_iota(jnp.int32, s.shape, 1) % TOKENS
            s = jnp.where(key_pos <= query_pos, s, -jnp.inf)
        top = jnp.max(fold(s, jnp.max), axis=0, keepdims=True)
        e = jnp.exp2((s - top) * EXP2_SCALE)
        e_buf[rows, :] = e.astype(BF16)
        tops[chunk] = top
        sums[chunk] = jnp.sum(fold(e, jnp.sum), axis=0, keepdims=True)

    def slopes(chunk):
        rows = rows_of(chunk)
        values = mm_t(kv[1, rows, :], gs[...])
        dp_buf[rows, :] = values
        products = values * e_buf[rows, :].astype(F32)
        dots[chunk] = jnp.sum(fold(products, jnp.sum), axis=0, keepdims=True)

    def level_of(number, step):
        slots = LEVELS[number]
        each(len(slots), lambda i: step(slots[0] + i))

    def project(piece, block):
        w_copies[piece].wait()
        return mm_t(w_v[piece], block[...])

    grad = project(0, go_v)
    for d in range(2):
        go(first_hop(1, d))
    for dy in range(1, NY):
        go(own_copy(1, dy))
    for h in range(HEADS):
        qs[h * HEAD : (h + 1) * HEAD, :] = q_v[:, h * HEAD : (h + 1) * HEAD]
    share(0).wait_recv()
    grad = grad + project(1, gos.at[0])
    scores(LAST)
    for way in range(2):
        x_copy(way, way).wait_recv()
        go(x_pass(way))
    relay(0)
    for way in range(2):
        x_copy(way, 1 - way).wait_recv()
    go(share(1))
    go(share(3))
    grad = grad + project(2, gox.at[1])
    grad = grad + project(6, gox.at[3])
    for way in range(2):
        x_pass(way).wait_recv()
    go(share(2))
    share(1).wait_recv()
    grad = grad + project(3, gos.at[1])
    share(3).wait_recv()
    grad = grad + project(7, gos.at[3])
    relay(1)
    grad = grad + project(4, gox.at[2])
    share(2).wait_recv()
    grad = grad + project(5, gos.at[2])
    column = lax.broadcasted_iota(jnp.int32, grad.shape, 1)
    grad = jnp.where(column < lb_ref[0] * TOKENS, grad, 0.0).astype(BF16)
    for h in range(HEADS):
        rows = slice(h * HEAD, (h + 1) * HEAD)
        gs[rows, :] = grad[rows, :].T

    arrived(0, 0)
    level_of(0, scores)
    slopes(LAST)
    arrived(0, 1)
    level_of(1, scores)
    arrived(1, 0)
    level_of(0, slopes)
    arrived(0, 2)
    level_of(2, scores)
    arrived(0, 3)
    level_of(3, scores)

    highest = tops[0]
    for chunk in range(1, LAST + 1):
        highest = jnp.maximum(highest, tops[chunk])
    factors = [jnp.exp2((tops[chunk] - highest) * EXP2_SCALE) for chunk in range(LAST + 1)]
    total = sums[0] * factors[0]
    for chunk in range(1, LAST + 1):
        total = total + sums[chunk] * factors[chunk]
    for chunk in range(LAST + 1):
        coef[chunk] = factors[chunk] / total

    def back(c, slot, dy):
        src = terms.at[c, place(slot, dy)]
        if slot == 0:
            dst, device = direct.at[c, -dy % NY], at(dy, 0)
        else:
            m, d = (3, dy // 2) if slot == 7 else divmod(slot - 1, 2)
            index = 12 + dy % 2 if slot == 7 else m * NY + -dy % NY
            dst, device = relayed.at[c, d, index], at(dy, -m if d == 0 else m)
        return remote(("back", c, slot, dy), src, dst, device)

    def summed_copy(c, d):
        return remote(
            ("summed", c, d), summed.at[c, d], back_in[c][d], at(0, -1 if d == 0 else 1)
        )

    def returned(slot):
        return (1, 2, 3) if slot < 3 else (0, 1, 2, 3)

    def fill(c, chunk):
        rows = rows_of(chunk)
        if c == 1:
            p = e_buf[rows, :].astype(F32) * coef[chunk]
            p_buf[rows, :] = p.astype(BF16)
            return mm(p_buf[rows, :], gs[...])
        ds = p_buf[rows, :].astype(F32) * (dp_buf[rows, :] - row_delta[...])
        ds_buf[rows, :] = ds.astype(BF16)
        return mm(ds_buf[rows, :], qs[...]) * SCALE

    def send_back(c, number):
        def one(chunk):
            terms[c, rows_of(chunk), :] = fill(c, chunk).astype(BF16)

        level_of(number, one)
        for slot in reversed(LEVELS[number]):
            for dy in returned(slot):
                go(back(c, slot, dy))

    def mark(d, i, g):
        return marks[(d * 14 + i) * GROUPS + g]

    def add_up(c):
        for d in range(2):
            for slot in (7, 5 + d, 3 + d, 1 + d):
                for dy in (2 * d, 2 * d + 1) if slot == 7 else returned(slot):
                    back(c, slot, dy).wait_recv()

            def one(g):
                mine = terms[c, (1 + d) * SLOT : (1 + d) * SLOT + BLOCK, :]
                result = mine.astype(F32) * mark(d, 0, g)
                for i in range(1, 14):
                    result = result + relayed[c, d, i].astype(F32) * mark(d, i, g)
                summed[c, d, g] = result.astype(BF16)

            each_pair(GROUPS, one)
            go(summed_copy(c, d))

    def finish(c):
        for dy in returned(0):
            back(c, 0, dy).wait_recv()
        for d in range(2):
            summed_copy(c, d).wait_recv()
        for slot in range(GROUPS):
            g = pg_ref[0, slot]
            result = back_in[c][0][g].astype(F32) + back_in[c][1][g].astype(F32)
            result = result + terms[c, 0:BLOCK, :].astype(F32) * mark(0, 0, g)
            for dy in range(1, NY):
                result = result + direct[c, dy].astype(F32) * mark(0, dy, g)
            op_ref[0, slot, :, c * HEAD : (c + 1) * HEAD] = result.astype(BF16)

    send_back(1, 3)
    send_back(1, 2)
    arrived(1, 1)
    level_of(1, slopes)
    arrived(1, 2)
    level_of(2, slopes)
    arrived(1, 3)
    level_of(3, slopes)
    delta = dots[0] * coef[0]
    for chunk in range(1, LAST + 1):
        delta = delta + dots[chunk] * coef[chunk]
    row_delta[...] = delta
    send_back(0, 3)
    send_back(0, 2)
    send_back(1, 1)
    send_back(1, 0)
    send_back(0, 1)
    send_back(0, 0)
    listed = []
    for d, sign in ((0, 1), (1, -1)):
        for m in range(3):
            listed += groups[sign * m]
        listed += [groups[sign * 3][-dy % NY] for dy in (2 * d, 2 * d + 1)]
    for n, group in enumerate(listed):
        for g in range(GROUPS):
            marks[n * GROUPS + g] = jnp.where(group == g, 1.0, 0.0).astype(F32)
    or_ref[:, HEAD:] = fill(1, LAST).astype(BF16)
    or_ref[:, :HEAD] = fill(0, LAST).astype(BF16)
    add_up(1)
    dq = mm(kv[0].T, ds_buf[...]) * SCALE
    for h in range(HEADS):
        oq_ref[:, h * HEAD : (h + 1) * HEAD] = dq[:, h * HEAD : (h + 1) * HEAD].T.astype(BF16)
    add_up(0)
    finish(1)
    for copy in started:
        copy.wait_send()
    finish(0)


def hand_on(*refs):
    sem = refs[6]
    copies = [pltpu.make_async_copy(refs[n], refs[3 + n], sem.at[n]) for n in range(3)]
    for copy in copies:
        copy.start()
    for copy in copies:
        copy.wait()


def body(
    queries, response_key_value, prompt_kv, prompt_group, response_order, live_blocks,
    out_weight, grad_out,
):
    hbm = pl.BlockSpec(memory_space=pl.ANY)
    vmem = pl.BlockSpec(memory_space=pltpu.VMEM)
    smem = pl.BlockSpec(memory_space=pltpu.SMEM)
    block = (BLOCK, HEAD)
    square = (WIDTH, WIDTH)

    def space(*shape, kind=BF16):
        return pltpu.VMEM(shape, kind)

    def streams():
        return [[space(GROUPS, *block) for _ in range(2)] for _ in range(2)]

    scratch = [
        space(*queries.shape),
        space(*prompt_kv.shape),
        space(*grad_out.shape),
        space(PIECES, *square),
        space(NX, TOKENS, WIDTH),
        space(NX, TOKENS, WIDTH),
        space(WIDTH, HEAD),
        space(WIDTH, HEAD),
        space(2, GROUPS, *block),
        streams(),
        space(2, 2, 4, NY, *block),
        space(2, NY, *block),
        space(2, PROMPT + TOKENS, HEAD),
        space(PROMPT + TOKENS, WIDTH),
        space(PROMPT + TOKENS, WIDTH),
        space(PROMPT + TOKENS, WIDTH, kind=F32),
        space(PROMPT + TOKENS, WIDTH),
        space(LAST + 1, 1, WIDTH, kind=F32),
        space(LAST + 1, 1, WIDTH, kind=F32),
        space(LAST + 1, 1, WIDTH, kind=F32),
        space(LAST + 1, 1, WIDTH, kind=F32),
        space(1, WIDTH, kind=F32),
        space(2, PROMPT, HEAD),
        space(2, 2, 14, *block),
        space(2, NY, *block),
        space(2, 2, GROUPS, *block),
        streams(),
        pltpu.SMEM((28 * GROUPS,), F32),
        pltpu.SemaphoreType.DMA((5,)),
        pltpu.SemaphoreType.DMA((PIECES,)),
        pltpu.SemaphoreType.DMA((N_COPIES,)),
        pltpu.SemaphoreType.DMA((N_COPIES,)),
    ]
    kinds = tuple(
        jax.ShapeDtypeStruct(a.shape, BF16) for a in (queries, response_key_value, prompt_kv)
    )
    outs = pl.pallas_call(
        kernel,
        out_shape=tuple(pltpu.VMEM(a.shape, BF16) for a in kinds),
        in_specs=[hbm, hbm, hbm, smem, smem, smem, hbm, hbm],
        out_specs=(vmem, vmem, vmem),
        scratch_shapes=scratch,
        compiler_params=pltpu.CompilerParams(
            collective_id=0, has_side_effects=True, vmem_limit_bytes=56 * 1024 * 1024
        ),
        cost_estimate=pl.CostEstimate(
            flops=3_000_000_000, bytes_accessed=8_000_000, transcendentals=1_400_000
        ),
    )(
        queries, response_key_value, prompt_kv, prompt_group, response_order, live_blocks,
        out_weight, grad_out,
    )
    outs = [pltpu.with_memory_space_constraint(out, pltpu.VMEM) for out in outs]
    return pl.pallas_call(
        hand_on,
        out_shape=kinds,
        in_specs=[vmem, vmem, vmem],
        out_specs=(hbm, hbm, hbm),
        scratch_shapes=[pltpu.SemaphoreType.DMA((3,))],
        compiler_params=pltpu.CompilerParams(vmem_limit_bytes=1024 * 1024),
    )(*outs)


def solution(mesh):
    return jax.shard_map(
        body,
        mesh=mesh,
        in_specs=(
            P("dp", "tensor"),
            P("dp", "tensor"),
            P("dp", None, None, "tensor"),
            P("dp", None),
            P(),
            P("dp"),
            P("tensor", None),
            P("dp", "tensor"),
        ),
        out_specs=(P("dp", "tensor"), P("dp", "tensor"), P("dp", None, None, "tensor")),
        check_vma=False,
    )
```

```python
import math

import jax
import jax.numpy as jnp
from jax import lax
from jax.experimental import pallas as pl
from jax.experimental.pallas import tpu as pltpu
from jax.sharding import PartitionSpec as P

HEAD = 128
HEADS = 5
WIDTH = HEAD * HEADS
TOKENS = 128
BLOCK = 64
GROUPS = 8
NY, NZ, NX = 4, 8, 4
PROMPT = NZ * NY * BLOCK
SLOT = NY * BLOCK
SCALE = 1.0 / math.sqrt(HEAD)
EXP2_SCALE = SCALE * math.log2(math.e)
N_COPIES = 150
MESH = pl.DeviceIdType.MESH
BF16, F32 = jnp.bfloat16, jnp.float32

def mm(a, b):
    return jnp.dot(a, b, preferred_element_type=F32)


def mm_t(a, b):
    return lax.dot_general(a, b, (((1,), (1,)), ((), ())), preferred_element_type=F32)


def fold(x, op):
    return op(x.reshape(x.shape[0] // 8, 8, x.shape[1]), axis=0)


def each(count, step):
    def run(index, carry):
        step(index)
        return carry

    lax.fori_loop(0, count, run, 0)


def each_pair(count, step):
    def both(index):
        step(2 * index)
        step(2 * index + 1)

    each(count // 2, both)


LEVELS = [(0,), (1, 2), (3, 4), (5, 6, 7)]
LAST = 8


def kernel(
    q_ref, rkv_ref, pkv_ref, pg_ref, ro_ref, lb_ref, w_ref, go_ref,
    oq_ref, or_ref, op_ref,
    q_v, pkv_v,
    w_v, gathered, qs, gs,
    own, r1, picked, picked_own, kv,
    e_buf, p_buf, dp_buf, ds_buf,
    tops, sums, dots, coef, row_delta,
    terms, relayed, direct, summed, back_in, local,
    marks, in_sem, w_sem, send_sem, recv_sem,
):
    dp = lax.axis_index("dp")
    tensor = lax.axis_index("tensor")
    y, z = lax.div(dp, NZ), lax.rem(dp, NZ)
    x, core = lax.div(tensor, 2), lax.rem(tensor, 2)

    ys = [lax.rem(y + dy, NY) for dy in range(NY)]
    zs = {dz: lax.rem(z + dz + NZ, NZ) for dz in range(-3, 4)}
    places = {(dy, dz): ys[dy] * NZ + zs[dz] for dy in range(NY) for dz in zs}
    along_x = {step: lax.rem(x + step + NX, NX) * 2 + core for step in (-1, 1)}

    def at(dy, dz):
        return (places[dy, dz], tensor)

    def at_x(step):
        return (dp, along_x[step])

    sibling = (dp, x * 2 + 1 - core)

    numbers = {}
    started = []

    def remote(name, src, dst, device):
        n = numbers.setdefault(name, len(numbers))
        return pltpu.make_async_remote_copy(
            src_ref=src, dst_ref=dst, send_sem=send_sem.at[n], recv_sem=recv_sem.at[n],
            device_id=device, device_id_type=MESH,
        )

    def go(copy):
        copy.start()
        started.append(copy)

    in_copies = [
        pltpu.make_async_copy(src, dst, in_sem.at[n])
        for n, (src, dst) in enumerate(
            [
                (pkv_ref, pkv_v), (go_ref, gathered.at[0, :, pl.ds(0, WIDTH)]), (q_ref, q_v),
                (rkv_ref.at[:, pl.ds(0, HEAD)], kv.at[0, pl.ds(PROMPT, TOKENS)]),
                (rkv_ref.at[:, pl.ds(HEAD, HEAD)], kv.at[1, pl.ds(PROMPT, TOKENS)]),
            ]
        )
    ]
    in_copies[0].start()
    barrier = pltpu.get_barrier_semaphore()
    partners = [at(dy, dz) for dz in range(-3, 4) for dy in range(NY) if (dy, dz) != (0, 0)]
    partners += [at_x(1), at_x(-1), sibling]
    for partner in partners:
        pl.semaphore_signal(barrier, inc=1, device_id=partner, device_id_type=MESH)
    for copy in in_copies[1:]:
        copy.start()

    slot_of = []
    for g in range(GROUPS):
        slot = jnp.int32(0)
        for c in range(GROUPS):
            slot = jnp.where(pg_ref[0, c] == g, c, slot)
        slot_of.append(slot)
    in_copies[0].wait()
    for g in range(GROUPS):
        own[0, g] = pkv_v[0, slot_of[g], :, :HEAD]
    for copy in in_copies[1:]:
        copy.wait()
    pl.semaphore_wait(barrier, len(partners))

    def first_hop(c, d):
        return remote(("first", c, d), own.at[c], r1[c][d], at(0, 1 if d == 0 else -1))

    def place(slot, dy):
        return pl.ds(slot * SLOT + (dy % NY) * BLOCK, BLOCK)

    def own_copy(dy):
        return remote(
            ("own", dy), picked_own.at[:, dy], kv.at[:, place(0, -dy)], at(dy, 0)
        )

    def forward(c, d, m, dy):
        slot = 7 if m == 3 else 1 + d + 2 * m
        return remote(
            ("forward", c, d, m, dy), picked.at[c, d, m, dy], kv.at[c, place(slot, -dy)],
            at(dy, m if d == 0 else -m),
        )

    def sent(d, m):
        if m == 3:
            return (2 * d, 2 * d + 1)
        return (1, 2, 3) if m == 0 else (0, 1, 2, 3)

    def relay(c):
        for d in range(2):
            sign = 1 if d == 0 else -1
            first_hop(c, d).wait_recv()
            for m in (3, 2, 1, 0):
                for dy in sent(d, m):
                    picked[c, d, m, dy] = r1[c][d][groups[sign * m][dy]]
                    go(forward(c, d, m, dy))
            kv[c, (1 + d) * SLOT : (1 + d) * SLOT + BLOCK, :] = r1[c][d][groups[0][0]]

    def arrived(c, level):
        if level == 0:
            for dy in range(1, NY):
                own_copy(dy).wait_recv()
        else:
            for m in (3, 2) if level == 3 else (level - 1,):
                for d in range(2):
                    for dy in sent(d, m):
                        forward(c, d, m, dy).wait_recv()

    half = TOKENS // 2

    def slice_of(r, other, rows=pl.ds(0, TOKENS)):
        return gathered.at[r, rows, pl.ds(other * WIDTH, WIDTH)]

    def x_copy(way, part):
        rows = pl.ds(part * half, half)
        return remote(
            ("x", way, part), slice_of(0, 0, rows), slice_of(1 if way == 0 else 3, 0, rows),
            at_x(-1 if way == 0 else 1),
        )

    def x_pass(way):
        rows = pl.ds(way * half, half)
        return remote(
            ("x", way, 2), slice_of(1 if way == 0 else 3, 0, rows), slice_of(2, 0, rows),
            at_x(-1 if way == 0 else 1),
        )

    def share(r):
        return remote(("share", r), slice_of(r, 0), slice_of(r, 1), sibling)

    for d in range(2):
        go(first_hop(0, d))
    for part in range(2):
        for way in range(2):
            go(x_copy(way, way if part == 0 else 1 - way))
    go(share(0))

    w_copies = {}
    for r in (0, 1, 3, 2):
        for other in range(2):
            piece = lax.rem(x + r, NX) * 2 + (core if other == 0 else 1 - core)
            copy = pltpu.make_async_copy(
                w_ref.at[:, pl.ds(pl.multiple_of(piece * WIDTH, WIDTH), WIDTH)],
                w_v.at[r, :, pl.ds(other * WIDTH, WIDTH)], w_sem.at[r, other],
            )
            copy.start()
            w_copies[r, other] = copy
    for g in range(GROUPS):
        own[1, g] = pkv_v[0, slot_of[g], :, HEAD:]
    for d in range(2):
        go(first_hop(1, d))

    groups = {
        dz: [lax.div(ro_ref[places[dy, dz]], 4) for dy in range(NY)] for dz in range(-3, 4)
    }
    for dy in range(NY):
        for c in range(2):
            if dy == 0:
                kv[c, 0:BLOCK, :] = own[c, groups[0][0]]
            else:
                picked_own[c, dy] = own[c, groups[0][dy]]
        if dy > 0:
            go(own_copy(dy))

    def rows_of(chunk):
        if isinstance(chunk, int) and chunk == LAST:
            return pl.ds(PROMPT, TOKENS)
        return pl.ds(pl.multiple_of(chunk * SLOT, SLOT), SLOT)

    def scores(chunk):
        rows = rows_of(chunk)
        s = mm_t(kv[0, rows, :], qs[...])
        if isinstance(chunk, int) and chunk == LAST:
            key_pos = lax.broadcasted_iota(jnp.int32, s.shape, 0)
            query_pos = lax.broadcasted_iota(jnp.int32, s.shape, 1) % TOKENS
            s = jnp.where(key_pos <= query_pos, s, -jnp.inf)
        top = jnp.max(fold(s, jnp.max), axis=0, keepdims=True)
        e = jnp.exp2((s - top) * EXP2_SCALE)
        e_buf[rows, :] = e.astype(BF16)
        tops[chunk] = top
        sums[chunk] = jnp.sum(fold(e, jnp.sum), axis=0, keepdims=True)

    def slopes(chunk):
        rows = rows_of(chunk)
        values = mm_t(kv[1, rows, :], gs[...])
        dp_buf[rows, :] = values
        products = values * e_buf[rows, :].astype(F32)
        dots[chunk] = jnp.sum(fold(products, jnp.sum), axis=0, keepdims=True)

    def level_of(number, step):
        slots = LEVELS[number]
        each(len(slots), lambda i: step(slots[0] + i))

    def project(r):
        for other in range(2):
            w_copies[r, other].wait()
        return mm_t(w_v[r], gathered[r])

    for h in range(HEADS):
        qs[h * HEAD : (h + 1) * HEAD, :] = q_v[:, h * HEAD : (h + 1) * HEAD]
    scores(LAST)
    share(0).wait_recv()
    grad = project(0)
    for way in range(2):
        x_copy(way, way).wait_recv()
        go(x_pass(way))
    relay(0)
    for way in range(2):
        x_copy(way, 1 - way).wait_recv()
        go(share(1 if way == 0 else 3))
    arrived(0, 0)
    level_of(0, scores)
    for way in range(2):
        x_pass(way).wait_recv()
    go(share(2))
    share(1).wait_recv()
    grad = grad + project(1)
    relay(1)
    share(3).wait_recv()
    grad = grad + project(3)
    share(2).wait_recv()
    grad = grad + project(2)
    column = lax.broadcasted_iota(jnp.int32, grad.shape, 1)
    grad = jnp.where(column < lb_ref[0] * TOKENS, grad, 0.0).astype(BF16)
    for h in range(HEADS):
        rows = slice(h * HEAD, (h + 1) * HEAD)
        gs[rows, :] = grad[rows, :].T

    slopes(LAST)
    level_of(0, slopes)
    arrived(0, 1)
    level_of(1, scores)
    arrived(0, 2)
    level_of(2, scores)
    arrived(0, 3)
    level_of(3, scores)

    highest = tops[0]
    for chunk in range(1, LAST + 1):
        highest = jnp.maximum(highest, tops[chunk])
    factors = [jnp.exp2((tops[chunk] - highest) * EXP2_SCALE) for chunk in range(LAST + 1)]
    total = sums[0] * factors[0]
    for chunk in range(1, LAST + 1):
        total = total + sums[chunk] * factors[chunk]
    for chunk in range(LAST + 1):
        coef[chunk] = factors[chunk] / total

    def back(c, slot, dy):
        both = slot < 3
        rows = place(slot, dy)
        src = terms.at[:, rows] if both else terms.at[c, rows]
        if slot == 0:
            dst, device = direct.at[:, -dy % NY], at(dy, 0)
        else:
            m, d = (3, dy // 2) if slot == 7 else divmod(slot - 1, 2)
            index = 12 + dy % 2 if slot == 7 else m * NY + -dy % NY
            dst = relayed.at[:, d, index] if both else relayed.at[c, d, index]
            device = at(dy, -m if d == 0 else m)
        return remote(("back", 0 if both else c, slot, dy), src, dst, device)

    def summed_copy(c, d):
        return remote(
            ("summed", c, d), summed.at[c, d], back_in[c][d], at(0, -1 if d == 0 else 1)
        )

    def returned(slot):
        return (1, 2, 3) if slot < 3 else (0, 1, 2, 3)

    def fill(c, chunk):
        rows = rows_of(chunk)
        if c == 1:
            p = e_buf[rows, :].astype(F32) * coef[chunk]
            p_buf[rows, :] = p.astype(BF16)
            return mm(p_buf[rows, :], gs[...])
        ds = p_buf[rows, :].astype(F32) * (dp_buf[rows, :] - row_delta[...])
        ds_buf[rows, :] = ds.astype(BF16)
        return mm(ds_buf[rows, :], qs[...]) * SCALE

    def send_back(c, slots):
        for slot in slots:
            terms[c, slot * SLOT : (slot + 1) * SLOT, :] = fill(c, slot).astype(BF16)
            if slot > 2 or c == 0:
                for dy in returned(slot):
                    go(back(c, slot, dy))

    def mark(d, i, g):
        return marks[(d * 14 + i) * GROUPS + g]

    def mine(c, slot):
        return terms[c, slot * SLOT : slot * SLOT + BLOCK, :].astype(F32)

    def add_up(c):
        for d in range(2):
            for slot in (7, 5 + d, 3 + d):
                for dy in (2 * d, 2 * d + 1) if slot == 7 else returned(slot):
                    back(c, slot, dy).wait_recv()

            def one(g):
                result = mine(c, 1 + d) * mark(d, 0, g)
                for i in range(1, 14):
                    result = result + relayed[c, d, i].astype(F32) * mark(d, i, g)
                summed[c, d, g] = result.astype(BF16)

            each_pair(GROUPS, one)
            go(summed_copy(c, d))

    def add_up_own(c):
        def one(g):
            result = mine(c, 0) * mark(0, 0, g)
            for dy in range(1, NY):
                result = result + direct[c, dy].astype(F32) * mark(0, dy, g)
            local[c, g] = result

        each_pair(GROUPS, one)

    def finish(c):
        for d in range(2):
            summed_copy(c, d).wait_recv()
        for slot in range(GROUPS):
            g = pg_ref[0, slot]
            result = back_in[c][0][g].astype(F32) + back_in[c][1][g].astype(F32)
            op_ref[0, slot, :, c * HEAD : (c + 1) * HEAD] = (result + local[c, g]).astype(BF16)

    sent_first = list(started)
    started.clear()
    send_back(1, (7, 5, 6, 3, 4))
    arrived(1, 1)
    level_of(1, slopes)
    arrived(1, 2)
    level_of(2, slopes)
    arrived(1, 3)
    level_of(3, slopes)
    delta = dots[0] * coef[0]
    for chunk in range(1, LAST + 1):
        delta = delta + dots[chunk] * coef[chunk]
    row_delta[...] = delta
    send_back(0, (7, 5, 6, 3, 4))
    send_back(1, (1, 2, 0))
    send_back(0, (1, 2, 0))
    listed = []
    for d, sign in ((0, 1), (1, -1)):
        for m in range(3):
            listed += groups[sign * m]
        listed += [groups[sign * 3][-dy % NY] for dy in (2 * d, 2 * d + 1)]
    for n, group in enumerate(listed):
        for g in range(GROUPS):
            marks[n * GROUPS + g] = jnp.where(group == g, 1.0, 0.0).astype(F32)
    for slot in (1, 2, 0):
        for dy in returned(slot):
            back(0, slot, dy).wait_recv()
    add_up(1)
    for copy in sent_first:
        copy.wait_send()
    or_ref[:, HEAD:] = fill(1, LAST).astype(BF16)
    or_ref[:, :HEAD] = fill(0, LAST).astype(BF16)
    dq = mm(kv[0].T, ds_buf[...]) * SCALE
    for h in range(HEADS):
        oq_ref[:, h * HEAD : (h + 1) * HEAD] = dq[:, h * HEAD : (h + 1) * HEAD].T.astype(BF16)
    add_up_own(1)
    add_up_own(0)
    add_up(0)
    finish(1)
    for copy in started:
        copy.wait_send()
    finish(0)


def hand_on(*refs):
    sem = refs[6]
    copies = [pltpu.make_async_copy(refs[n], refs[3 + n], sem.at[n]) for n in range(3)]
    for copy in copies:
        copy.start()
    for copy in copies:
        copy.wait()


def body(
    queries, response_key_value, prompt_kv, prompt_group, response_order, live_blocks,
    out_weight, grad_out,
):
    hbm = pl.BlockSpec(memory_space=pl.ANY)
    vmem = pl.BlockSpec(memory_space=pltpu.VMEM)
    smem = pl.BlockSpec(memory_space=pltpu.SMEM)
    block = (BLOCK, HEAD)

    def space(*shape, kind=BF16):
        return pltpu.VMEM(shape, kind)

    def streams():
        return [[space(GROUPS, *block) for _ in range(2)] for _ in range(2)]

    scratch = [
        space(*queries.shape),
        space(*prompt_kv.shape),
        space(NX, WIDTH, 2 * WIDTH),
        space(NX, TOKENS, 2 * WIDTH),
        space(WIDTH, HEAD),
        space(WIDTH, HEAD),
        space(2, GROUPS, *block),
        streams(),
        space(2, 2, 4, NY, *block),
        space(2, NY, *block),
        space(2, PROMPT + TOKENS, HEAD),
        space(PROMPT + TOKENS, WIDTH),
        space(PROMPT + TOKENS, WIDTH),
        space(PROMPT + TOKENS, WIDTH, kind=F32),
        space(PROMPT + TOKENS, WIDTH),
        space(LAST + 1, 1, WIDTH, kind=F32),
        space(LAST + 1, 1, WIDTH, kind=F32),
        space(LAST + 1, 1, WIDTH, kind=F32),
        space(LAST + 1, 1, WIDTH, kind=F32),
        space(1, WIDTH, kind=F32),
        space(2, PROMPT, HEAD),
        space(2, 2, 14, *block),
        space(2, NY, *block),
        space(2, 2, GROUPS, *block),
        streams(),
        space(2, GROUPS, *block, kind=F32),
        pltpu.SMEM((28 * GROUPS,), F32),
        pltpu.SemaphoreType.DMA((5,)),
        pltpu.SemaphoreType.DMA((NX, 2)),
        pltpu.SemaphoreType.DMA((N_COPIES,)),
        pltpu.SemaphoreType.DMA((N_COPIES,)),
    ]
    kinds = tuple(
        jax.ShapeDtypeStruct(a.shape, BF16) for a in (queries, response_key_value, prompt_kv)
    )
    outs = pl.pallas_call(
        kernel,
        out_shape=tuple(pltpu.VMEM(a.shape, BF16) for a in kinds),
        in_specs=[hbm, hbm, hbm, smem, smem, smem, hbm, hbm],
        out_specs=(vmem, vmem, vmem),
        scratch_shapes=scratch,
        compiler_params=pltpu.CompilerParams(
            collective_id=0, has_side_effects=True, vmem_limit_bytes=56 * 1024 * 1024
        ),
        cost_estimate=pl.CostEstimate(
            flops=3_000_000_000, bytes_accessed=8_000_000, transcendentals=1_400_000
        ),
    )(
        queries, response_key_value, prompt_kv, prompt_group, response_order, live_blocks,
        out_weight, grad_out,
    )
    outs = [pltpu.with_memory_space_constraint(out, pltpu.VMEM) for out in outs]
    return pl.pallas_call(
        hand_on,
        out_shape=kinds,
        in_specs=[vmem, vmem, vmem],
        out_specs=(hbm, hbm, hbm),
        scratch_shapes=[pltpu.SemaphoreType.DMA((3,))],
        compiler_params=pltpu.CompilerParams(vmem_limit_bytes=1024 * 1024),
    )(*outs)


def solution(mesh):
    return jax.shard_map(
        body,
        mesh=mesh,
        in_specs=(
            P("dp", "tensor"),
            P("dp", "tensor"),
            P("dp", None, None, "tensor"),
            P("dp", None),
            P(),
            P("dp"),
            P("tensor", None),
            P("dp", "tensor"),
        ),
        out_specs=(P("dp", "tensor"), P("dp", "tensor"), P("dp", None, None, "tensor")),
        check_vma=False,
    )
```

```python
import math

import jax
import jax.numpy as jnp
from jax import lax
from jax.experimental import pallas as pl
from jax.experimental.pallas import tpu as pltpu
from jax.sharding import PartitionSpec as P

HEAD = 128
HEADS = 5
WIDTH = HEAD * HEADS
TOKENS = 128
BLOCK = 64
GROUPS = 8
NY, NZ, NX = 4, 8, 4
PROMPT = NZ * NY * BLOCK
SLOT = NY * BLOCK
SCALE = 1.0 / math.sqrt(HEAD)
EXP2_SCALE = SCALE * math.log2(math.e)
N_COPIES = 150
MESH = pl.DeviceIdType.MESH
BF16, F32 = jnp.bfloat16, jnp.float32

def mm(a, b):
    return jnp.dot(a, b, preferred_element_type=F32)


def mm_t(a, b):
    return lax.dot_general(a, b, (((1,), (1,)), ((), ())), preferred_element_type=F32)


def fold(x, op):
    return op(x.reshape(x.shape[0] // 8, 8, x.shape[1]), axis=0)


def each(count, step):
    def run(index, carry):
        step(index)
        return carry

    lax.fori_loop(0, count, run, 0)


def each_pair(count, step):
    def both(index):
        step(2 * index)
        step(2 * index + 1)

    each(count // 2, both)


LEVELS = [(0,), (1, 2), (3, 4), (5, 6, 7)]
LAST = 8


def kernel(
    q_ref, rkv_ref, pkv_ref, pg_ref, ro_ref, lb_ref, w_ref, go_ref,
    oq_ref, or_ref, op_ref,
    q_v, pkv_v,
    w_v, gathered, qs, gs,
    own, r1, picked, picked_own, kv,
    e_buf, p_buf, dp_buf, ds_buf,
    tops, sums, dots, coef, row_delta,
    terms, relayed, direct, summed, back_in, local,
    marks, in_sem, w_sem, send_sem, recv_sem,
):
    dp = lax.axis_index("dp")
    tensor = lax.axis_index("tensor")
    y, z = lax.div(dp, NZ), lax.rem(dp, NZ)
    x, core = lax.div(tensor, 2), lax.rem(tensor, 2)

    ys = [lax.rem(y + dy, NY) for dy in range(NY)]
    zs = {dz: lax.rem(z + dz + NZ, NZ) for dz in range(-3, 4)}
    places = {(dy, dz): ys[dy] * NZ + zs[dz] for dy in range(NY) for dz in zs}
    along_x = {step: lax.rem(x + step + NX, NX) * 2 + core for step in (-1, 1)}

    def at(dy, dz):
        return (places[dy, dz], tensor)

    def at_x(step):
        return (dp, along_x[step])

    sibling = (dp, x * 2 + 1 - core)

    numbers = {}
    started = []

    def remote(name, src, dst, device):
        n = numbers.setdefault(name, len(numbers))
        return pltpu.make_async_remote_copy(
            src_ref=src, dst_ref=dst, send_sem=send_sem.at[n], recv_sem=recv_sem.at[n],
            device_id=device, device_id_type=MESH,
        )

    def go(copy):
        copy.start()
        started.append(copy)

    in_copies = [
        pltpu.make_async_copy(src, dst, in_sem.at[n])
        for n, (src, dst) in enumerate(
            [
                (pkv_ref, pkv_v), (go_ref, gathered.at[0, :, pl.ds(0, WIDTH)]), (q_ref, q_v),
                (rkv_ref.at[:, pl.ds(0, HEAD)], kv.at[0, pl.ds(PROMPT, TOKENS)]),
                (rkv_ref.at[:, pl.ds(HEAD, HEAD)], kv.at[1, pl.ds(PROMPT, TOKENS)]),
            ]
        )
    ]
    in_copies[0].start()
    barrier = pltpu.get_barrier_semaphore()
    partners = [at(dy, dz) for dz in range(-3, 4) for dy in range(NY) if (dy, dz) != (0, 0)]
    partners += [at_x(1), at_x(-1), sibling]
    for partner in partners:
        pl.semaphore_signal(barrier, inc=1, device_id=partner, device_id_type=MESH)
    for copy in in_copies[1:]:
        copy.start()

    w_copies = {}
    for r in (0, 1, 3, 2):
        for other in range(2):
            piece = lax.rem(x + r, NX) * 2 + (core if other == 0 else 1 - core)
            copy = pltpu.make_async_copy(
                w_ref.at[:, pl.ds(pl.multiple_of(piece * WIDTH, WIDTH), WIDTH)],
                w_v.at[r, :, pl.ds(other * WIDTH, WIDTH)], w_sem.at[r, other],
            )
            copy.start()
            w_copies[r, other] = copy

    slot_of = []
    for g in range(GROUPS):
        slot = jnp.int32(0)
        for c in range(GROUPS):
            slot = jnp.where(pg_ref[0, c] == g, c, slot)
        slot_of.append(slot)
    in_copies[0].wait()
    for g in range(GROUPS):
        own[0, g] = pkv_v[0, slot_of[g], :, :HEAD]
    for copy in in_copies[1:]:
        copy.wait()
    pl.semaphore_wait(barrier, len(partners))

    def first_hop(c, d):
        return remote(("first", c, d), own.at[c], r1[c][d], at(0, 1 if d == 0 else -1))

    def place(slot, dy):
        return pl.ds(slot * SLOT + (dy % NY) * BLOCK, BLOCK)

    def own_copy(dy):
        return remote(
            ("own", dy), picked_own.at[:, dy], kv.at[:, place(0, -dy)], at(dy, 0)
        )

    def forward(c, d, m, dy):
        slot = 7 if m == 3 else 1 + d + 2 * m
        return remote(
            ("forward", c, d, m, dy), picked.at[c, d, m, dy], kv.at[c, place(slot, -dy)],
            at(dy, m if d == 0 else -m),
        )

    def sent(d, m):
        if m == 3:
            return (2 * d, 2 * d + 1)
        return (1, 2, 3) if m == 0 else (0, 1, 2, 3)

    def relay(c):
        for d in range(2):
            sign = 1 if d == 0 else -1
            first_hop(c, d).wait_recv()
            for m in (3, 2, 1, 0):
                for dy in sent(d, m):
                    picked[c, d, m, dy] = r1[c][d][groups[sign * m][dy]]
                    go(forward(c, d, m, dy))
            kv[c, (1 + d) * SLOT : (1 + d) * SLOT + BLOCK, :] = r1[c][d][groups[0][0]]

    def arrived(c, level):
        if level == 0:
            for dy in range(1, NY):
                own_copy(dy).wait_recv()
        else:
            for m in (3, 2) if level == 3 else (level - 1,):
                for d in range(2):
                    for dy in sent(d, m):
                        forward(c, d, m, dy).wait_recv()

    half = TOKENS // 2

    def slice_of(r, other, rows=pl.ds(0, TOKENS)):
        return gathered.at[r, rows, pl.ds(other * WIDTH, WIDTH)]

    def x_copy(way, part):
        rows = pl.ds(part * half, half)
        return remote(
            ("x", way, part), slice_of(0, 0, rows), slice_of(1 if way == 0 else 3, 0, rows),
            at_x(-1 if way == 0 else 1),
        )

    def x_pass(way):
        rows = pl.ds(way * half, half)
        return remote(
            ("x", way, 2), slice_of(1 if way == 0 else 3, 0, rows), slice_of(2, 0, rows),
            at_x(-1 if way == 0 else 1),
        )

    def share(r):
        return remote(("share", r), slice_of(r, 0), slice_of(r, 1), sibling)

    for d in range(2):
        go(first_hop(0, d))
    for part in range(2):
        for way in range(2):
            go(x_copy(way, way if part == 0 else 1 - way))
    go(share(0))

    for g in range(GROUPS):
        own[1, g] = pkv_v[0, slot_of[g], :, HEAD:]

    groups = {
        dz: [lax.div(ro_ref[places[dy, dz]], 4) for dy in range(NY)] for dz in range(-3, 4)
    }
    for dy in range(NY):
        for c in range(2):
            if dy == 0:
                kv[c, 0:BLOCK, :] = own[c, groups[0][0]]
            else:
                picked_own[c, dy] = own[c, groups[0][dy]]
        if dy > 0:
            go(own_copy(dy))

    def rows_of(chunk):
        if isinstance(chunk, int) and chunk == LAST:
            return pl.ds(PROMPT, TOKENS)
        return pl.ds(pl.multiple_of(chunk * SLOT, SLOT), SLOT)

    def scores(chunk):
        rows = rows_of(chunk)
        s = mm_t(kv[0, rows, :], qs[...])
        if isinstance(chunk, int) and chunk == LAST:
            key_pos = lax.broadcasted_iota(jnp.int32, s.shape, 0)
            query_pos = lax.broadcasted_iota(jnp.int32, s.shape, 1) % TOKENS
            s = jnp.where(key_pos <= query_pos, s, -jnp.inf)
        top = jnp.max(fold(s, jnp.max), axis=0, keepdims=True)
        e = jnp.exp2((s - top) * EXP2_SCALE)
        e_buf[rows, :] = e.astype(BF16)
        tops[chunk] = top
        sums[chunk] = jnp.sum(fold(e, jnp.sum), axis=0, keepdims=True)

    def slopes(chunk):
        rows = rows_of(chunk)
        values = mm_t(kv[1, rows, :], gs[...])
        dp_buf[rows, :] = values
        products = values * e_buf[rows, :].astype(F32)
        dots[chunk] = jnp.sum(fold(products, jnp.sum), axis=0, keepdims=True)

    def level_of(number, step):
        slots = LEVELS[number]
        each(len(slots), lambda i: step(slots[0] + i))

    def project(r):
        for other in range(2):
            w_copies[r, other].wait()
        return mm_t(w_v[r], gathered[r])

    for h in range(HEADS):
        qs[h * HEAD : (h + 1) * HEAD, :] = q_v[:, h * HEAD : (h + 1) * HEAD]
    scores(LAST)
    share(0).wait_recv()
    for d in range(2):
        go(first_hop(1, d))
    grad = project(0)
    for way in range(2):
        x_copy(way, way).wait_recv()
        go(x_pass(way))
    relay(0)
    for way in range(2):
        x_copy(way, 1 - way).wait_recv()
        go(share(1 if way == 0 else 3))
    arrived(0, 0)
    level_of(0, scores)
    share(1).wait_recv()
    grad = grad + project(1)
    for way in range(2):
        x_pass(way).wait_recv()
    go(share(2))
    relay(1)
    share(3).wait_recv()
    grad = grad + project(3)
    arrived(0, 1)
    level_of(1, scores)
    share(2).wait_recv()
    grad = grad + project(2)
    column = lax.broadcasted_iota(jnp.int32, grad.shape, 1)
    grad = jnp.where(column < lb_ref[0] * TOKENS, grad, 0.0).astype(BF16)
    for h in range(HEADS):
        rows = slice(h * HEAD, (h + 1) * HEAD)
        gs[rows, :] = grad[rows, :].T

    slopes(LAST)
    level_of(0, slopes)
    arrived(0, 2)
    level_of(2, scores)
    arrived(0, 3)
    level_of(3, scores)

    highest = tops[0]
    for chunk in range(1, LAST + 1):
        highest = jnp.maximum(highest, tops[chunk])
    factors = [jnp.exp2((tops[chunk] - highest) * EXP2_SCALE) for chunk in range(LAST + 1)]
    total = sums[0] * factors[0]
    for chunk in range(1, LAST + 1):
        total = total + sums[chunk] * factors[chunk]
    for chunk in range(LAST + 1):
        coef[chunk] = factors[chunk] / total

    def back(c, slot, dy):
        both = slot == 0
        rows = place(slot, dy)
        src = terms.at[:, rows] if both else terms.at[c, rows]
        if slot == 0:
            dst, device = direct.at[:, -dy % NY], at(dy, 0)
        else:
            m, d = (3, dy // 2) if slot == 7 else divmod(slot - 1, 2)
            index = 12 + dy % 2 if slot == 7 else m * NY + -dy % NY
            dst = relayed.at[:, d, index] if both else relayed.at[c, d, index]
            device = at(dy, -m if d == 0 else m)
        return remote(("back", 0 if both else c, slot, dy), src, dst, device)

    def summed_copy(c, d):
        return remote(
            ("summed", c, d), summed.at[c, d], back_in[c][d], at(0, -1 if d == 0 else 1)
        )

    def returned(slot):
        return (1, 2, 3) if slot < 3 else (0, 1, 2, 3)

    def fill(c, chunk):
        rows = rows_of(chunk)
        if c == 1:
            p = e_buf[rows, :].astype(F32) * coef[chunk]
            p_buf[rows, :] = p.astype(BF16)
            return mm(p_buf[rows, :], gs[...])
        ds = p_buf[rows, :].astype(F32) * (dp_buf[rows, :] - row_delta[...])
        ds_buf[rows, :] = ds.astype(BF16)
        return mm(ds_buf[rows, :], qs[...]) * SCALE

    def send_back(c, slots):
        for slot in slots:
            terms[c, slot * SLOT : (slot + 1) * SLOT, :] = fill(c, slot).astype(BF16)
            if slot > 0 or c == 0:
                for dy in returned(slot):
                    go(back(c, slot, dy))

    def mark(d, i, g):
        return marks[(d * 14 + i) * GROUPS + g]

    def mine(c, slot):
        return terms[c, slot * SLOT : slot * SLOT + BLOCK, :].astype(F32)

    def add_up(c):
        for d in range(2):
            for slot in (7, 5 + d, 3 + d, 1 + d):
                for dy in (2 * d, 2 * d + 1) if slot == 7 else returned(slot):
                    back(c, slot, dy).wait_recv()

            def one(g):
                result = mine(c, 1 + d) * mark(d, 0, g)
                for i in range(1, 14):
                    result = result + relayed[c, d, i].astype(F32) * mark(d, i, g)
                summed[c, d, g] = result.astype(BF16)

            each_pair(GROUPS, one)
            go(summed_copy(c, d))

    def add_up_own(c):
        def one(g):
            result = mine(c, 0) * mark(0, 0, g)
            for dy in range(1, NY):
                result = result + direct[c, dy].astype(F32) * mark(0, dy, g)
            local[c, g] = result

        each_pair(GROUPS, one)

    def finish(c):
        for d in range(2):
            summed_copy(c, d).wait_recv()
        for slot in range(GROUPS):
            g = pg_ref[0, slot]
            result = back_in[c][0][g].astype(F32) + back_in[c][1][g].astype(F32)
            op_ref[0, slot, :, c * HEAD : (c + 1) * HEAD] = (result + local[c, g]).astype(BF16)

    listed = []
    for d, sign in ((0, 1), (1, -1)):
        for m in range(3):
            listed += groups[sign * m]
        listed += [groups[sign * 3][-dy % NY] for dy in (2 * d, 2 * d + 1)]
    for n, group in enumerate(listed):
        for g in range(GROUPS):
            marks[n * GROUPS + g] = jnp.where(group == g, 1.0, 0.0).astype(F32)
    send_back(1, (7, 5, 6, 3, 4))
    arrived(1, 1)
    level_of(1, slopes)
    arrived(1, 2)
    level_of(2, slopes)
    arrived(1, 3)
    level_of(3, slopes)
    delta = dots[0] * coef[0]
    for chunk in range(1, LAST + 1):
        delta = delta + dots[chunk] * coef[chunk]
    row_delta[...] = delta
    send_back(0, (7, 5, 6, 3, 4))
    send_back(1, (1, 2))
    send_back(0, (1, 2))
    add_up(1)
    add_up(0)
    send_back(1, (0,))
    send_back(0, (0,))
    or_ref[:, HEAD:] = fill(1, LAST).astype(BF16)
    or_ref[:, :HEAD] = fill(0, LAST).astype(BF16)
    dq = mm(kv[0].T, ds_buf[...]) * SCALE
    for h in range(HEADS):
        oq_ref[:, h * HEAD : (h + 1) * HEAD] = dq[:, h * HEAD : (h + 1) * HEAD].T.astype(BF16)
    for dy in returned(0):
        back(0, 0, dy).wait_recv()
    add_up_own(1)
    add_up_own(0)
    finish(1)
    for copy in started:
        copy.wait_send()
    finish(0)


def hand_on(*refs):
    sem = refs[6]
    copies = [pltpu.make_async_copy(refs[n], refs[3 + n], sem.at[n]) for n in range(3)]
    for copy in copies:
        copy.start()
    for copy in copies:
        copy.wait()


def body(
    queries, response_key_value, prompt_kv, prompt_group, response_order, live_blocks,
    out_weight, grad_out,
):
    hbm = pl.BlockSpec(memory_space=pl.ANY)
    vmem = pl.BlockSpec(memory_space=pltpu.VMEM)
    smem = pl.BlockSpec(memory_space=pltpu.SMEM)
    block = (BLOCK, HEAD)

    def space(*shape, kind=BF16):
        return pltpu.VMEM(shape, kind)

    def streams():
        return [[space(GROUPS, *block) for _ in range(2)] for _ in range(2)]

    scratch = [
        space(*queries.shape),
        space(*prompt_kv.shape),
        space(NX, WIDTH, 2 * WIDTH),
        space(NX, TOKENS, 2 * WIDTH),
        space(WIDTH, HEAD),
        space(WIDTH, HEAD),
        space(2, GROUPS, *block),
        streams(),
        space(2, 2, 4, NY, *block),
        space(2, NY, *block),
        space(2, PROMPT + TOKENS, HEAD),
        space(PROMPT + TOKENS, WIDTH),
        space(PROMPT + TOKENS, WIDTH),
        space(PROMPT + TOKENS, WIDTH, kind=F32),
        space(PROMPT + TOKENS, WIDTH),
        space(LAST + 1, 1, WIDTH, kind=F32),
        space(LAST + 1, 1, WIDTH, kind=F32),
        space(LAST + 1, 1, WIDTH, kind=F32),
        space(LAST + 1, 1, WIDTH, kind=F32),
        space(1, WIDTH, kind=F32),
        space(2, PROMPT, HEAD),
        space(2, 2, 14, *block),
        space(2, NY, *block),
        space(2, 2, GROUPS, *block),
        streams(),
        space(2, GROUPS, *block, kind=F32),
        pltpu.SMEM((28 * GROUPS,), F32),
        pltpu.SemaphoreType.DMA((5,)),
        pltpu.SemaphoreType.DMA((NX, 2)),
        pltpu.SemaphoreType.DMA((N_COPIES,)),
        pltpu.SemaphoreType.DMA((N_COPIES,)),
    ]
    kinds = tuple(
        jax.ShapeDtypeStruct(a.shape, BF16) for a in (queries, response_key_value, prompt_kv)
    )
    outs = pl.pallas_call(
        kernel,
        out_shape=tuple(pltpu.VMEM(a.shape, BF16) for a in kinds),
        in_specs=[hbm, hbm, hbm, smem, smem, smem, hbm, hbm],
        out_specs=(vmem, vmem, vmem),
        scratch_shapes=scratch,
        compiler_params=pltpu.CompilerParams(
            collective_id=0, has_side_effects=True, vmem_limit_bytes=56 * 1024 * 1024
        ),
        cost_estimate=pl.CostEstimate(
            flops=3_000_000_000, bytes_accessed=8_000_000, transcendentals=1_400_000
        ),
    )(
        queries, response_key_value, prompt_kv, prompt_group, response_order, live_blocks,
        out_weight, grad_out,
    )
    outs = [pltpu.with_memory_space_constraint(out, pltpu.VMEM) for out in outs]
    return pl.pallas_call(
        hand_on,
        out_shape=kinds,
        in_specs=[vmem, vmem, vmem],
        out_specs=(hbm, hbm, hbm),
        scratch_shapes=[pltpu.SemaphoreType.DMA((3,))],
        compiler_params=pltpu.CompilerParams(vmem_limit_bytes=1024 * 1024),
    )(*outs)


def solution(mesh):
    return jax.shard_map(
        body,
        mesh=mesh,
        in_specs=(
            P("dp", "tensor"),
            P("dp", "tensor"),
            P("dp", None, None, "tensor"),
            P("dp", None),
            P(),
            P("dp"),
            P("tensor", None),
            P("dp", "tensor"),
        ),
        out_specs=(P("dp", "tensor"), P("dp", "tensor"), P("dp", None, None, "tensor")),
        check_vma=False,
    )
```

```python
import math

import jax
import jax.numpy as jnp
from jax import lax
from jax.experimental import pallas as pl
from jax.experimental.pallas import tpu as pltpu
from jax.sharding import PartitionSpec as P

HEAD = 128
HEADS = 5
WIDTH = HEAD * HEADS
TOKENS = 128
BLOCK = 64
GROUPS = 8
NY, NZ, NX = 4, 8, 4
PROMPT = NZ * NY * BLOCK
SLOT = NY * BLOCK
SCALE = 1.0 / math.sqrt(HEAD)
EXP2_SCALE = SCALE * math.log2(math.e)
N_COPIES = 150
MESH = pl.DeviceIdType.MESH
BF16, F32 = jnp.bfloat16, jnp.float32

def mm(a, b):
    return jnp.dot(a, b, preferred_element_type=F32)


def mm_t(a, b):
    return lax.dot_general(a, b, (((1,), (1,)), ((), ())), preferred_element_type=F32)


def fold(x, op):
    return op(x.reshape(x.shape[0] // 8, 8, x.shape[1]), axis=0)


def each(count, step):
    def run(index, carry):
        step(index)
        return carry

    lax.fori_loop(0, count, run, 0)


def each_pair(count, step):
    def both(index):
        step(2 * index)
        step(2 * index + 1)

    each(count // 2, both)


LEVELS = [(0,), (1, 2), (3, 4), (5, 6, 7)]
LAST = 8


def kernel(
    q_ref, rkv_ref, pkv_ref, pg_ref, ro_ref, lb_ref, w_ref, go_ref,
    oq_ref, or_ref, op_ref,
    q_v, pkv_v,
    w_v, gathered, qs, gs,
    own, r1, picked, picked_own, kv,
    e_buf, p_buf, dp_buf, ds_buf,
    tops, sums, dots, coef, row_delta,
    terms, relayed, direct, summed, back_in, local,
    marks, in_sem, w_sem, send_sem, recv_sem,
):
    dp = lax.axis_index("dp")
    tensor = lax.axis_index("tensor")
    y, z = lax.div(dp, NZ), lax.rem(dp, NZ)
    x, core = lax.div(tensor, 2), lax.rem(tensor, 2)

    ys = [lax.rem(y + dy, NY) for dy in range(NY)]
    zs = {dz: lax.rem(z + dz + NZ, NZ) for dz in range(-3, 4)}
    places = {(dy, dz): ys[dy] * NZ + zs[dz] for dy in range(NY) for dz in zs}
    along_x = {step: lax.rem(x + step + NX, NX) * 2 + core for step in (-1, 1)}

    def at(dy, dz):
        return (places[dy, dz], tensor)

    def at_x(step):
        return (dp, along_x[step])

    sibling = (dp, x * 2 + 1 - core)

    numbers = {}
    started = []

    def remote(name, src, dst, device):
        n = numbers.setdefault(name, len(numbers))
        return pltpu.make_async_remote_copy(
            src_ref=src, dst_ref=dst, send_sem=send_sem.at[n], recv_sem=recv_sem.at[n],
            device_id=device, device_id_type=MESH,
        )

    def go(copy):
        copy.start()
        started.append(copy)

    in_copies = [
        pltpu.make_async_copy(src, dst, in_sem.at[n])
        for n, (src, dst) in enumerate(
            [
                (pkv_ref, pkv_v), (go_ref, gathered.at[0, :, pl.ds(0, WIDTH)]), (q_ref, q_v),
                (rkv_ref.at[:, pl.ds(0, HEAD)], kv.at[0, pl.ds(PROMPT, TOKENS)]),
                (rkv_ref.at[:, pl.ds(HEAD, HEAD)], kv.at[1, pl.ds(PROMPT, TOKENS)]),
            ]
        )
    ]
    in_copies[0].start()
    barrier = pltpu.get_barrier_semaphore()
    partners = [at(dy, dz) for dz in range(-3, 4) for dy in range(NY) if (dy, dz) != (0, 0)]
    partners += [at_x(1), at_x(-1), sibling]
    for partner in partners:
        pl.semaphore_signal(barrier, inc=1, device_id=partner, device_id_type=MESH)
    for copy in in_copies[1:]:
        copy.start()

    w_copies = {}
    for r in (0, 1, 3, 2):
        for other in range(2):
            piece = lax.rem(x + r, NX) * 2 + (core if other == 0 else 1 - core)
            copy = pltpu.make_async_copy(
                w_ref.at[:, pl.ds(pl.multiple_of(piece * WIDTH, WIDTH), WIDTH)],
                w_v.at[r, :, pl.ds(other * WIDTH, WIDTH)], w_sem.at[r, other],
            )
            copy.start()
            w_copies[r, other] = copy

    slot_of = []
    for g in range(GROUPS):
        slot = jnp.int32(0)
        for c in range(GROUPS):
            slot = jnp.where(pg_ref[0, c] == g, c, slot)
        slot_of.append(slot)
    in_copies[0].wait()
    for g in range(GROUPS):
        own[0, g] = pkv_v[0, slot_of[g], :, :HEAD]
    for copy in in_copies[1:]:
        copy.wait()
    pl.semaphore_wait(barrier, len(partners))

    def first_hop(c, d):
        return remote(("first", c, d), own.at[c], r1[c][d], at(0, 1 if d == 0 else -1))

    def place(slot, dy):
        return pl.ds(slot * SLOT + (dy % NY) * BLOCK, BLOCK)

    def own_copy(dy):
        return remote(
            ("own", dy), picked_own.at[:, dy], kv.at[:, place(0, -dy)], at(dy, 0)
        )

    def forward(c, d, m, dy):
        slot = 7 if m == 3 else 1 + d + 2 * m
        return remote(
            ("forward", c, d, m, dy), picked.at[c, d, m, dy], kv.at[c, place(slot, -dy)],
            at(dy, m if d == 0 else -m),
        )

    def sent(d, m):
        if m == 3:
            return (2 * d, 2 * d + 1)
        return (1, 2, 3) if m == 0 else (0, 1, 2, 3)

    def relay(c):
        for d in range(2):
            first_hop(c, d).wait_recv()
        for m in (3, 2, 1, 0):
            for pair in zip(sent(0, m), sent(1, m)):
                for d, dy in enumerate(pair):
                    picked[c, d, m, dy] = r1[c][d][groups[m if d == 0 else -m][dy]]
                    go(forward(c, d, m, dy))
        for d in range(2):
            kv[c, (1 + d) * SLOT : (1 + d) * SLOT + BLOCK, :] = r1[c][d][groups[0][0]]

    def arrived(c, level):
        if level == 0:
            for dy in range(1, NY):
                own_copy(dy).wait_recv()
        else:
            for m in (3, 2) if level == 3 else (level - 1,):
                for d in range(2):
                    for dy in sent(d, m):
                        forward(c, d, m, dy).wait_recv()

    half = TOKENS // 2

    def slice_of(r, other, rows=pl.ds(0, TOKENS)):
        return gathered.at[r, rows, pl.ds(other * WIDTH, WIDTH)]

    def x_copy(way, part):
        rows = pl.ds(part * half, half)
        return remote(
            ("x", way, part), slice_of(0, 0, rows), slice_of(1 if way == 0 else 3, 0, rows),
            at_x(-1 if way == 0 else 1),
        )

    def x_pass(way):
        rows = pl.ds(way * half, half)
        return remote(
            ("x", way, 2), slice_of(1 if way == 0 else 3, 0, rows), slice_of(2, 0, rows),
            at_x(-1 if way == 0 else 1),
        )

    def share(r):
        return remote(("share", r), slice_of(r, 0), slice_of(r, 1), sibling)

    for d in range(2):
        go(first_hop(0, d))
    for part in range(2):
        for way in range(2):
            go(x_copy(way, way if part == 0 else 1 - way))
    go(share(0))

    for g in range(GROUPS):
        own[1, g] = pkv_v[0, slot_of[g], :, HEAD:]

    groups = {
        dz: [lax.div(ro_ref[places[dy, dz]], 4) for dy in range(NY)] for dz in range(-3, 4)
    }
    for dy in range(NY):
        for c in range(2):
            if dy == 0:
                kv[c, 0:BLOCK, :] = own[c, groups[0][0]]
            else:
                picked_own[c, dy] = own[c, groups[0][dy]]
        if dy > 0:
            go(own_copy(dy))

    def rows_of(chunk):
        if isinstance(chunk, int) and chunk == LAST:
            return pl.ds(PROMPT, TOKENS)
        return pl.ds(pl.multiple_of(chunk * SLOT, SLOT), SLOT)

    def scores(chunk):
        rows = rows_of(chunk)
        s = mm_t(kv[0, rows, :], qs[...])
        if isinstance(chunk, int) and chunk == LAST:
            key_pos = lax.broadcasted_iota(jnp.int32, s.shape, 0)
            query_pos = lax.broadcasted_iota(jnp.int32, s.shape, 1) % TOKENS
            s = jnp.where(key_pos <= query_pos, s, -jnp.inf)
        top = jnp.max(fold(s, jnp.max), axis=0, keepdims=True)
        e = jnp.exp2((s - top) * EXP2_SCALE)
        e_buf[rows, :] = e.astype(BF16)
        tops[chunk] = top
        sums[chunk] = jnp.sum(fold(e, jnp.sum), axis=0, keepdims=True)

    def slopes(chunk):
        rows = rows_of(chunk)
        values = mm_t(kv[1, rows, :], gs[...])
        dp_buf[rows, :] = values
        products = values * e_buf[rows, :].astype(F32)
        dots[chunk] = jnp.sum(fold(products, jnp.sum), axis=0, keepdims=True)

    def level_of(number, step):
        slots = LEVELS[number]
        each(len(slots), lambda i: step(slots[0] + i))

    def project(r):
        for other in range(2):
            w_copies[r, other].wait()
        return mm_t(w_v[r], gathered[r])

    for h in range(HEADS):
        qs[h * HEAD : (h + 1) * HEAD, :] = q_v[:, h * HEAD : (h + 1) * HEAD]
    scores(LAST)
    share(0).wait_recv()
    for d in range(2):
        go(first_hop(1, d))
    grad = project(0)
    for way in range(2):
        x_copy(way, way).wait_recv()
        go(x_pass(way))
    relay(0)
    for way in range(2):
        x_copy(way, 1 - way).wait_recv()
        go(share(1 if way == 0 else 3))
    arrived(0, 0)
    level_of(0, scores)
    share(1).wait_recv()
    grad = grad + project(1)
    for way in range(2):
        x_pass(way).wait_recv()
    go(share(2))
    relay(1)
    share(3).wait_recv()
    grad = grad + project(3)
    arrived(0, 1)
    level_of(1, scores)
    share(2).wait_recv()
    grad = grad + project(2)
    column = lax.broadcasted_iota(jnp.int32, grad.shape, 1)
    grad = jnp.where(column < lb_ref[0] * TOKENS, grad, 0.0).astype(BF16)
    for h in range(HEADS):
        rows = slice(h * HEAD, (h + 1) * HEAD)
        gs[rows, :] = grad[rows, :].T

    slopes(LAST)
    level_of(0, slopes)
    arrived(0, 2)
    level_of(2, scores)
    arrived(0, 3)
    level_of(3, scores)

    highest = tops[0]
    for chunk in range(1, LAST + 1):
        highest = jnp.maximum(highest, tops[chunk])
    factors = [jnp.exp2((tops[chunk] - highest) * EXP2_SCALE) for chunk in range(LAST + 1)]
    total = sums[0] * factors[0]
    for chunk in range(1, LAST + 1):
        total = total + sums[chunk] * factors[chunk]
    for chunk in range(LAST + 1):
        coef[chunk] = factors[chunk] / total

    def back(c, slot, dy):
        both = slot == 0
        rows = place(slot, dy)
        src = terms.at[:, rows] if both else terms.at[c, rows]
        if slot == 0:
            dst, device = direct.at[:, -dy % NY], at(dy, 0)
        else:
            m, d = (3, dy // 2) if slot == 7 else divmod(slot - 1, 2)
            index = 12 + dy % 2 if slot == 7 else m * NY + -dy % NY
            dst = relayed.at[:, d, index] if both else relayed.at[c, d, index]
            device = at(dy, -m if d == 0 else m)
        return remote(("back", 0 if both else c, slot, dy), src, dst, device)

    def summed_copy(c, d, part):
        groups_of = pl.ds(part * GROUPS // 2, GROUPS // 2)
        return remote(
            ("summed", c, d, part), summed.at[c, d, groups_of], back_in[c][d].at[groups_of],
            at(0, -1 if d == 0 else 1),
        )

    def returned(slot):
        return (1, 2, 3) if slot < 3 else (0, 1, 2, 3)

    def fill(c, chunk):
        rows = rows_of(chunk)
        if c == 1:
            p = e_buf[rows, :].astype(F32) * coef[chunk]
            p_buf[rows, :] = p.astype(BF16)
            return mm(p_buf[rows, :], gs[...])
        ds = p_buf[rows, :].astype(F32) * (dp_buf[rows, :] - row_delta[...])
        ds_buf[rows, :] = ds.astype(BF16)
        return mm(ds_buf[rows, :], qs[...]) * SCALE

    def send_back(c, slots):
        for slot in slots:
            terms[c, slot * SLOT : (slot + 1) * SLOT, :] = fill(c, slot).astype(BF16)
        if slots == (0,) and c == 1:
            return
        for dy in (0, 2, 1, 3):
            for slot in slots:
                if dy in returned(slot):
                    go(back(c, slot, dy))

    def mark(d, i, g):
        return marks[(d * 14 + i) * GROUPS + g]

    def mine(c, slot):
        return terms[c, slot * SLOT : slot * SLOT + BLOCK, :].astype(F32)

    def add_up(c):
        for d in range(2):
            for slot in (7, 5 + d, 3 + d, 1 + d):
                for dy in (2 * d, 2 * d + 1) if slot == 7 else returned(slot):
                    back(c, slot, dy).wait_recv()
        for part in range(2):
            for d in range(2):

                def one(i):
                    g = part * GROUPS // 2 + i
                    result = mine(c, 1 + d) * mark(d, 0, g)
                    for i in range(1, 14):
                        result = result + relayed[c, d, i].astype(F32) * mark(d, i, g)
                    summed[c, d, g] = result.astype(BF16)

                each_pair(GROUPS // 2, one)
                go(summed_copy(c, d, part))

    def add_up_own(c):
        def one(g):
            result = mine(c, 0) * mark(0, 0, g)
            for dy in range(1, NY):
                result = result + direct[c, dy].astype(F32) * mark(0, dy, g)
            local[c, g] = result

        each_pair(GROUPS, one)

    def finish(c):
        for part in range(2):
            for d in range(2):
                summed_copy(c, d, part).wait_recv()
        for slot in range(GROUPS):
            g = pg_ref[0, slot]
            result = back_in[c][0][g].astype(F32) + back_in[c][1][g].astype(F32)
            op_ref[0, slot, :, c * HEAD : (c + 1) * HEAD] = (result + local[c, g]).astype(BF16)

    listed = []
    for d, sign in ((0, 1), (1, -1)):
        for m in range(3):
            listed += groups[sign * m]
        listed += [groups[sign * 3][-dy % NY] for dy in (2 * d, 2 * d + 1)]
    for n, group in enumerate(listed):
        for g in range(GROUPS):
            marks[n * GROUPS + g] = jnp.where(group == g, 1.0, 0.0).astype(F32)
    for slots in ((7,), (5, 6), (3, 4)):
        send_back(1, slots)
    arrived(1, 1)
    level_of(1, slopes)
    arrived(1, 2)
    level_of(2, slopes)
    arrived(1, 3)
    level_of(3, slopes)
    delta = dots[0] * coef[0]
    for chunk in range(1, LAST + 1):
        delta = delta + dots[chunk] * coef[chunk]
    row_delta[...] = delta
    for slots in ((7,), (5, 6), (3, 4)):
        send_back(0, slots)
    send_back(1, (1, 2))
    send_back(0, (1, 2))
    add_up(1)
    add_up(0)
    send_back(1, (0,))
    send_back(0, (0,))
    or_ref[:, HEAD:] = fill(1, LAST).astype(BF16)
    or_ref[:, :HEAD] = fill(0, LAST).astype(BF16)
    dq = mm(kv[0].T, ds_buf[...]) * SCALE
    for h in range(HEADS):
        oq_ref[:, h * HEAD : (h + 1) * HEAD] = dq[:, h * HEAD : (h + 1) * HEAD].T.astype(BF16)
    for dy in returned(0):
        back(0, 0, dy).wait_recv()
    add_up_own(1)
    add_up_own(0)
    finish(1)
    for copy in started:
        copy.wait_send()
    finish(0)


def hand_on(*refs):
    sem = refs[6]
    copies = [pltpu.make_async_copy(refs[n], refs[3 + n], sem.at[n]) for n in range(3)]
    for copy in copies:
        copy.start()
    for copy in copies:
        copy.wait()


def body(
    queries, response_key_value, prompt_kv, prompt_group, response_order, live_blocks,
    out_weight, grad_out,
):
    hbm = pl.BlockSpec(memory_space=pl.ANY)
    vmem = pl.BlockSpec(memory_space=pltpu.VMEM)
    smem = pl.BlockSpec(memory_space=pltpu.SMEM)
    block = (BLOCK, HEAD)

    def space(*shape, kind=BF16):
        return pltpu.VMEM(shape, kind)

    def streams():
        return [[space(GROUPS, *block) for _ in range(2)] for _ in range(2)]

    scratch = [
        space(*queries.shape),
        space(*prompt_kv.shape),
        space(NX, WIDTH, 2 * WIDTH),
        space(NX, TOKENS, 2 * WIDTH),
        space(WIDTH, HEAD),
        space(WIDTH, HEAD),
        space(2, GROUPS, *block),
        streams(),
        space(2, 2, 4, NY, *block),
        space(2, NY, *block),
        space(2, PROMPT + TOKENS, HEAD),
        space(PROMPT + TOKENS, WIDTH),
        space(PROMPT + TOKENS, WIDTH),
        space(PROMPT + TOKENS, WIDTH, kind=F32),
        space(PROMPT + TOKENS, WIDTH),
        space(LAST + 1, 1, WIDTH, kind=F32),
        space(LAST + 1, 1, WIDTH, kind=F32),
        space(LAST + 1, 1, WIDTH, kind=F32),
        space(LAST + 1, 1, WIDTH, kind=F32),
        space(1, WIDTH, kind=F32),
        space(2, PROMPT, HEAD),
        space(2, 2, 14, *block),
        space(2, NY, *block),
        space(2, 2, GROUPS, *block),
        streams(),
        space(2, GROUPS, *block, kind=F32),
        pltpu.SMEM((28 * GROUPS,), F32),
        pltpu.SemaphoreType.DMA((5,)),
        pltpu.SemaphoreType.DMA((NX, 2)),
        pltpu.SemaphoreType.DMA((N_COPIES,)),
        pltpu.SemaphoreType.DMA((N_COPIES,)),
    ]
    kinds = tuple(
        jax.ShapeDtypeStruct(a.shape, BF16) for a in (queries, response_key_value, prompt_kv)
    )
    outs = pl.pallas_call(
        kernel,
        out_shape=tuple(pltpu.VMEM(a.shape, BF16) for a in kinds),
        in_specs=[hbm, hbm, hbm, smem, smem, smem, hbm, hbm],
        out_specs=(vmem, vmem, vmem),
        scratch_shapes=scratch,
        compiler_params=pltpu.CompilerParams(
            collective_id=0, has_side_effects=True, vmem_limit_bytes=56 * 1024 * 1024
        ),
        cost_estimate=pl.CostEstimate(
            flops=3_000_000_000, bytes_accessed=8_000_000, transcendentals=1_400_000
        ),
    )(
        queries, response_key_value, prompt_kv, prompt_group, response_order, live_blocks,
        out_weight, grad_out,
    )
    outs = [pltpu.with_memory_space_constraint(out, pltpu.VMEM) for out in outs]
    return pl.pallas_call(
        hand_on,
        out_shape=kinds,
        in_specs=[vmem, vmem, vmem],
        out_specs=(hbm, hbm, hbm),
        scratch_shapes=[pltpu.SemaphoreType.DMA((3,))],
        compiler_params=pltpu.CompilerParams(vmem_limit_bytes=1024 * 1024),
    )(*outs)


def solution(mesh):
    return jax.shard_map(
        body,
        mesh=mesh,
        in_specs=(
            P("dp", "tensor"),
            P("dp", "tensor"),
            P("dp", None, None, "tensor"),
            P("dp", None),
            P(),
            P("dp"),
            P("tensor", None),
            P("dp", "tensor"),
        ),
        out_specs=(P("dp", "tensor"), P("dp", "tensor"), P("dp", None, None, "tensor")),
        check_vma=False,
    )
```

```python
import math

import jax
import jax.numpy as jnp
from jax import lax
from jax.experimental import pallas as pl
from jax.experimental.pallas import tpu as pltpu
from jax.sharding import PartitionSpec as P

HEAD = 128
HEADS = 5
WIDTH = HEAD * HEADS
TOKENS = 128
BLOCK = 64
GROUPS = 8
NY, NZ, NX = 4, 8, 4
PROMPT = NZ * NY * BLOCK
SLOT = NY * BLOCK
SCALE = 1.0 / math.sqrt(HEAD)
EXP2_SCALE = SCALE * math.log2(math.e)
N_COPIES = 150
MESH = pl.DeviceIdType.MESH
BF16, F32 = jnp.bfloat16, jnp.float32

def mm(a, b):
    return jnp.dot(a, b, preferred_element_type=F32)


def mm_t(a, b):
    return lax.dot_general(a, b, (((1,), (1,)), ((), ())), preferred_element_type=F32)


def fold(x, op):
    return op(x.reshape(x.shape[0] // 8, 8, x.shape[1]), axis=0)


def each(count, step):
    def run(index, carry):
        step(index)
        return carry

    lax.fori_loop(0, count, run, 0)


def each_pair(count, step):
    def both(index):
        step(2 * index)
        step(2 * index + 1)

    each(count // 2, both)


LEVELS = [(0,), (1, 2), (3, 4), (5, 6, 7)]
LAST = 8


def kernel(
    q_ref, rkv_ref, pkv_ref, pg_ref, ro_ref, lb_ref, w_ref, go_ref,
    oq_ref, or_ref, op_ref,
    q_v, pkv_v,
    w_v, gathered, qs, gs,
    own, r1, picked, picked_own, kv,
    e_buf, p_buf, dp_buf, ds_buf,
    tops, sums, dots, coef, row_delta,
    terms, relayed, direct, summed, back_in, local,
    marks, in_sem, w_sem, send_sem, recv_sem,
):
    dp = lax.axis_index("dp")
    tensor = lax.axis_index("tensor")
    y, z = lax.div(dp, NZ), lax.rem(dp, NZ)
    x, core = lax.div(tensor, 2), lax.rem(tensor, 2)

    ys = [lax.rem(y + dy, NY) for dy in range(NY)]
    zs = {dz: lax.rem(z + dz + NZ, NZ) for dz in range(-3, 4)}
    places = {(dy, dz): ys[dy] * NZ + zs[dz] for dy in range(NY) for dz in zs}
    along_x = {step: lax.rem(x + step + NX, NX) * 2 + core for step in (-1, 1)}

    def at(dy, dz):
        return (places[dy, dz], tensor)

    def at_x(step):
        return (dp, along_x[step])

    sibling = (dp, x * 2 + 1 - core)

    numbers = {}
    started = []

    def remote(name, src, dst, device):
        n = numbers.setdefault(name, len(numbers))
        return pltpu.make_async_remote_copy(
            src_ref=src, dst_ref=dst, send_sem=send_sem.at[n], recv_sem=recv_sem.at[n],
            device_id=device, device_id_type=MESH,
        )

    def go(copy):
        copy.start()
        started.append(copy)

    in_copies = [
        pltpu.make_async_copy(src, dst, in_sem.at[n])
        for n, (src, dst) in enumerate(
            [
                (pkv_ref, pkv_v), (go_ref, gathered.at[0, :, pl.ds(0, WIDTH)]), (q_ref, q_v),
                (rkv_ref.at[:, pl.ds(0, HEAD)], kv.at[0, pl.ds(PROMPT, TOKENS)]),
                (rkv_ref.at[:, pl.ds(HEAD, HEAD)], kv.at[1, pl.ds(PROMPT, TOKENS)]),
            ]
        )
    ]
    in_copies[0].start()
    barrier = pltpu.get_barrier_semaphore()
    partners = [at(dy, dz) for dz in range(-3, 4) for dy in range(NY) if (dy, dz) != (0, 0)]
    partners += [at_x(1), at_x(-1), sibling]
    for partner in partners:
        pl.semaphore_signal(barrier, inc=1, device_id=partner, device_id_type=MESH)
    for copy in in_copies[1:]:
        copy.start()

    w_copies = {}
    for r in (0, 1, 3, 2):
        for other in range(2):
            piece = lax.rem(x + r, NX) * 2 + (core if other == 0 else 1 - core)
            copy = pltpu.make_async_copy(
                w_ref.at[:, pl.ds(pl.multiple_of(piece * WIDTH, WIDTH), WIDTH)],
                w_v.at[r, :, pl.ds(other * WIDTH, WIDTH)], w_sem.at[r, other],
            )
            copy.start()
            w_copies[r, other] = copy

    slot_of = []
    for g in range(GROUPS):
        slot = jnp.int32(0)
        for c in range(GROUPS):
            slot = jnp.where(pg_ref[0, c] == g, c, slot)
        slot_of.append(slot)
    in_copies[0].wait()
    for g in range(GROUPS):
        own[0, g] = pkv_v[0, slot_of[g], :, :HEAD]
    pl.semaphore_wait(barrier, len(partners))

    def first_hop(c, d):
        return remote(("first", c, d), own.at[c], r1[c][d], at(0, 1 if d == 0 else -1))

    def place(slot, dy):
        return pl.ds(slot * SLOT + (dy % NY) * BLOCK, BLOCK)

    def own_copy(dy):
        return remote(
            ("own", dy), picked_own.at[:, dy], kv.at[:, place(0, -dy)], at(dy, 0)
        )

    def forward(c, d, m, dy):
        slot = 7 if m == 3 else 1 + d + 2 * m
        return remote(
            ("forward", c, d, m, dy), picked.at[c, d, m, dy], kv.at[c, place(slot, -dy)],
            at(dy, m if d == 0 else -m),
        )

    def sent(d, m):
        if m == 3:
            return (2 * d, 2 * d + 1)
        return (1, 2, 3) if m == 0 else (0, 1, 2, 3)

    def relay(c):
        for d in range(2):
            first_hop(c, d).wait_recv()
        for m in (3, 2, 1, 0):
            for pair in zip(sent(0, m), sent(1, m)):
                for d, dy in enumerate(pair):
                    picked[c, d, m, dy] = r1[c][d][groups[m if d == 0 else -m][dy]]
                    go(forward(c, d, m, dy))
        for d in range(2):
            kv[c, (1 + d) * SLOT : (1 + d) * SLOT + BLOCK, :] = r1[c][d][groups[0][0]]

    def arrived(c, level):
        if level == 0:
            for dy in range(1, NY):
                own_copy(dy).wait_recv()
        else:
            for m in (3, 2) if level == 3 else (level - 1,):
                for d in range(2):
                    for dy in sent(d, m):
                        forward(c, d, m, dy).wait_recv()

    half = TOKENS // 2

    def slice_of(r, other, rows=pl.ds(0, TOKENS)):
        return gathered.at[r, rows, pl.ds(other * WIDTH, WIDTH)]

    def x_copy(way, part):
        rows = pl.ds(part * half, half)
        return remote(
            ("x", way, part), slice_of(0, 0, rows), slice_of(1 if way == 0 else 3, 0, rows),
            at_x(-1 if way == 0 else 1),
        )

    def x_pass(way):
        rows = pl.ds(way * half, half)
        return remote(
            ("x", way, 2), slice_of(1 if way == 0 else 3, 0, rows), slice_of(2, 0, rows),
            at_x(-1 if way == 0 else 1),
        )

    def share(r):
        return remote(("share", r), slice_of(r, 0), slice_of(r, 1), sibling)

    for d in range(2):
        go(first_hop(0, d))
    for copy in in_copies[1:]:
        copy.wait()
    for part in range(2):
        for way in range(2):
            go(x_copy(way, way if part == 0 else 1 - way))
    go(share(0))

    for g in range(GROUPS):
        own[1, g] = pkv_v[0, slot_of[g], :, HEAD:]
    for d in range(2):
        go(first_hop(1, d))

    groups = {
        dz: [lax.div(ro_ref[places[dy, dz]], 4) for dy in range(NY)] for dz in range(-3, 4)
    }
    for dy in range(NY):
        for c in range(2):
            if dy == 0:
                kv[c, 0:BLOCK, :] = own[c, groups[0][0]]
            else:
                picked_own[c, dy] = own[c, groups[0][dy]]
        if dy > 0:
            go(own_copy(dy))

    def rows_of(chunk):
        if isinstance(chunk, int) and chunk == LAST:
            return pl.ds(PROMPT, TOKENS)
        return pl.ds(pl.multiple_of(chunk * SLOT, SLOT), SLOT)

    def scores(chunk):
        rows = rows_of(chunk)
        s = mm_t(kv[0, rows, :], qs[...])
        if isinstance(chunk, int) and chunk == LAST:
            key_pos = lax.broadcasted_iota(jnp.int32, s.shape, 0)
            query_pos = lax.broadcasted_iota(jnp.int32, s.shape, 1) % TOKENS
            s = jnp.where(key_pos <= query_pos, s, -jnp.inf)
        top = jnp.max(fold(s, jnp.max), axis=0, keepdims=True)
        e = jnp.exp2((s - top) * EXP2_SCALE)
        e_buf[rows, :] = e.astype(BF16)
        tops[chunk] = top
        sums[chunk] = jnp.sum(fold(e, jnp.sum), axis=0, keepdims=True)

    def slopes(chunk):
        rows = rows_of(chunk)
        values = mm_t(kv[1, rows, :], gs[...])
        dp_buf[rows, :] = values
        products = values * e_buf[rows, :].astype(F32)
        dots[chunk] = jnp.sum(fold(products, jnp.sum), axis=0, keepdims=True)

    def level_of(number, step):
        slots = LEVELS[number]
        each(len(slots), lambda i: step(slots[0] + i))

    def project(r):
        for other in range(2):
            w_copies[r, other].wait()
        return mm_t(w_v[r], gathered[r])

    for h in range(HEADS):
        qs[h * HEAD : (h + 1) * HEAD, :] = q_v[:, h * HEAD : (h + 1) * HEAD]
    scores(LAST)
    share(0).wait_recv()
    grad = project(0)
    for way in range(2):
        x_copy(way, way).wait_recv()
        go(x_pass(way))
    relay(0)
    for way in range(2):
        x_copy(way, 1 - way).wait_recv()
        go(share(1 if way == 0 else 3))
    relay(1)
    arrived(0, 0)
    level_of(0, scores)
    share(1).wait_recv()
    grad = grad + project(1)
    for way in range(2):
        x_pass(way).wait_recv()
    go(share(2))
    share(3).wait_recv()
    grad = grad + project(3)
    arrived(0, 1)
    level_of(1, scores)
    share(2).wait_recv()
    grad = grad + project(2)
    column = lax.broadcasted_iota(jnp.int32, grad.shape, 1)
    grad = jnp.where(column < lb_ref[0] * TOKENS, grad, 0.0).astype(BF16)
    for h in range(HEADS):
        rows = slice(h * HEAD, (h + 1) * HEAD)
        gs[rows, :] = grad[rows, :].T

    slopes(LAST)
    level_of(0, slopes)
    arrived(0, 2)
    level_of(2, scores)
    arrived(0, 3)
    level_of(3, scores)

    highest = tops[0]
    for chunk in range(1, LAST + 1):
        highest = jnp.maximum(highest, tops[chunk])
    factors = [jnp.exp2((tops[chunk] - highest) * EXP2_SCALE) for chunk in range(LAST + 1)]
    total = sums[0] * factors[0]
    for chunk in range(1, LAST + 1):
        total = total + sums[chunk] * factors[chunk]
    for chunk in range(LAST + 1):
        coef[chunk] = factors[chunk] / total

    def back(c, slot, dy):
        both = slot == 0
        rows = place(slot, dy)
        src = terms.at[:, rows] if both else terms.at[c, rows]
        if slot == 0:
            dst, device = direct.at[:, -dy % NY], at(dy, 0)
        else:
            m, d = (3, dy // 2) if slot == 7 else divmod(slot - 1, 2)
            index = 12 + dy % 2 if slot == 7 else m * NY + -dy % NY
            dst = relayed.at[:, d, index] if both else relayed.at[c, d, index]
            device = at(dy, -m if d == 0 else m)
        return remote(("back", 0 if both else c, slot, dy), src, dst, device)

    def summed_copy(c, d, part):
        groups_of = pl.ds(part * GROUPS // 2, GROUPS // 2)
        return remote(
            ("summed", c, d, part), summed.at[c, d, groups_of], back_in[c][d].at[groups_of],
            at(0, -1 if d == 0 else 1),
        )

    def returned(slot):
        return (1, 2, 3) if slot < 3 else (0, 1, 2, 3)

    def fill(c, chunk):
        rows = rows_of(chunk)
        if c == 1:
            p = e_buf[rows, :].astype(F32) * coef[chunk]
            p_buf[rows, :] = p.astype(BF16)
            return mm(p_buf[rows, :], gs[...])
        ds = p_buf[rows, :].astype(F32) * (dp_buf[rows, :] - row_delta[...])
        ds_buf[rows, :] = ds.astype(BF16)
        return mm(ds_buf[rows, :], qs[...]) * SCALE

    def send_back(c, slots):
        for slot in slots:
            terms[c, slot * SLOT : (slot + 1) * SLOT, :] = fill(c, slot).astype(BF16)
        if slots == (0,) and c == 1:
            return
        for dy in (0, 2, 1, 3):
            for slot in slots:
                if dy in returned(slot):
                    go(back(c, slot, dy))

    def mark(d, i, g):
        return marks[(d * 14 + i) * GROUPS + g]

    def mine(c, slot):
        return terms[c, slot * SLOT : slot * SLOT + BLOCK, :].astype(F32)

    def add_up(c):
        for d in range(2):
            for slot in (7, 5 + d, 3 + d, 1 + d):
                for dy in (2 * d, 2 * d + 1) if slot == 7 else returned(slot):
                    back(c, slot, dy).wait_recv()
        for part in range(2):
            for d in range(2):

                def one(i):
                    g = part * GROUPS // 2 + i
                    result = mine(c, 1 + d) * mark(d, 0, g)
                    for i in range(1, 14):
                        result = result + relayed[c, d, i].astype(F32) * mark(d, i, g)
                    summed[c, d, g] = result.astype(BF16)

                each_pair(GROUPS // 2, one)
                go(summed_copy(c, d, part))

    def add_up_own(c):
        def one(g):
            result = mine(c, 0) * mark(0, 0, g)
            for dy in range(1, NY):
                result = result + direct[c, dy].astype(F32) * mark(0, dy, g)
            local[c, g] = result

        each_pair(GROUPS, one)

    def finish(c):
        for part in range(2):
            for d in range(2):
                summed_copy(c, d, part).wait_recv()
        for slot in range(GROUPS):
            g = pg_ref[0, slot]
            result = back_in[c][0][g].astype(F32) + back_in[c][1][g].astype(F32)
            op_ref[0, slot, :, c * HEAD : (c + 1) * HEAD] = (result + local[c, g]).astype(BF16)

    listed = []
    for d, sign in ((0, 1), (1, -1)):
        for m in range(3):
            listed += groups[sign * m]
        listed += [groups[sign * 3][-dy % NY] for dy in (2 * d, 2 * d + 1)]
    for n, group in enumerate(listed):
        for g in range(GROUPS):
            marks[n * GROUPS + g] = jnp.where(group == g, 1.0, 0.0).astype(F32)
    for slots in ((7,), (5, 6), (3, 4)):
        send_back(1, slots)
    arrived(1, 1)
    level_of(1, slopes)
    arrived(1, 2)
    level_of(2, slopes)
    arrived(1, 3)
    level_of(3, slopes)
    delta = dots[0] * coef[0]
    for chunk in range(1, LAST + 1):
        delta = delta + dots[chunk] * coef[chunk]
    row_delta[...] = delta
    for slots in ((7,), (5, 6), (3, 4)):
        send_back(0, slots)
    send_back(1, (1, 2))
    send_back(0, (1, 2))
    add_up(1)
    add_up(0)
    send_back(1, (0,))
    send_back(0, (0,))
    or_ref[:, HEAD:] = fill(1, LAST).astype(BF16)
    or_ref[:, :HEAD] = fill(0, LAST).astype(BF16)
    dq = mm(kv[0].T, ds_buf[...]) * SCALE
    for h in range(HEADS):
        oq_ref[:, h * HEAD : (h + 1) * HEAD] = dq[:, h * HEAD : (h + 1) * HEAD].T.astype(BF16)
    for dy in returned(0):
        back(0, 0, dy).wait_recv()
    add_up_own(1)
    add_up_own(0)
    finish(1)
    for copy in started:
        copy.wait_send()
    finish(0)


def hand_on(*refs):
    sem = refs[6]
    copies = [pltpu.make_async_copy(refs[n], refs[3 + n], sem.at[n]) for n in range(3)]
    for copy in copies:
        copy.start()
    for copy in copies:
        copy.wait()


def body(
    queries, response_key_value, prompt_kv, prompt_group, response_order, live_blocks,
    out_weight, grad_out,
):
    hbm = pl.BlockSpec(memory_space=pl.ANY)
    vmem = pl.BlockSpec(memory_space=pltpu.VMEM)
    smem = pl.BlockSpec(memory_space=pltpu.SMEM)
    block = (BLOCK, HEAD)

    def space(*shape, kind=BF16):
        return pltpu.VMEM(shape, kind)

    def streams():
        return [[space(GROUPS, *block) for _ in range(2)] for _ in range(2)]

    scratch = [
        space(*queries.shape),
        space(*prompt_kv.shape),
        space(NX, WIDTH, 2 * WIDTH),
        space(NX, TOKENS, 2 * WIDTH),
        space(WIDTH, HEAD),
        space(WIDTH, HEAD),
        space(2, GROUPS, *block),
        streams(),
        space(2, 2, 4, NY, *block),
        space(2, NY, *block),
        space(2, PROMPT + TOKENS, HEAD),
        space(PROMPT + TOKENS, WIDTH),
        space(PROMPT + TOKENS, WIDTH),
        space(PROMPT + TOKENS, WIDTH, kind=F32),
        space(PROMPT + TOKENS, WIDTH),
        space(LAST + 1, 1, WIDTH, kind=F32),
        space(LAST + 1, 1, WIDTH, kind=F32),
        space(LAST + 1, 1, WIDTH, kind=F32),
        space(LAST + 1, 1, WIDTH, kind=F32),
        space(1, WIDTH, kind=F32),
        space(2, PROMPT, HEAD),
        space(2, 2, 14, *block),
        space(2, NY, *block),
        space(2, 2, GROUPS, *block),
        streams(),
        space(2, GROUPS, *block, kind=F32),
        pltpu.SMEM((28 * GROUPS,), F32),
        pltpu.SemaphoreType.DMA((5,)),
        pltpu.SemaphoreType.DMA((NX, 2)),
        pltpu.SemaphoreType.DMA((N_COPIES,)),
        pltpu.SemaphoreType.DMA((N_COPIES,)),
    ]
    kinds = tuple(
        jax.ShapeDtypeStruct(a.shape, BF16) for a in (queries, response_key_value, prompt_kv)
    )
    outs = pl.pallas_call(
        kernel,
        out_shape=tuple(pltpu.VMEM(a.shape, BF16) for a in kinds),
        in_specs=[hbm, hbm, hbm, smem, smem, smem, hbm, hbm],
        out_specs=(vmem, vmem, vmem),
        scratch_shapes=scratch,
        compiler_params=pltpu.CompilerParams(
            collective_id=0, has_side_effects=True, vmem_limit_bytes=56 * 1024 * 1024
        ),
        cost_estimate=pl.CostEstimate(
            flops=3_000_000_000, bytes_accessed=8_000_000, transcendentals=1_400_000
        ),
    )(
        queries, response_key_value, prompt_kv, prompt_group, response_order, live_blocks,
        out_weight, grad_out,
    )
    outs = [pltpu.with_memory_space_constraint(out, pltpu.VMEM) for out in outs]
    return pl.pallas_call(
        hand_on,
        out_shape=kinds,
        in_specs=[vmem, vmem, vmem],
        out_specs=(hbm, hbm, hbm),
        scratch_shapes=[pltpu.SemaphoreType.DMA((3,))],
        compiler_params=pltpu.CompilerParams(vmem_limit_bytes=1024 * 1024),
    )(*outs)


def solution(mesh):
    return jax.shard_map(
        body,
        mesh=mesh,
        in_specs=(
            P("dp", "tensor"),
            P("dp", "tensor"),
            P("dp", None, None, "tensor"),
            P("dp", None),
            P(),
            P("dp"),
            P("tensor", None),
            P("dp", "tensor"),
        ),
        out_specs=(P("dp", "tensor"), P("dp", "tensor"), P("dp", None, None, "tensor")),
        check_vma=False,
    )
```

```python
import math

import jax
import jax.numpy as jnp
from jax import lax
from jax.experimental import pallas as pl
from jax.experimental.pallas import tpu as pltpu
from jax.sharding import PartitionSpec as P

HEAD = 128
HEADS = 5
WIDTH = HEAD * HEADS
TOKENS = 128
BLOCK = 64
GROUPS = 8
NY, NZ, NX = 4, 8, 4
PROMPT = NZ * NY * BLOCK
SLOT = NY * BLOCK
SCALE = 1.0 / math.sqrt(HEAD)
EXP2_SCALE = SCALE * math.log2(math.e)
N_COPIES = 150
MESH = pl.DeviceIdType.MESH
BF16, F32 = jnp.bfloat16, jnp.float32

def mm(a, b):
    return jnp.dot(a, b, preferred_element_type=F32)


def mm_t(a, b):
    return lax.dot_general(a, b, (((1,), (1,)), ((), ())), preferred_element_type=F32)


def fold(x, op):
    return op(x.reshape(x.shape[0] // 8, 8, x.shape[1]), axis=0)


def each(count, step):
    def run(index, carry):
        step(index)
        return carry

    lax.fori_loop(0, count, run, 0)


def each_pair(count, step):
    def both(index):
        step(2 * index)
        step(2 * index + 1)

    each(count // 2, both)


LEVELS = [(0,), (1, 2), (3, 4), (5, 6, 7)]
LAST = 8


def kernel(
    q_ref, rkv_ref, pkv_ref, pg_ref, ro_ref, lb_ref, w_ref, go_ref,
    oq_ref, or_ref, op_ref,
    q_v, pkv_v,
    w_v, gathered, qs, gs,
    own, r1, picked, picked_own, kv, keys_turned,
    e_buf, p_buf, dp_buf, ds_buf,
    tops, sums, dots, coef, row_delta,
    terms, relayed, direct, summed, back_in, local,
    marks, in_sem, w_sem, send_sem, recv_sem,
):
    dp = lax.axis_index("dp")
    tensor = lax.axis_index("tensor")
    y, z = lax.div(dp, NZ), lax.rem(dp, NZ)
    x, core = lax.div(tensor, 2), lax.rem(tensor, 2)

    ys = [lax.rem(y + dy, NY) for dy in range(NY)]
    zs = {dz: lax.rem(z + dz + NZ, NZ) for dz in range(-3, 4)}
    places = {(dy, dz): ys[dy] * NZ + zs[dz] for dy in range(NY) for dz in zs}
    along_x = {step: lax.rem(x + step + NX, NX) * 2 + core for step in (-1, 1)}

    def at(dy, dz):
        return (places[dy, dz], tensor)

    def at_x(step):
        return (dp, along_x[step])

    sibling = (dp, x * 2 + 1 - core)

    numbers = {}
    started = []

    def remote(name, src, dst, device):
        n = numbers.setdefault(name, len(numbers))
        return pltpu.make_async_remote_copy(
            src_ref=src, dst_ref=dst, send_sem=send_sem.at[n], recv_sem=recv_sem.at[n],
            device_id=device, device_id_type=MESH,
        )

    def go(copy):
        copy.start()
        started.append(copy)

    in_copies = [
        pltpu.make_async_copy(src, dst, in_sem.at[n])
        for n, (src, dst) in enumerate(
            [
                (pkv_ref, pkv_v), (go_ref, gathered.at[0, :, pl.ds(0, WIDTH)]), (q_ref, q_v),
                (rkv_ref.at[:, pl.ds(0, HEAD)], kv.at[0, pl.ds(PROMPT, TOKENS)]),
                (rkv_ref.at[:, pl.ds(HEAD, HEAD)], kv.at[1, pl.ds(PROMPT, TOKENS)]),
            ]
        )
    ]
    in_copies[0].start()
    barrier = pltpu.get_barrier_semaphore()
    partners = [at(dy, dz) for dz in range(-3, 4) for dy in range(NY) if (dy, dz) != (0, 0)]
    partners += [at_x(1), at_x(-1), sibling]
    for partner in partners:
        pl.semaphore_signal(barrier, inc=1, device_id=partner, device_id_type=MESH)
    for copy in in_copies[1:]:
        copy.start()

    w_copies = {}
    for r in (0, 1, 3, 2):
        for other in range(2):
            piece = lax.rem(x + r, NX) * 2 + (core if other == 0 else 1 - core)
            copy = pltpu.make_async_copy(
                w_ref.at[:, pl.ds(pl.multiple_of(piece * WIDTH, WIDTH), WIDTH)],
                w_v.at[r, :, pl.ds(other * WIDTH, WIDTH)], w_sem.at[r, other],
            )
            copy.start()
            w_copies[r, other] = copy

    slot_of = []
    for g in range(GROUPS):
        slot = jnp.int32(0)
        for c in range(GROUPS):
            slot = jnp.where(pg_ref[0, c] == g, c, slot)
        slot_of.append(slot)
    in_copies[0].wait()
    for g in range(GROUPS):
        own[0, g] = pkv_v[0, slot_of[g], :, :HEAD]
    pl.semaphore_wait(barrier, len(partners))

    def first_hop(c, d):
        return remote(("first", c, d), own.at[c], r1[c][d], at(0, 1 if d == 0 else -1))

    def place(slot, dy):
        return pl.ds(slot * SLOT + (dy % NY) * BLOCK, BLOCK)

    def own_copy(dy):
        return remote(
            ("own", dy), picked_own.at[:, dy], kv.at[:, place(0, -dy)], at(dy, 0)
        )

    def forward(c, d, m, dy):
        slot = 7 if m == 3 else 1 + d + 2 * m
        return remote(
            ("forward", c, d, m, dy), picked.at[c, d, m, dy], kv.at[c, place(slot, -dy)],
            at(dy, m if d == 0 else -m),
        )

    def sent(d, m):
        if m == 3:
            return (2 * d, 2 * d + 1)
        return (1, 2, 3) if m == 0 else (0, 1, 2, 3)

    def relay(c):
        for d in range(2):
            first_hop(c, d).wait_recv()
        for m in (3, 2, 1, 0):
            for pair in zip(sent(0, m), sent(1, m)):
                for d, dy in enumerate(pair):
                    picked[c, d, m, dy] = r1[c][d][groups[m if d == 0 else -m][dy]]
                    go(forward(c, d, m, dy))
        for d in range(2):
            kv[c, (1 + d) * SLOT : (1 + d) * SLOT + BLOCK, :] = r1[c][d][groups[0][0]]

    def arrived(c, level):
        if level == 0:
            for dy in range(1, NY):
                own_copy(dy).wait_recv()
        else:
            for m in (3, 2) if level == 3 else (level - 1,):
                for d in range(2):
                    for dy in sent(d, m):
                        forward(c, d, m, dy).wait_recv()

    half = TOKENS // 2

    def slice_of(r, other, rows=pl.ds(0, TOKENS)):
        return gathered.at[r, rows, pl.ds(other * WIDTH, WIDTH)]

    def x_copy(way, part):
        rows = pl.ds(part * half, half)
        return remote(
            ("x", way, part), slice_of(0, 0, rows), slice_of(1 if way == 0 else 3, 0, rows),
            at_x(-1 if way == 0 else 1),
        )

    def x_pass(way):
        rows = pl.ds(way * half, half)
        return remote(
            ("x", way, 2), slice_of(1 if way == 0 else 3, 0, rows), slice_of(2, 0, rows),
            at_x(-1 if way == 0 else 1),
        )

    def share(r):
        return remote(("share", r), slice_of(r, 0), slice_of(r, 1), sibling)

    for d in range(2):
        go(first_hop(0, d))
    for copy in in_copies[1:]:
        copy.wait()
    for part in range(2):
        for way in range(2):
            go(x_copy(way, way if part == 0 else 1 - way))
    go(share(0))

    for g in range(GROUPS):
        own[1, g] = pkv_v[0, slot_of[g], :, HEAD:]
    for d in range(2):
        go(first_hop(1, d))

    groups = {
        dz: [lax.div(ro_ref[places[dy, dz]], 4) for dy in range(NY)] for dz in range(-3, 4)
    }
    for dy in range(NY):
        for c in range(2):
            if dy == 0:
                kv[c, 0:BLOCK, :] = own[c, groups[0][0]]
            else:
                picked_own[c, dy] = own[c, groups[0][dy]]
        if dy > 0:
            go(own_copy(dy))

    def rows_of(chunk):
        if isinstance(chunk, int) and chunk == LAST:
            return pl.ds(PROMPT, TOKENS)
        return pl.ds(pl.multiple_of(chunk * SLOT, SLOT), SLOT)

    def scores(chunk):
        rows = rows_of(chunk)
        s = mm_t(kv[0, rows, :], qs[...])
        if isinstance(chunk, int) and chunk == LAST:
            key_pos = lax.broadcasted_iota(jnp.int32, s.shape, 0)
            query_pos = lax.broadcasted_iota(jnp.int32, s.shape, 1) % TOKENS
            s = jnp.where(key_pos <= query_pos, s, -jnp.inf)
        top = jnp.max(fold(s, jnp.max), axis=0, keepdims=True)
        e = jnp.exp2((s - top) * EXP2_SCALE)
        e_buf[rows, :] = e.astype(BF16)
        tops[chunk] = top
        sums[chunk] = jnp.sum(fold(e, jnp.sum), axis=0, keepdims=True)

    def slopes(chunk):
        rows = rows_of(chunk)
        values = mm_t(kv[1, rows, :], gs[...])
        dp_buf[rows, :] = values
        products = values * e_buf[rows, :].astype(F32)
        dots[chunk] = jnp.sum(fold(products, jnp.sum), axis=0, keepdims=True)

    def level_of(number, step):
        slots = LEVELS[number]
        each(len(slots), lambda i: step(slots[0] + i))

    def project(r):
        for other in range(2):
            w_copies[r, other].wait()
        return mm_t(w_v[r], gathered[r])

    for h in range(HEADS):
        qs[h * HEAD : (h + 1) * HEAD, :] = q_v[:, h * HEAD : (h + 1) * HEAD]
    scores(LAST)
    share(0).wait_recv()
    grad = project(0)
    for way in range(2):
        x_copy(way, way).wait_recv()
        go(x_pass(way))
    relay(0)
    for way in range(2):
        x_copy(way, 1 - way).wait_recv()
        go(share(1 if way == 0 else 3))
    early = list(started)
    started.clear()
    relay(1)
    arrived(0, 0)
    level_of(0, scores)
    share(1).wait_recv()
    grad = grad + project(1)
    for way in range(2):
        x_pass(way).wait_recv()
    go(share(2))
    share(3).wait_recv()
    grad = grad + project(3)
    arrived(0, 1)
    level_of(1, scores)
    share(2).wait_recv()
    grad = grad + project(2)
    column = lax.broadcasted_iota(jnp.int32, grad.shape, 1)
    grad = jnp.where(column < lb_ref[0] * TOKENS, grad, 0.0).astype(BF16)
    for h in range(HEADS):
        rows = slice(h * HEAD, (h + 1) * HEAD)
        gs[rows, :] = grad[rows, :].T

    slopes(LAST)
    level_of(0, slopes)
    arrived(0, 2)
    level_of(2, scores)
    arrived(0, 3)
    level_of(3, scores)

    highest = tops[0]
    for chunk in range(1, LAST + 1):
        highest = jnp.maximum(highest, tops[chunk])
    factors = [jnp.exp2((tops[chunk] - highest) * EXP2_SCALE) for chunk in range(LAST + 1)]
    total = sums[0] * factors[0]
    for chunk in range(1, LAST + 1):
        total = total + sums[chunk] * factors[chunk]
    for chunk in range(LAST + 1):
        coef[chunk] = factors[chunk] / total

    def back(c, slot, dy):
        both = slot == 0
        rows = place(slot, dy)
        src = terms.at[:, rows] if both else terms.at[c, rows]
        if slot == 0:
            dst, device = direct.at[:, -dy % NY], at(dy, 0)
        else:
            m, d = (3, dy // 2) if slot == 7 else divmod(slot - 1, 2)
            index = 12 + dy % 2 if slot == 7 else m * NY + -dy % NY
            dst = relayed.at[:, d, index] if both else relayed.at[c, d, index]
            device = at(dy, -m if d == 0 else m)
        return remote(("back", 0 if both else c, slot, dy), src, dst, device)

    def summed_copy(c, d, part):
        groups_of = pl.ds(part * GROUPS // 2, GROUPS // 2)
        return remote(
            ("summed", c, d, part), summed.at[c, d, groups_of], back_in[c][d].at[groups_of],
            at(0, -1 if d == 0 else 1),
        )

    def returned(slot):
        return (1, 2, 3) if slot < 3 else (0, 1, 2, 3)

    def fill(c, chunk):
        rows = rows_of(chunk)
        if c == 1:
            p_buf[rows, :] = e_buf[rows, :] * coef[chunk].astype(BF16)
            return mm(p_buf[rows, :], gs[...])
        ds = p_buf[rows, :].astype(F32) * (dp_buf[rows, :] - row_delta[...])
        ds_buf[rows, :] = ds.astype(BF16)
        return mm(ds_buf[rows, :], qs[...]) * SCALE

    def send_back(c, slots):
        for slot in slots:
            terms[c, slot * SLOT : (slot + 1) * SLOT, :] = fill(c, slot).astype(BF16)
        if slots == (0,) and c == 1:
            return
        for dy in (0, 2, 1, 3):
            for slot in slots:
                if dy in returned(slot):
                    go(back(c, slot, dy))

    def mark(d, i, g):
        return marks[(d * 14 + i) * GROUPS + g]

    def mine(c, slot):
        return terms[c, slot * SLOT : slot * SLOT + BLOCK, :].astype(F32)

    def add_up(c):
        for d in range(2):
            for slot in (7, 5 + d, 3 + d, 1 + d):
                for dy in (2 * d, 2 * d + 1) if slot == 7 else returned(slot):
                    back(c, slot, dy).wait_recv()
        for part in range(2):
            for d in range(2):

                def one(i):
                    g = part * GROUPS // 2 + i
                    result = mine(c, 1 + d) * mark(d, 0, g)
                    for i in range(1, 14):
                        result = result + relayed[c, d, i].astype(F32) * mark(d, i, g)
                    summed[c, d, g] = result.astype(BF16)

                each_pair(GROUPS // 2, one)
                go(summed_copy(c, d, part))

    def add_up_own(c):
        def one(g):
            result = mine(c, 0) * mark(0, 0, g)
            for dy in range(1, NY):
                result = result + direct[c, dy].astype(F32) * mark(0, dy, g)
            local[c, g] = result

        each_pair(GROUPS, one)

    def finish(c):
        for part in range(2):
            for d in range(2):
                summed_copy(c, d, part).wait_recv()
        for slot in range(GROUPS):
            g = pg_ref[0, slot]
            result = back_in[c][0][g].astype(F32) + back_in[c][1][g].astype(F32)
            op_ref[0, slot, :, c * HEAD : (c + 1) * HEAD] = (result + local[c, g]).astype(BF16)

    listed = []
    for d, sign in ((0, 1), (1, -1)):
        for m in range(3):
            listed += groups[sign * m]
        listed += [groups[sign * 3][-dy % NY] for dy in (2 * d, 2 * d + 1)]
    for n, group in enumerate(listed):
        for g in range(GROUPS):
            marks[n * GROUPS + g] = jnp.where(group == g, 1.0, 0.0).astype(F32)
    for slots in ((7,), (5, 6), (3, 4)):
        send_back(1, slots)
    keys_turned[...] = kv[0].T
    for copy in early:
        copy.wait_send()
    arrived(1, 1)
    level_of(1, slopes)
    arrived(1, 2)
    level_of(2, slopes)
    arrived(1, 3)
    level_of(3, slopes)
    delta = dots[0] * coef[0]
    for chunk in range(1, LAST + 1):
        delta = delta + dots[chunk] * coef[chunk]
    row_delta[...] = delta
    for slots in ((7,), (5, 6), (3, 4)):
        send_back(0, slots)
    send_back(1, (1, 2))
    send_back(0, (1, 2))
    add_up(1)
    or_ref[:, HEAD:] = fill(1, LAST).astype(BF16)
    or_ref[:, :HEAD] = fill(0, LAST).astype(BF16)
    add_up(0)
    send_back(1, (0,))
    send_back(0, (0,))
    dq = mm(keys_turned[...], ds_buf[...]) * SCALE
    for h in range(HEADS):
        oq_ref[:, h * HEAD : (h + 1) * HEAD] = dq[:, h * HEAD : (h + 1) * HEAD].T.astype(BF16)
    for dy in returned(0):
        back(0, 0, dy).wait_recv()
    add_up_own(1)
    add_up_own(0)
    finish(1)
    for copy in started:
        copy.wait_send()
    finish(0)


def hand_on(*refs):
    sem = refs[6]
    copies = [pltpu.make_async_copy(refs[n], refs[3 + n], sem.at[n]) for n in range(3)]
    for copy in copies:
        copy.start()
    for copy in copies:
        copy.wait()


def body(
    queries, response_key_value, prompt_kv, prompt_group, response_order, live_blocks,
    out_weight, grad_out,
):
    hbm = pl.BlockSpec(memory_space=pl.ANY)
    vmem = pl.BlockSpec(memory_space=pltpu.VMEM)
    smem = pl.BlockSpec(memory_space=pltpu.SMEM)
    block = (BLOCK, HEAD)

    def space(*shape, kind=BF16):
        return pltpu.VMEM(shape, kind)

    def streams():
        return [[space(GROUPS, *block) for _ in range(2)] for _ in range(2)]

    scratch = [
        space(*queries.shape),
        space(*prompt_kv.shape),
        space(NX, WIDTH, 2 * WIDTH),
        space(NX, TOKENS, 2 * WIDTH),
        space(WIDTH, HEAD),
        space(WIDTH, HEAD),
        space(2, GROUPS, *block),
        streams(),
        space(2, 2, 4, NY, *block),
        space(2, NY, *block),
        space(2, PROMPT + TOKENS, HEAD),
        space(HEAD, PROMPT + TOKENS),
        space(PROMPT + TOKENS, WIDTH),
        space(PROMPT + TOKENS, WIDTH),
        space(PROMPT + TOKENS, WIDTH, kind=F32),
        space(PROMPT + TOKENS, WIDTH),
        space(LAST + 1, 1, WIDTH, kind=F32),
        space(LAST + 1, 1, WIDTH, kind=F32),
        space(LAST + 1, 1, WIDTH, kind=F32),
        space(LAST + 1, 1, WIDTH, kind=F32),
        space(1, WIDTH, kind=F32),
        space(2, PROMPT, HEAD),
        space(2, 2, 14, *block),
        space(2, NY, *block),
        space(2, 2, GROUPS, *block),
        streams(),
        space(2, GROUPS, *block, kind=F32),
        pltpu.SMEM((28 * GROUPS,), F32),
        pltpu.SemaphoreType.DMA((5,)),
        pltpu.SemaphoreType.DMA((NX, 2)),
        pltpu.SemaphoreType.DMA((N_COPIES,)),
        pltpu.SemaphoreType.DMA((N_COPIES,)),
    ]
    kinds = tuple(
        jax.ShapeDtypeStruct(a.shape, BF16) for a in (queries, response_key_value, prompt_kv)
    )
    outs = pl.pallas_call(
        kernel,
        out_shape=tuple(pltpu.VMEM(a.shape, BF16) for a in kinds),
        in_specs=[hbm, hbm, hbm, smem, smem, smem, hbm, hbm],
        out_specs=(vmem, vmem, vmem),
        scratch_shapes=scratch,
        compiler_params=pltpu.CompilerParams(
            collective_id=0, has_side_effects=True, vmem_limit_bytes=56 * 1024 * 1024
        ),
        cost_estimate=pl.CostEstimate(
            flops=3_000_000_000, bytes_accessed=8_000_000, transcendentals=1_400_000
        ),
    )(
        queries, response_key_value, prompt_kv, prompt_group, response_order, live_blocks,
        out_weight, grad_out,
    )
    outs = [pltpu.with_memory_space_constraint(out, pltpu.VMEM) for out in outs]
    return pl.pallas_call(
        hand_on,
        out_shape=kinds,
        in_specs=[vmem, vmem, vmem],
        out_specs=(hbm, hbm, hbm),
        scratch_shapes=[pltpu.SemaphoreType.DMA((3,))],
        compiler_params=pltpu.CompilerParams(vmem_limit_bytes=1024 * 1024),
    )(*outs)


def solution(mesh):
    return jax.shard_map(
        body,
        mesh=mesh,
        in_specs=(
            P("dp", "tensor"),
            P("dp", "tensor"),
            P("dp", None, None, "tensor"),
            P("dp", None),
            P(),
            P("dp"),
            P("tensor", None),
            P("dp", "tensor"),
        ),
        out_specs=(P("dp", "tensor"), P("dp", "tensor"), P("dp", None, None, "tensor")),
        check_vma=False,
    )
```

```python
import math

import jax
import jax.numpy as jnp
from jax import lax
from jax.experimental import pallas as pl
from jax.experimental.pallas import tpu as pltpu
from jax.sharding import PartitionSpec as P

HEAD = 128
HEADS = 5
WIDTH = HEAD * HEADS
TOKENS = 128
BLOCK = 64
GROUPS = 8
NY, NZ, NX = 4, 8, 4
PROMPT = NZ * NY * BLOCK
SLOT = NY * BLOCK
SCALE = 1.0 / math.sqrt(HEAD)
EXP2_SCALE = SCALE * math.log2(math.e)
N_COPIES = 150
MESH = pl.DeviceIdType.MESH
BF16, F32 = jnp.bfloat16, jnp.float32

def mm(a, b):
    return jnp.dot(a, b, preferred_element_type=F32)


def mm_t(a, b):
    return lax.dot_general(a, b, (((1,), (1,)), ((), ())), preferred_element_type=F32)


def fold(x, op):
    return op(x.reshape(x.shape[0] // 8, 8, x.shape[1]), axis=0)


def each(count, step):
    def run(index, carry):
        step(index)
        return carry

    lax.fori_loop(0, count, run, 0)


def each_pair(count, step):
    def both(index):
        step(2 * index)
        step(2 * index + 1)

    each(count // 2, both)


LEVELS = [(0,), (1, 2), (3, 4), (5, 6, 7)]
LAST = 8
REACH = (0, 0, 1, 2)


def kernel(
    q_ref, rkv_ref, pkv_ref, pg_ref, ro_ref, lb_ref, w_ref, go_ref,
    oq_ref, or_ref, op_ref,
    q_v, pkv_v,
    w_v, gathered, qs, gs,
    own, r1, r2, picked, picked_own, kv, keys_turned,
    e_buf, p_buf, dp_buf, ds_buf,
    tops, sums, dots, coef, row_delta,
    terms, relayed, direct, summed, back_in, local,
    marks, in_sem, w_sem, send_sem, recv_sem,
):
    dp = lax.axis_index("dp")
    tensor = lax.axis_index("tensor")
    y, z = lax.div(dp, NZ), lax.rem(dp, NZ)
    x, core = lax.div(tensor, 2), lax.rem(tensor, 2)

    ys = [lax.rem(y + dy, NY) for dy in range(NY)]
    zs = {dz: lax.rem(z + dz + NZ, NZ) for dz in range(-3, 4)}
    places = {(dy, dz): ys[dy] * NZ + zs[dz] for dy in range(NY) for dz in zs}
    along_x = {step: lax.rem(x + step + NX, NX) * 2 + core for step in (-1, 1)}

    def at(dy, dz):
        return (places[dy, dz], tensor)

    def at_x(step):
        return (dp, along_x[step])

    sibling = (dp, x * 2 + 1 - core)

    numbers = {}
    started = []

    def remote(name, src, dst, device):
        n = numbers.setdefault(name, len(numbers))
        return pltpu.make_async_remote_copy(
            src_ref=src, dst_ref=dst, send_sem=send_sem.at[n], recv_sem=recv_sem.at[n],
            device_id=device, device_id_type=MESH,
        )

    def go(copy):
        copy.start()
        started.append(copy)

    in_copies = [
        pltpu.make_async_copy(src, dst, in_sem.at[n])
        for n, (src, dst) in enumerate(
            [
                (pkv_ref, pkv_v), (go_ref, gathered.at[0, :, pl.ds(0, WIDTH)]), (q_ref, q_v),
                (rkv_ref.at[:, pl.ds(0, HEAD)], kv.at[0, pl.ds(PROMPT, TOKENS)]),
                (rkv_ref.at[:, pl.ds(HEAD, HEAD)], kv.at[1, pl.ds(PROMPT, TOKENS)]),
            ]
        )
    ]
    in_copies[0].start()
    barrier = pltpu.get_barrier_semaphore()
    partners = [at(dy, dz) for dz in range(-3, 4) for dy in range(NY) if (dy, dz) != (0, 0)]
    partners += [at_x(1), at_x(-1), sibling]
    for partner in partners:
        pl.semaphore_signal(barrier, inc=1, device_id=partner, device_id_type=MESH)
    for copy in in_copies[1:]:
        copy.start()

    w_copies = {}
    for r in (0, 1, 3, 2):
        for other in range(2):
            piece = lax.rem(x + r, NX) * 2 + (core if other == 0 else 1 - core)
            copy = pltpu.make_async_copy(
                w_ref.at[:, pl.ds(pl.multiple_of(piece * WIDTH, WIDTH), WIDTH)],
                w_v.at[r, :, pl.ds(other * WIDTH, WIDTH)], w_sem.at[r, other],
            )
            copy.start()
            w_copies[r, other] = copy

    slot_of = []
    for g in range(GROUPS):
        slot = jnp.int32(0)
        for c in range(GROUPS):
            slot = jnp.where(pg_ref[0, c] == g, c, slot)
        slot_of.append(slot)
    in_copies[0].wait()
    for g in range(GROUPS):
        own[0, g] = pkv_v[0, slot_of[g], :, :HEAD]
    pl.semaphore_wait(barrier, len(partners))

    def first_hop(c, d):
        return remote(("first", c, d), own.at[c], r1[c][d], at(0, 1 if d == 0 else -1))

    def second_hop(c, d):
        return remote(("second", c, d), r1[c][d], r2[c][d], at(0, 1 if d == 0 else -1))

    def place(slot, dy):
        return pl.ds(slot * SLOT + (dy % NY) * BLOCK, BLOCK)

    def own_copy(dy):
        return remote(
            ("own", dy), picked_own.at[:, dy], kv.at[:, place(0, -dy)], at(dy, 0)
        )

    def forward(c, d, m, dy):
        slot = 7 if m == 3 else 1 + d + 2 * m
        return remote(
            ("forward", c, d, m, dy), picked.at[c, d, m, dy], kv.at[c, place(slot, -dy)],
            at(dy, REACH[m] if d == 0 else -REACH[m]),
        )

    def sent(d, m):
        if m == 3:
            return (2 * d, 2 * d + 1)
        return (1, 2, 3) if m < 2 else (0, 1, 2, 3)

    def pick(c, m, src):
        for pair in zip(sent(0, m), sent(1, m)):
            for d, dy in enumerate(pair):
                picked[c, d, m, dy] = src[c][d][groups[REACH[m] if d == 0 else -REACH[m]][dy]]
                go(forward(c, d, m, dy))

    def relay_near(c):
        for d in range(2):
            first_hop(c, d).wait_recv()
            go(second_hop(c, d))
        pick(c, 0, r1)
        for d in range(2):
            kv[c, (1 + d) * SLOT : (1 + d) * SLOT + BLOCK, :] = r1[c][d][groups[0][0]]

    def relay_far(c):
        for d in range(2):
            second_hop(c, d).wait_recv()
        for m in (3, 2, 1):
            pick(c, m, r2)
        for d in range(2):
            kv[c, (3 + d) * SLOT : (3 + d) * SLOT + BLOCK, :] = r2[c][d][groups[0][0]]

    def arrived(c, level):
        if level == 0:
            for dy in range(1, NY):
                own_copy(dy).wait_recv()
        else:
            for m in (3, 2) if level == 3 else (level - 1,):
                for d in range(2):
                    for dy in sent(d, m):
                        forward(c, d, m, dy).wait_recv()

    half = TOKENS // 2

    def slice_of(r, other, rows=pl.ds(0, TOKENS)):
        return gathered.at[r, rows, pl.ds(other * WIDTH, WIDTH)]

    def x_copy(way, part):
        rows = pl.ds(part * half, half)
        return remote(
            ("x", way, part), slice_of(0, 0, rows), slice_of(1 if way == 0 else 3, 0, rows),
            at_x(-1 if way == 0 else 1),
        )

    def x_pass(way):
        rows = pl.ds(way * half, half)
        return remote(
            ("x", way, 2), slice_of(1 if way == 0 else 3, 0, rows), slice_of(2, 0, rows),
            at_x(-1 if way == 0 else 1),
        )

    def share(r):
        return remote(("share", r), slice_of(r, 0), slice_of(r, 1), sibling)

    for d in range(2):
        go(first_hop(0, d))
    for copy in in_copies[1:]:
        copy.wait()
    for part in range(2):
        for way in range(2):
            go(x_copy(way, way if part == 0 else 1 - way))
    go(share(0))

    for g in range(GROUPS):
        own[1, g] = pkv_v[0, slot_of[g], :, HEAD:]
    for d in range(2):
        go(first_hop(1, d))

    groups = {
        dz: [lax.div(ro_ref[places[dy, dz]], 4) for dy in range(NY)] for dz in range(-3, 4)
    }
    for dy in range(NY):
        for c in range(2):
            if dy == 0:
                kv[c, 0:BLOCK, :] = own[c, groups[0][0]]
            else:
                picked_own[c, dy] = own[c, groups[0][dy]]
        if dy > 0:
            go(own_copy(dy))

    def rows_of(chunk):
        if isinstance(chunk, int) and chunk == LAST:
            return pl.ds(PROMPT, TOKENS)
        return pl.ds(pl.multiple_of(chunk * SLOT, SLOT), SLOT)

    def scores(chunk):
        rows = rows_of(chunk)
        s = mm_t(kv[0, rows, :], qs[...])
        if isinstance(chunk, int) and chunk == LAST:
            key_pos = lax.broadcasted_iota(jnp.int32, s.shape, 0)
            query_pos = lax.broadcasted_iota(jnp.int32, s.shape, 1) % TOKENS
            s = jnp.where(key_pos <= query_pos, s, -jnp.inf)
        top = jnp.max(fold(s, jnp.max), axis=0, keepdims=True)
        e = jnp.exp2((s - top) * EXP2_SCALE)
        e_buf[rows, :] = e.astype(BF16)
        tops[chunk] = top
        sums[chunk] = jnp.sum(fold(e, jnp.sum), axis=0, keepdims=True)

    def slopes(chunk):
        rows = rows_of(chunk)
        values = mm_t(kv[1, rows, :], gs[...])
        dp_buf[rows, :] = values
        products = values * e_buf[rows, :].astype(F32)
        dots[chunk] = jnp.sum(fold(products, jnp.sum), axis=0, keepdims=True)

    def level_of(number, step):
        slots = LEVELS[number]
        each(len(slots), lambda i: step(slots[0] + i))

    def project(r):
        for other in range(2):
            w_copies[r, other].wait()
        return mm_t(w_v[r], gathered[r])

    for h in range(HEADS):
        qs[h * HEAD : (h + 1) * HEAD, :] = q_v[:, h * HEAD : (h + 1) * HEAD]
    scores(LAST)
    share(0).wait_recv()
    grad = project(0)
    for way in range(2):
        x_copy(way, way).wait_recv()
        go(x_pass(way))
    relay_near(0)
    for way in range(2):
        x_copy(way, 1 - way).wait_recv()
        go(share(1 if way == 0 else 3))
    early = list(started)
    started.clear()
    relay_near(1)
    arrived(0, 0)
    level_of(0, scores)
    share(1).wait_recv()
    grad = grad + project(1)
    for way in range(2):
        x_pass(way).wait_recv()
    go(share(2))
    share(3).wait_recv()
    grad = grad + project(3)
    arrived(0, 1)
    level_of(1, scores)
    relay_far(0)
    share(2).wait_recv()
    grad = grad + project(2)
    column = lax.broadcasted_iota(jnp.int32, grad.shape, 1)
    grad = jnp.where(column < lb_ref[0] * TOKENS, grad, 0.0).astype(BF16)
    for h in range(HEADS):
        rows = slice(h * HEAD, (h + 1) * HEAD)
        gs[rows, :] = grad[rows, :].T

    slopes(LAST)
    level_of(0, slopes)
    relay_far(1)
    arrived(0, 2)
    level_of(2, scores)
    arrived(0, 3)
    level_of(3, scores)

    highest = tops[0]
    for chunk in range(1, LAST + 1):
        highest = jnp.maximum(highest, tops[chunk])
    factors = [jnp.exp2((tops[chunk] - highest) * EXP2_SCALE) for chunk in range(LAST + 1)]
    total = sums[0] * factors[0]
    for chunk in range(1, LAST + 1):
        total = total + sums[chunk] * factors[chunk]
    for chunk in range(LAST + 1):
        coef[chunk] = factors[chunk] / total

    def back(c, slot, dy):
        both = slot == 0
        rows = place(slot, dy)
        src = terms.at[:, rows] if both else terms.at[c, rows]
        if slot == 0:
            dst, device = direct.at[:, -dy % NY], at(dy, 0)
        else:
            m, d = (3, dy // 2) if slot == 7 else divmod(slot - 1, 2)
            index = 12 + dy % 2 if slot == 7 else m * NY + -dy % NY
            dst = relayed.at[:, d, index] if both else relayed.at[c, d, index]
            device = at(dy, -m if d == 0 else m)
        return remote(("back", 0 if both else c, slot, dy), src, dst, device)

    def summed_copy(c, d, part):
        groups_of = pl.ds(part * GROUPS // 2, GROUPS // 2)
        return remote(
            ("summed", c, d, part), summed.at[c, d, groups_of], back_in[c][d].at[groups_of],
            at(0, -1 if d == 0 else 1),
        )

    def returned(slot):
        return (1, 2, 3) if slot < 3 else (0, 1, 2, 3)

    def fill(c, chunk):
        rows = rows_of(chunk)
        if c == 1:
            p_buf[rows, :] = e_buf[rows, :] * coef[chunk].astype(BF16)
            return mm(p_buf[rows, :], gs[...])
        ds = p_buf[rows, :].astype(F32) * (dp_buf[rows, :] - row_delta[...])
        ds_buf[rows, :] = ds.astype(BF16)
        return mm(ds_buf[rows, :], qs[...]) * SCALE

    def send_back(c, slots):
        for slot in slots:
            terms[c, slot * SLOT : (slot + 1) * SLOT, :] = fill(c, slot).astype(BF16)
        if slots == (0,) and c == 1:
            return
        for dy in (0, 2, 1, 3):
            for slot in slots:
                if dy in returned(slot):
                    go(back(c, slot, dy))

    def mark(d, i, g):
        return marks[(d * 14 + i) * GROUPS + g]

    def mine(c, slot):
        return terms[c, slot * SLOT : slot * SLOT + BLOCK, :].astype(F32)

    def add_up(c):
        for d in range(2):
            for slot in (7, 5 + d, 3 + d, 1 + d):
                for dy in (2 * d, 2 * d + 1) if slot == 7 else returned(slot):
                    back(c, slot, dy).wait_recv()
        for part in range(2):
            for d in range(2):

                def one(i):
                    g = part * GROUPS // 2 + i
                    result = mine(c, 1 + d) * mark(d, 0, g)
                    for i in range(1, 14):
                        result = result + relayed[c, d, i].astype(F32) * mark(d, i, g)
                    summed[c, d, g] = result.astype(BF16)

                each_pair(GROUPS // 2, one)
                go(summed_copy(c, d, part))

    def add_up_own(c):
        def one(g):
            result = mine(c, 0) * mark(0, 0, g)
            for dy in range(1, NY):
                result = result + direct[c, dy].astype(F32) * mark(0, dy, g)
            local[c, g] = result

        each_pair(GROUPS, one)

    def finish(c):
        for part in range(2):
            for d in range(2):
                summed_copy(c, d, part).wait_recv()
        for slot in range(GROUPS):
            g = pg_ref[0, slot]
            result = back_in[c][0][g].astype(F32) + back_in[c][1][g].astype(F32)
            op_ref[0, slot, :, c * HEAD : (c + 1) * HEAD] = (result + local[c, g]).astype(BF16)

    listed = []
    for d, sign in ((0, 1), (1, -1)):
        for m in range(3):
            listed += groups[sign * m]
        listed += [groups[sign * 3][-dy % NY] for dy in (2 * d, 2 * d + 1)]
    for n, group in enumerate(listed):
        for g in range(GROUPS):
            marks[n * GROUPS + g] = jnp.where(group == g, 1.0, 0.0).astype(F32)
    for slots in ((7,), (5, 6), (3, 4)):
        send_back(1, slots)
    keys_turned[...] = kv[0].T
    for copy in early:
        copy.wait_send()
    arrived(1, 1)
    level_of(1, slopes)
    arrived(1, 2)
    level_of(2, slopes)
    arrived(1, 3)
    level_of(3, slopes)
    delta = dots[0] * coef[0]
    for chunk in range(1, LAST + 1):
        delta = delta + dots[chunk] * coef[chunk]
    row_delta[...] = delta
    for slots in ((7,), (5, 6), (3, 4)):
        send_back(0, slots)
    send_back(1, (1, 2))
    send_back(0, (1, 2))
    add_up(1)
    or_ref[:, HEAD:] = fill(1, LAST).astype(BF16)
    or_ref[:, :HEAD] = fill(0, LAST).astype(BF16)
    add_up(0)
    send_back(1, (0,))
    send_back(0, (0,))
    dq = mm(keys_turned[...], ds_buf[...]) * SCALE
    for h in range(HEADS):
        oq_ref[:, h * HEAD : (h + 1) * HEAD] = dq[:, h * HEAD : (h + 1) * HEAD].T.astype(BF16)
    for dy in returned(0):
        back(0, 0, dy).wait_recv()
    add_up_own(1)
    add_up_own(0)
    finish(1)
    for copy in started:
        copy.wait_send()
    finish(0)


def hand_on(*refs):
    sem = refs[6]
    copies = [pltpu.make_async_copy(refs[n], refs[3 + n], sem.at[n]) for n in range(3)]
    for copy in copies:
        copy.start()
    for copy in copies:
        copy.wait()


def body(
    queries, response_key_value, prompt_kv, prompt_group, response_order, live_blocks,
    out_weight, grad_out,
):
    hbm = pl.BlockSpec(memory_space=pl.ANY)
    vmem = pl.BlockSpec(memory_space=pltpu.VMEM)
    smem = pl.BlockSpec(memory_space=pltpu.SMEM)
    block = (BLOCK, HEAD)

    def space(*shape, kind=BF16):
        return pltpu.VMEM(shape, kind)

    def streams():
        return [[space(GROUPS, *block) for _ in range(2)] for _ in range(2)]

    scratch = [
        space(*queries.shape),
        space(*prompt_kv.shape),
        space(NX, WIDTH, 2 * WIDTH),
        space(NX, TOKENS, 2 * WIDTH),
        space(WIDTH, HEAD),
        space(WIDTH, HEAD),
        space(2, GROUPS, *block),
        streams(),
        streams(),
        space(2, 2, 4, NY, *block),
        space(2, NY, *block),
        space(2, PROMPT + TOKENS, HEAD),
        space(HEAD, PROMPT + TOKENS),
        space(PROMPT + TOKENS, WIDTH),
        space(PROMPT + TOKENS, WIDTH),
        space(PROMPT + TOKENS, WIDTH, kind=F32),
        space(PROMPT + TOKENS, WIDTH),
        space(LAST + 1, 1, WIDTH, kind=F32),
        space(LAST + 1, 1, WIDTH, kind=F32),
        space(LAST + 1, 1, WIDTH, kind=F32),
        space(LAST + 1, 1, WIDTH, kind=F32),
        space(1, WIDTH, kind=F32),
        space(2, PROMPT, HEAD),
        space(2, 2, 14, *block),
        space(2, NY, *block),
        space(2, 2, GROUPS, *block),
        streams(),
        space(2, GROUPS, *block, kind=F32),
        pltpu.SMEM((28 * GROUPS,), F32),
        pltpu.SemaphoreType.DMA((5,)),
        pltpu.SemaphoreType.DMA((NX, 2)),
        pltpu.SemaphoreType.DMA((N_COPIES,)),
        pltpu.SemaphoreType.DMA((N_COPIES,)),
    ]
    kinds = tuple(
        jax.ShapeDtypeStruct(a.shape, BF16) for a in (queries, response_key_value, prompt_kv)
    )
    outs = pl.pallas_call(
        kernel,
        out_shape=tuple(pltpu.VMEM(a.shape, BF16) for a in kinds),
        in_specs=[hbm, hbm, hbm, smem, smem, smem, hbm, hbm],
        out_specs=(vmem, vmem, vmem),
        scratch_shapes=scratch,
        compiler_params=pltpu.CompilerParams(
            collective_id=0, has_side_effects=True, vmem_limit_bytes=56 * 1024 * 1024
        ),
        cost_estimate=pl.CostEstimate(
            flops=3_000_000_000, bytes_accessed=8_000_000, transcendentals=1_400_000
        ),
    )(
        queries, response_key_value, prompt_kv, prompt_group, response_order, live_blocks,
        out_weight, grad_out,
    )
    outs = [pltpu.with_memory_space_constraint(out, pltpu.VMEM) for out in outs]
    return pl.pallas_call(
        hand_on,
        out_shape=kinds,
        in_specs=[vmem, vmem, vmem],
        out_specs=(hbm, hbm, hbm),
        scratch_shapes=[pltpu.SemaphoreType.DMA((3,))],
        compiler_params=pltpu.CompilerParams(vmem_limit_bytes=1024 * 1024),
    )(*outs)


def solution(mesh):
    return jax.shard_map(
        body,
        mesh=mesh,
        in_specs=(
            P("dp", "tensor"),
            P("dp", "tensor"),
            P("dp", None, None, "tensor"),
            P("dp", None),
            P(),
            P("dp"),
            P("tensor", None),
            P("dp", "tensor"),
        ),
        out_specs=(P("dp", "tensor"), P("dp", "tensor"), P("dp", None, None, "tensor")),
        check_vma=False,
    )
```
